32 devices in a mesh: pipe: 4 (over x, core), dp: 8 (over z, y).
Axes of the slice: x: 2, y: 2, z: 4, core: 2. Of those that a mesh axis runs over, the one named last changes fastest.
Arguments:
- lookback_readings: bfloat16 [4, 4096, 336], P('pipe', 'dp'), may hold values from -6 to 6
- prediction_adjoint: bfloat16 [4, 4096, 96], P('pipe', 'dp'), may hold values from -6 to 6
- variate_tallies: int32 [4, 8, 4], P(None, 'dp'), may hold values from 1 to 321, 512 in all within a row
- lookback_classes: int32 [4, 8, 4], P(None, 'dp'), may hold values from 0 to 2
- brief_lift_table: bfloat16 [96, 512], replicated, may hold values from -0.625 to 0.625
- moderate_lift_table: bfloat16 [192, 512], replicated, may hold values from -0.4375 to 0.4375
- distant_lift_table: bfloat16 [336, 512], replicated, may hold values from -0.3125 to 0.3125
- lift_offsets: float32 [3, 512], replicated, may hold values from -3 to 3
- part_entry_arrays: bfloat16 [4, 512, 2048], P('pipe'), may hold values from -3 to 3
- part_shrink_lines: bfloat16 [4, 1024, 512], P('pipe'), may hold values from -0.125 to 0.125
- part_layernorm_scale: float32 [4, 512], P('pipe'), may hold values from 0.5 to 1.5
- part_layernorm_offset: float32 [4, 512], P('pipe'), may hold values from -2 to 2
- mixing_offsets: float32 [2, 3, 512], replicated, may hold values from -2 to 2
- expand_offsets: float32 [2, 2048], replicated, may hold values from -2 to 2
- shrink_offsets: float32 [2, 512], replicated, may hold values from -2 to 2
- prediction_matrix: bfloat16 [512, 96], replicated, may hold values from -0.25 to 0.25
- prediction_offset: float32 [96], replicated, may hold values from -3 to 3
Outputs:
- prediction: bfloat16 [4, 4096, 96], P('pipe', 'dp')
- series_grad: float32 [4, 4096, 336], P('pipe', 'dp')
- emb_short_grad: float32 [96, 512], replicated
- emb_mid_grad: float32 [192, 512], replicated
- emb_long_grad: float32 [336, 512], replicated
- emb_bias_grad: float32 [3, 512], replicated
- section_in_grad: float32 [4, 512, 2048], P('pipe')
- section_down_grad: float32 [4, 1024, 512], P('pipe')
- norm_gain_grad: float32 [4, 512], P('pipe')
- norm_bias_grad: float32 [4, 512], P('pipe')
- att_bias_grad: float32 [2, 3, 512], replicated
- up_bias_grad: float32 [2, 2048], replicated
- down_bias_grad: float32 [2, 512], replicated
- proj_w_grad: float32 [512, 96], replicated
- proj_b_grad: float32 [96], replicated
The draws below stay inside these ranges and needn't reach their ends.
Inputs may be any that keep to these rules, and one draw needn't show every extreme that they name: `variate_tallies`: each row's 4 window sizes sum to 512, and in every row the largest is 321.
All inputs are finite; a program needn't handle non-finite values.
Results may differ from the reference program's by a relative error of at most 0.023.
Values may be sent and summed in bfloat16 or wider, within the bound.
No kernel may reach another device: no remote copies, remote signals or barrier semaphores. Data moves between devices by JAX's collectives and lax.ppermute only.
A program may use at most 384 MiB of HBM per device.

```python
import math
import jax
import jax.numpy as jnp
import numpy as np
from jax import lax

MODEL_BREADTH = 512
HEADS = 8
HEAD_DIM = 64
FF = 2048
PREDICT_STEPS = 96
L_SHORT = 96
L_MID = 192
LOOK = 336
ROW = 512
WIN = 4
MOST = 321
SMALL_GROUPINGS = 4
SECTIONS = 4
ROWS_MB = 1
VARIATE_EACH_SUB = 512
N_DP = 8


def draw_part_entry_arrays(key, part):
    key = jax.random.fold_in(key, 11)
    entries = jnp.clip(jax.random.normal(key, (SECTIONS, MODEL_BREADTH, 4 * MODEL_BREADTH), jnp.float32), -6.0, 6.0)
    column = jnp.arange(4 * MODEL_BREADTH)[None, None, :]
    section_row = jnp.arange(SECTIONS)[:, None, None]
    column_scale = jnp.where((section_row % 2 == 0) & (column >= 3 * MODEL_BREADTH), 4.0, 1.0)
    return (entries * column_scale / math.sqrt(MODEL_BREADTH)).astype(jnp.bfloat16)


def plant(values, rng, least, high):
    extent = values.shape
    spot = [jax.random.randint(jax.random.fold_in(rng, axis), (), 0, extent[axis]) for axis in range(len(extent))]
    values = values.at[tuple(spot)].set(least)
    longest = extent.index(max(extent))
    spot[longest] = (spot[longest] + 1) % extent[longest]
    return values.at[tuple(spot)].set(high)


def level_of(own_key, dims, shards, smallest, largest):
    level, own = 1.0, jax.random.fold_in(own_key, 6)
    for dim, blocks in shards:
        draws = jnp.exp(jax.random.uniform(jax.random.fold_in(own, dim), (blocks,), jnp.float32, smallest / len(shards), largest / len(shards)))
        level = level * jnp.repeat(draws, dims[dim] // blocks).reshape([-1 if axis == dim else 1 for axis in range(len(dims))])
    return level


def profile(count, total, limit, slope):
    weights = [(1 << 20) // math.isqrt(standing ** slope) + 1 for standing in range(2, count + 1)]
    rest, counts = total - limit - (count - 1), [1] * (count - 1)
    while rest > 0:
        candidates = [i for i in range(count - 1) if counts[i] < limit]
        pool, budget = sum([weights[i] for i in candidates]), rest
        for i in candidates:
            more = min(limit - counts[i], max(1, budget * weights[i] // pool), rest)
            counts[i] = counts[i] + more
            rest = rest - more
    return np.array([limit] + counts)


def uneven(own_key, amount, total, limit, slope):
    if amount == 2:
        one = jax.random.randint(own_key, (), max(1, total - limit), min(limit, total - 1) + 1)
        return jnp.stack([one, total - one])
    tallies = jnp.asarray(profile(amount, total, limit, slope), jnp.int32)
    pairs = (amount - 1) // 2
    donor, sink = tallies[1:1 + 2 * pairs:2], tallies[2:2 + 2 * pairs:2]
    slack = jnp.minimum(donor - 1, limit - sink)
    shifted = jax.random.randint(jax.random.fold_in(own_key, 1), (pairs,), 0, 1 << 20) % (slack + 1)
    tallies = tallies.at[1:1 + 2 * pairs:2].set(donor - shifted).at[2:2 + 2 * pairs:2].set(sink + shifted)
    return tallies[jax.random.permutation(jax.random.fold_in(own_key, 2), amount)]


def centred(key, dims, width, limit, split=(), kind=jnp.bfloat16):
    values = width * jax.random.normal(key, dims, jnp.float32)
    if split:
        values = values * level_of(key, dims, split, -0.22, 0.18)
    return jnp.clip(values, -limit, limit).astype(kind)


def setup_inputs(seed: int = 0) -> dict:
    streams_of = jax.random.split(jax.random.key(seed), 18)
    return {
        "lookback_readings": centred(streams_of[0], (SMALL_GROUPINGS, N_DP * VARIATE_EACH_SUB, LOOK), 1.0, 6.0, ((0, 4), (1, 8))),
        "prediction_adjoint": centred(streams_of[1], (SMALL_GROUPINGS, N_DP * VARIATE_EACH_SUB, PREDICT_STEPS), 1.0, 6.0, ((0, 4), (1, 8))),
        "variate_tallies": jax.vmap(lambda own: uneven(own, WIN, ROW, MOST, 0))(jax.random.split(streams_of[2], SMALL_GROUPINGS * (N_DP * ROWS_MB))).reshape((SMALL_GROUPINGS, N_DP * ROWS_MB, WIN)).astype(jnp.int32),
        "lookback_classes": plant(jax.random.randint(streams_of[3], (SMALL_GROUPINGS, N_DP * ROWS_MB, WIN), 0, 3), jax.random.fold_in(streams_of[3], 1), 0, 2).astype(jnp.int32),
        "brief_lift_table": centred(streams_of[4], (L_SHORT, MODEL_BREADTH), L_SHORT ** -0.5, 0.625),
        "moderate_lift_table": centred(streams_of[5], (L_MID, MODEL_BREADTH), L_MID ** -0.5, 0.4375),
        "distant_lift_table": centred(streams_of[6], (LOOK, MODEL_BREADTH), LOOK ** -0.5, 0.3125),
        "lift_offsets": centred(streams_of[7], (3, MODEL_BREADTH), 0.5, 3.0, (), jnp.float32),
        "part_entry_arrays": draw_part_entry_arrays(jax.random.fold_in(streams_of[17], 71), 0),
        "part_shrink_lines": centred(streams_of[9], (SECTIONS, FF // 2, MODEL_BREADTH), FF ** -0.5, 0.125, ((0, 4),)),
        "part_layernorm_scale": jnp.clip(1.0 + 0.1 * jax.random.normal(streams_of[10], (SECTIONS, MODEL_BREADTH), jnp.float32), 0.5, 1.5),
        "part_layernorm_offset": centred(streams_of[11], (SECTIONS, MODEL_BREADTH), 0.3, 2.0, ((0, 4),), jnp.float32),
        "mixing_offsets": centred(streams_of[12], (2, 3, MODEL_BREADTH), 0.3, 2.0, (), jnp.float32),
        "expand_offsets": centred(streams_of[13], (2, FF), 0.3, 2.0, (), jnp.float32),
        "shrink_offsets": centred(streams_of[14], (2, MODEL_BREADTH), 0.3, 2.0, (), jnp.float32),
        "prediction_matrix": centred(streams_of[15], (MODEL_BREADTH, PREDICT_STEPS), MODEL_BREADTH ** -0.5, 0.25),
        "prediction_offset": centred(streams_of[16], (PREDICT_STEPS,), 0.5, 3.0, (), jnp.float32),
    }


@jax.custom_vjp
def reduced_precision(v):
    return lax.optimization_barrier(v.astype(jnp.bfloat16)).astype(jnp.float32)

@jax.custom_vjp
def low_back(v):
    return v

def low_keep(v):
    return (reduced_precision(v), None)

def low_pass(kept, grad):
    return (grad,)

def back_keep(v):
    return (v, None)

def back_low(kept, grad):
    return (reduced_precision(grad),)
reduced_precision.defvjp(low_keep, low_pass)
low_back.defvjp(back_keep, back_low)

def boundary(values):
    return reduced_precision(low_back(values))

def layer_norm(summed, norm_gain_row, norm_offset):
    centre = summed - lax.optimization_barrier(jnp.mean(summed, -1, keepdims=True))
    spread = lax.optimization_barrier(jnp.mean(centre * centre, -1, keepdims=True))
    return centre * lax.rsqrt(spread + 1e-05) * norm_gain_row + norm_offset

def row_layout(variate_tallies, lookback_classes):
    window_end = jnp.cumsum(variate_tallies, -1)
    position = jnp.arange(ROW, dtype=jnp.int32)
    packed_fragment = lax.optimization_barrier(jnp.sum((position[None, :, None] >= window_end[:, None, :]).astype(jnp.int32), -1))
    windows = jnp.arange(WIN, dtype=jnp.int32)
    picked = lax.optimization_barrier(jnp.sum(jnp.where(packed_fragment[:, :, None] == windows[None, None, :], lookback_classes[:, None, :], 0), -1))
    return (packed_fragment, picked)

def row_block(pieces):
    queries, key_rows, value_rows, packed_fragment = pieces
    scores = jnp.einsum('qhd,khd->hqk', queries, key_rows, precision=lax.Precision.HIGHEST) * HEAD_DIM ** (-0.5)
    scores = low_back(scores)
    same_window = packed_fragment[:, None] == packed_fragment[None, :]
    scores = jnp.where(same_window[None], scores, -1e+30)
    row_max = lax.optimization_barrier(jnp.max(scores, -1, keepdims=True))
    weights = jnp.exp(scores - row_max)
    weights = reduced_precision(weights / lax.optimization_barrier(jnp.sum(weights, -1, keepdims=True)))
    return jnp.einsum('hqk,khd->qhd', weights, value_rows, precision=lax.Precision.HIGHEST)

def attention_section(layer_input, matrix, biases, norm_gain_row, norm_offset, packed_fragment):
    model_width = layer_input.shape[1]
    project = jnp.dot(layer_input, matrix[:, :3 * model_width], precision=lax.Precision.HIGHEST)
    queries = reduced_precision(low_back(project[:, :model_width] + biases[0]))
    key_rows = reduced_precision(low_back(project[:, model_width:2 * model_width]))
    value_rows = reduced_precision(low_back(project[:, 2 * model_width:] + biases[1]))
    head_shape = (-1, ROW, HEADS, HEAD_DIM)
    mixture = lax.map(jax.checkpoint(row_block), (queries.reshape(head_shape), key_rows.reshape(head_shape), value_rows.reshape(head_shape), packed_fragment))
    mixture = reduced_precision(low_back(mixture.reshape(-1, model_width)))
    branch = low_back(jnp.dot(mixture, matrix[:, 3 * model_width:], precision=lax.Precision.HIGHEST) + biases[2])
    return layer_norm(layer_input + branch, norm_gain_row, norm_offset)

def feed_section(layer_input, up_matrix, down_matrix, up_offset, down_offset, norm_gain_row, norm_offset):
    hidden = low_back(jnp.dot(layer_input, up_matrix, precision=lax.Precision.HIGHEST) + up_offset)
    hidden = reduced_precision(jax.nn.gelu(hidden, approximate=False))
    branch = low_back(jnp.dot(hidden, down_matrix, precision=lax.Precision.HIGHEST) + down_offset)
    return layer_norm(layer_input + branch, norm_gain_row, norm_offset)

def embed_tokens(tokens, variate_class, brief_lift_table, moderate_lift_table, distant_lift_table, lift_offsets):
    result = jnp.zeros((tokens.shape[0], lift_offsets.shape[1]), tokens.dtype)
    for group_index, emb_table in enumerate((brief_lift_table, moderate_lift_table, distant_lift_table)):
        lookback = emb_table.shape[0]
        chosen = (variate_class == group_index).astype(tokens.dtype)[:, None]
        result = result + chosen * (jnp.dot(tokens[:, LOOK - lookback:], emb_table, precision=lax.Precision.HIGHEST) + lift_offsets[group_index])
    return result

def complete_primal(lookback_readings, brief_lift_table, moderate_lift_table, distant_lift_table, lift_offsets, part_entry_arrays, part_shrink_lines, part_layernorm_scale, part_layernorm_offset, mixing_offsets, expand_offsets, shrink_offsets, prediction_matrix, prediction_offset, packed_fragment, variate_class):
    tokens = lookback_readings.reshape(-1, LOOK)
    latent_activation = boundary(embed_tokens(tokens, variate_class, brief_lift_table, moderate_lift_table, distant_lift_table, lift_offsets))
    latent_activation = boundary(attention_section(latent_activation, part_entry_arrays[0], mixing_offsets[0], part_layernorm_scale[0], part_layernorm_offset[0], packed_fragment))
    first_down = jnp.concatenate([part_shrink_lines[0], part_shrink_lines[1]], 0)
    latent_activation = boundary(feed_section(latent_activation, part_entry_arrays[1], first_down, expand_offsets[0], shrink_offsets[0], part_layernorm_scale[1], part_layernorm_offset[1]))
    latent_activation = boundary(attention_section(latent_activation, part_entry_arrays[2], mixing_offsets[1], part_layernorm_scale[2], part_layernorm_offset[2], packed_fragment))
    second_down = jnp.concatenate([part_shrink_lines[2], part_shrink_lines[3]], 0)
    latent_activation = feed_section(latent_activation, part_entry_arrays[3], second_down, expand_offsets[1], shrink_offsets[1], part_layernorm_scale[3], part_layernorm_offset[3])
    return jnp.dot(reduced_precision(latent_activation), prediction_matrix, precision=lax.Precision.HIGHEST) + prediction_offset

def reference(lookback_readings, prediction_adjoint, variate_tallies, lookback_classes, brief_lift_table, moderate_lift_table, distant_lift_table, lift_offsets, part_entry_arrays, part_shrink_lines, part_layernorm_scale, part_layernorm_offset, mixing_offsets, expand_offsets, shrink_offsets, prediction_matrix, prediction_offset):
    packed_fragment, picked = row_layout(variate_tallies.reshape(-1, WIN), lookback_classes.reshape(-1, WIN))
    variate_class = picked.reshape(-1)
    single_precision_numbers = (lookback_readings.astype(jnp.float32), brief_lift_table.astype(jnp.float32), moderate_lift_table.astype(jnp.float32), distant_lift_table.astype(jnp.float32), lift_offsets.astype(jnp.float32), part_entry_arrays.astype(jnp.float32), part_shrink_lines.astype(jnp.float32), part_layernorm_scale.astype(jnp.float32), part_layernorm_offset.astype(jnp.float32), mixing_offsets.astype(jnp.float32), expand_offsets.astype(jnp.float32), shrink_offsets.astype(jnp.float32), prediction_matrix.astype(jnp.float32), prediction_offset.astype(jnp.float32))

    def primal_only(*params):
        return complete_primal(*params, packed_fragment, variate_class)
    prediction, adjoint_mapping = jax.vjp(primal_only, *single_precision_numbers)
    derivative_collection = adjoint_mapping(prediction_adjoint.astype(jnp.float32).reshape(-1, PREDICT_STEPS))
    return (prediction.reshape(prediction_adjoint.shape).astype(jnp.bfloat16), derivative_collection[0].reshape(lookback_readings.shape), derivative_collection[1], derivative_collection[2], derivative_collection[3], derivative_collection[4], derivative_collection[5], derivative_collection[6], derivative_collection[7], derivative_collection[8], derivative_collection[9], derivative_collection[10], derivative_collection[11], derivative_collection[12], derivative_collection[13])
```

```python
import jax
import jax.numpy as jnp
from jax import lax
from jax.sharding import PartitionSpec as P

HEADS = 8
HEAD_DIM = 64


def shifted(array, axis, by):
    devices = lax.axis_size(axis)
    pairs = [(i, i + by) for i in range(devices) if 0 <= i + by < devices]
    return lax.ppermute(array, axis, pairs)


def as_sent(array):
    return jax.tree.map(lambda a: a.astype(jnp.bfloat16) if a.dtype == jnp.float32 else a, array)


def layer_norm_parts(summed, norm_gain_row, norm_offset):
    centre = summed - jnp.mean(summed, -1, keepdims=True)
    spread = jnp.mean(centre * centre, -1, keepdims=True)
    inverse = lax.rsqrt(spread + 1e-05)
    normed = centre * inverse
    return (normed * norm_gain_row + norm_offset, normed, inverse)


def layer_norm_back(upstream, normed, inverse, norm_gain_row):
    gain_grad = jnp.sum(upstream * normed, 0)
    offset_grad = jnp.sum(upstream, 0)
    scaled = upstream * norm_gain_row
    centred_grad = (
        scaled
        - jnp.mean(scaled, -1, keepdims=True)
        - normed * jnp.mean(scaled * normed, -1, keepdims=True)
    )
    return (centred_grad * inverse, gain_grad, offset_grad)


def row_layout(variate_tallies, lookback_classes, row_len):
    window_end = jnp.cumsum(variate_tallies, -1)
    position = jnp.arange(row_len, dtype=jnp.int32)
    packed_fragment = jnp.sum(
        (position[None, :, None] >= window_end[:, None, :]).astype(jnp.int32), -1
    )
    windows = jnp.arange(variate_tallies.shape[-1], dtype=jnp.int32)
    picked = jnp.sum(
        jnp.where(
            packed_fragment[:, :, None] == windows[None, None, :], lookback_classes[:, None, :], 0
        ),
        -1,
    )
    return (packed_fragment, picked)


def gelu_exact(inputs):
    return jax.nn.gelu(inputs, approximate=False)


def attention_forward(inputs_bf, matrix, biases, norm_gain_row, norm_offset, packed_fragment):
    model_width = inputs_bf.shape[1]
    project = jnp.dot(inputs_bf, matrix[:, : 3 * model_width], preferred_element_type=jnp.float32)
    head_shape = (packed_fragment.shape[0], packed_fragment.shape[1], HEADS, HEAD_DIM)
    query_heads = (project[:, :model_width] + biases[0]).astype(jnp.bfloat16).reshape(head_shape)
    key_heads = project[:, model_width : 2 * model_width].astype(jnp.bfloat16).reshape(head_shape)
    value_heads = (
        (project[:, 2 * model_width :] + biases[1]).astype(jnp.bfloat16).reshape(head_shape)
    )
    scores = jnp.einsum(
        "rqhd,rkhd->rhqk", query_heads, key_heads, preferred_element_type=jnp.float32
    ) * HEAD_DIM ** (-0.5)
    same_window = (packed_fragment[:, :, None] == packed_fragment[:, None, :])[:, None]
    scores = jnp.where(same_window, scores, -1e30)
    row_max = jnp.max(scores, -1, keepdims=True)
    weights = jnp.exp(scores - row_max)
    weights = weights / jnp.sum(weights, -1, keepdims=True)
    weights_bf = weights.astype(jnp.bfloat16)
    mixture = jnp.einsum(
        "rhqk,rkhd->rqhd", weights_bf, value_heads, preferred_element_type=jnp.float32
    )
    mixture_bf = mixture.reshape(-1, model_width).astype(jnp.bfloat16)
    branch = (
        jnp.dot(mixture_bf, matrix[:, 3 * model_width :], preferred_element_type=jnp.float32)
        + biases[2]
    )
    output, normed, inverse = layer_norm_parts(
        inputs_bf.astype(jnp.float32) + branch, norm_gain_row, norm_offset
    )
    return (
        output,
        (query_heads, key_heads, value_heads, weights, weights_bf, mixture_bf, normed, inverse),
    )


def attention_backward(upstream, inputs_bf, matrix, norm_gain_row, saved_parts):
    query_heads, key_heads, value_heads, weights, weights_bf, mixture_bf, normed, inverse = (
        saved_parts
    )
    model_width = inputs_bf.shape[1]
    summed_grad, gain_grad, offset_grad = layer_norm_back(upstream, normed, inverse, norm_gain_row)
    branch_bf = summed_grad.astype(jnp.bfloat16)
    out_matrix_grad = jnp.dot(mixture_bf.T, branch_bf, preferred_element_type=jnp.float32)
    out_bias_grad = jnp.sum(branch_bf.astype(jnp.float32), 0)
    mixture_grad = jnp.dot(
        branch_bf, matrix[:, 3 * model_width :].T, preferred_element_type=jnp.float32
    )
    mixture_grad = mixture_grad.astype(jnp.bfloat16).reshape(query_heads.shape)
    weight_grad = jnp.einsum(
        "rqhd,rkhd->rhqk", mixture_grad, value_heads, preferred_element_type=jnp.float32
    )
    value_grad = jnp.einsum(
        "rhqk,rqhd->rkhd", weights_bf, mixture_grad, preferred_element_type=jnp.float32
    )
    centred = jnp.sum(weights * weight_grad, -1, keepdims=True)
    score_grad = (weights * (weight_grad - centred)).astype(jnp.bfloat16)
    query_grad = jnp.einsum(
        "rhqk,rkhd->rqhd", score_grad, key_heads, preferred_element_type=jnp.float32
    ) * HEAD_DIM ** (-0.5)
    key_grad = jnp.einsum(
        "rhqk,rqhd->rkhd", score_grad, query_heads, preferred_element_type=jnp.float32
    ) * HEAD_DIM ** (-0.5)
    project_grad = jnp.concatenate(
        [
            query_grad.reshape(-1, model_width),
            key_grad.reshape(-1, model_width),
            value_grad.reshape(-1, model_width),
        ],
        1,
    ).astype(jnp.bfloat16)
    in_matrix_grad = jnp.dot(inputs_bf.T, project_grad, preferred_element_type=jnp.float32)
    project_float = project_grad.astype(jnp.float32)
    query_bias_grad = jnp.sum(project_float[:, :model_width], 0)
    value_bias_grad = jnp.sum(project_float[:, 2 * model_width :], 0)
    input_grad = summed_grad + jnp.dot(
        project_grad, matrix[:, : 3 * model_width].T, preferred_element_type=jnp.float32
    )
    matrix_grad = jnp.concatenate([in_matrix_grad, out_matrix_grad], 1)
    bias_grad = jnp.stack([query_bias_grad, value_bias_grad, out_bias_grad])
    return (input_grad, matrix_grad, bias_grad, gain_grad, offset_grad)


def feed_forward(
    inputs_bf, up_matrix, down_matrix, up_offset, down_offset, norm_gain_row, norm_offset
):
    hidden_pre = jnp.dot(inputs_bf, up_matrix, preferred_element_type=jnp.float32) + up_offset
    hidden_bf = gelu_exact(hidden_pre).astype(jnp.bfloat16)
    branch = jnp.dot(hidden_bf, down_matrix, preferred_element_type=jnp.float32) + down_offset
    output, normed, inverse = layer_norm_parts(
        inputs_bf.astype(jnp.float32) + branch, norm_gain_row, norm_offset
    )
    return (output, (hidden_pre, hidden_bf, normed, inverse))


def feed_backward(upstream, inputs_bf, up_matrix, down_matrix, norm_gain_row, saved_parts):
    hidden_pre, hidden_bf, normed, inverse = saved_parts
    summed_grad, gain_grad, offset_grad = layer_norm_back(upstream, normed, inverse, norm_gain_row)
    branch_bf = summed_grad.astype(jnp.bfloat16)
    down_grad = jnp.dot(hidden_bf.T, branch_bf, preferred_element_type=jnp.float32)
    down_offset_grad = jnp.sum(branch_bf.astype(jnp.float32), 0)
    hidden_grad = jnp.dot(branch_bf, down_matrix.T, preferred_element_type=jnp.float32)
    activated, gelu_pull = jax.vjp(gelu_exact, hidden_pre)
    pre_bf = gelu_pull(hidden_grad)[0].astype(jnp.bfloat16)
    up_grad = jnp.dot(inputs_bf.T, pre_bf, preferred_element_type=jnp.float32)
    up_offset_grad = jnp.sum(pre_bf.astype(jnp.float32), 0)
    input_grad = summed_grad + jnp.dot(pre_bf, up_matrix.T, preferred_element_type=jnp.float32)
    return (
        input_grad,
        up_grad,
        down_grad,
        up_offset_grad,
        down_offset_grad,
        gain_grad,
        offset_grad,
    )


def embed_forward(tokens_bf, variate_class, tables, lift_offsets):
    look_width = tokens_bf.shape[1]
    result = jnp.zeros((tokens_bf.shape[0], lift_offsets.shape[1]), jnp.float32)
    for group_index in range(3):
        emb_table = tables[group_index]
        lookback = emb_table.shape[0]
        chosen = (variate_class == group_index).astype(jnp.float32)[:, None]
        result = result + chosen * (
            jnp.dot(
                tokens_bf[:, look_width - lookback :], emb_table, preferred_element_type=jnp.float32
            )
            + lift_offsets[group_index]
        )
    return result


def embed_backward(embed_grad_bf, tokens_bf, variate_class, tables):
    look_width = tokens_bf.shape[1]
    table_grads = []
    bias_grads = []
    series_piece = jnp.zeros(tokens_bf.shape, jnp.float32)
    for group_index in range(3):
        emb_table = tables[group_index]
        lookback = emb_table.shape[0]
        start_col = look_width - lookback
        chosen = (variate_class == group_index).astype(jnp.bfloat16)[:, None]
        masked = embed_grad_bf * chosen
        table_grads.append(
            jnp.dot(tokens_bf[:, start_col:].T, masked, preferred_element_type=jnp.float32)
        )
        bias_grads.append(jnp.sum(masked.astype(jnp.float32), 0))
        spread_back = jnp.dot(masked, emb_table.T, preferred_element_type=jnp.float32)
        series_piece = series_piece + jnp.pad(spread_back, ((0, 0), (start_col, 0)))
    return (table_grads, jnp.stack(bias_grads), series_piece)


def per_device(
    lookback_readings,
    prediction_adjoint,
    variate_tallies,
    lookback_classes,
    brief_lift_table,
    moderate_lift_table,
    distant_lift_table,
    lift_offsets,
    part_entry_arrays,
    part_shrink_lines,
    part_layernorm_scale,
    part_layernorm_offset,
    mixing_offsets,
    expand_offsets,
    shrink_offsets,
    prediction_matrix,
    prediction_offset,
):
    bf16 = jnp.bfloat16
    place = lax.axis_index("pipe")
    sections = lax.axis_size("pipe")
    tokens_bf = lookback_readings[0]
    adjoint = prediction_adjoint[0]
    count = tokens_bf.shape[0]
    rows_mb = variate_tallies.shape[1]
    tallies = lax.dynamic_index_in_dim(variate_tallies, place, 0, False)
    classes = lax.dynamic_index_in_dim(lookback_classes, place, 0, False)
    fragment, picked = row_layout(tallies, classes, count // rows_mb)
    picked = picked.reshape(-1)
    entry, shrink = (
        lax.all_gather(part_entry_arrays, "pipe", axis=0, tiled=True),
        lax.all_gather(part_shrink_lines, "pipe", axis=0, tiled=True),
    )
    scale, offset = (
        lax.all_gather(part_layernorm_scale, "pipe", axis=0, tiled=True),
        lax.all_gather(part_layernorm_offset, "pipe", axis=0, tiled=True),
    )
    tables = (brief_lift_table, moderate_lift_table, distant_lift_table)
    xs = [embed_forward(tokens_bf, picked, tables, lift_offsets).astype(bf16)]
    saved = []
    half = shrink.shape[1]
    for s in range(sections):
        layer = s // 2
        if s % 2 == 0:
            y, kept = attention_forward(
                xs[s], entry[s], mixing_offsets[layer], scale[s], offset[s], fragment
            )
        else:
            down = shrink[2 * layer : 2 * layer + 2].reshape(2 * half, -1)
            y, kept = feed_forward(
                xs[s], entry[s], down, expand_offsets[layer], shrink_offsets[layer], scale[s], offset[s]
            )
        saved.append(kept)
        xs.append(y.astype(bf16))
    last = xs[-1]
    prediction = (
        jnp.dot(last, prediction_matrix, preferred_element_type=jnp.float32) + prediction_offset
    ).astype(bf16)
    proj_w = jnp.dot(last.T, adjoint, preferred_element_type=jnp.float32)
    proj_b = jnp.sum(adjoint.astype(jnp.float32), 0)
    g = jnp.dot(adjoint, prediction_matrix.T, preferred_element_type=jnp.float32)
    entry_grads, down_grads = [None] * sections, [None] * sections
    gains, offsets = [None] * sections, [None] * sections
    att_bias, up_bias, down_bias = [None] * 2, [None] * 2, [None] * 2
    for s in reversed(range(sections)):
        layer = s // 2
        if s % 2 == 0:
            g, entry_grads[s], att_bias[layer], gains[s], offsets[s] = attention_backward(
                g, xs[s], entry[s], scale[s], saved[s]
            )
        else:
            down = shrink[2 * layer : 2 * layer + 2].reshape(2 * half, -1)
            g, entry_grads[s], both, up_bias[layer], down_bias[layer], gains[s], offsets[s] = (
                feed_backward(g, xs[s], entry[s], down, scale[s], saved[s])
            )
            down_grads[2 * layer], down_grads[2 * layer + 1] = both[:half], both[half:]
        g_bf = g.astype(bf16)
        g = g_bf.astype(jnp.float32)
    table_grads, emb_bias, series = embed_backward(g_bf, tokens_bf, picked, tables)
    width = entry.shape[1]
    big = jnp.stack(
        [
            jnp.concatenate(
                [entry_grads[s].astype(bf16).reshape(-1, width), down_grads[s].astype(bf16)], 0
            )
            for s in range(sections)
        ]
    )
    big = lax.psum_scatter(big, "pipe", scatter_dimension=0, tiled=True)[0]
    big = lax.psum(big, "dp").astype(jnp.float32)
    entry_rows = entry.shape[1] * entry.shape[2] // width
    small = lax.psum(
        (
            *table_grads,
            emb_bias,
            jnp.stack(att_bias),
            jnp.stack(up_bias),
            jnp.stack(down_bias),
            proj_w,
            proj_b,
            jnp.stack(gains),
            jnp.stack(offsets),
        ),
        ("pipe", "dp"),
    )
    gain = lax.dynamic_index_in_dim(small[9], place, 0, True)
    bias = lax.dynamic_index_in_dim(small[10], place, 0, True)
    return (
        prediction[None],
        series[None],
        small[0],
        small[1],
        small[2],
        small[3],
        big[:entry_rows].reshape(1, *entry.shape[1:]),
        big[entry_rows:][None],
        gain,
        bias,
        small[4],
        small[5],
        small[6],
        small[7],
        small[8],
    )


def solution(mesh):
    placed = (
        P("pipe", "dp", None),
        P("pipe", "dp", None),
        P(None, "dp", None),
        P(None, "dp", None),
        P(),
        P(),
        P(),
        P(),
        P("pipe", None, None),
        P("pipe", None, None),
        P("pipe", None),
        P("pipe", None),
        P(),
        P(),
        P(),
        P(),
        P(),
    )
    return jax.shard_map(
        per_device,
        mesh=mesh,
        in_specs=placed,
        out_specs=(
            P("pipe", "dp", None),
            P("pipe", "dp", None),
            P(),
            P(),
            P(),
            P(),
            P("pipe", None, None),
            P("pipe", None, None),
            P("pipe", None),
            P("pipe", None),
            P(),
            P(),
            P(),
            P(),
            P(),
        ),
        check_vma=False,
    )
```

```python
import functools

import jax
import jax.numpy as jnp
from jax import lax
from jax.experimental import pallas as pl
from jax.experimental.pallas import tpu as pltpu
from jax.sharding import PartitionSpec as P

HEADS = 8
HEAD_DIM = 64
F32 = jnp.float32
BF16 = jnp.bfloat16
SHARED_ROWS = 768
VECTOR_ROW = 720


def nn(a, b):
    return lax.dot_general(a, b, (((1,), (0,)), ((), ())), preferred_element_type=F32)


def nt(a, b):
    return lax.dot_general(a, b, (((1,), (1,)), ((), ())), preferred_element_type=F32)


def tn(a, b):
    return lax.dot_general(a, b, (((0,), (0,)), ((), ())), preferred_element_type=F32)


def normalise(z):
    centre = z - jnp.mean(z, -1, keepdims=True)
    inverse = lax.rsqrt(jnp.mean(centre * centre, -1, keepdims=True) + 1e-05)
    return centre * inverse, inverse


def norm_back(upstream, z, gain):
    normed, inverse = normalise(z)
    gain_grad = jnp.sum(upstream * normed, 0, keepdims=True)
    offset_grad = jnp.sum(upstream, 0, keepdims=True)
    scaled = upstream * gain
    back = inverse * (
        scaled
        - jnp.mean(scaled, -1, keepdims=True)
        - normed * jnp.mean(scaled * normed, -1, keepdims=True)
    )
    return back, gain_grad, offset_grad


def gelu_both(u):
    bell = jnp.exp(u * u * -0.5)
    t = 1.0 / (1.0 + (0.3275911 * 0.5**0.5) * jnp.abs(u))
    poly = t * (
        0.127414796
        + t * (-0.142248368 + t * (0.7107068705 + t * (-0.7265760135 + t * 0.5307027145)))
    )
    half = poly * bell
    phi = jnp.where(u >= 0, 1.0 - half, half)
    return u * phi, phi + u * bell * 0.3989422804014327


def same_window_bias(seg_col, seg_row):
    return jnp.where(seg_col == seg_row, 0.0, -1e30).astype(F32)


class Choice:
    def __init__(self, index, sources, place, sem):
        self.index = index
        self.copies = [pltpu.make_async_copy(s, place, sem) for s in sources]

    def start(self):
        for k, copy in enumerate(self.copies):
            pl.when(self.index == k)(copy.start)

    def wait(self):
        for k, copy in enumerate(self.copies):
            pl.when(self.index == k)(copy.wait)


def attention_forward_kernel(
    at_ref, w0, w1, w2, w3, x_ref, bias_ref, norm_ref, segc_ref, segr_ref,
    y_ref, z_ref, qkv_ref, o_ref, lse_ref, mask_ref, w_ref, sem,
):
    choice = Choice(at_ref[0], (w0, w1, w2, w3), w_ref, sem.at[0])
    choice.start()
    width = x_ref.shape[1]
    x = x_ref[...]
    mask_ref[...] = same_window_bias(segc_ref[...], segr_ref[...])
    choice.wait()
    qkv_ref[:, :width] = ((nn(x, w_ref[:, :width]) + bias_ref[0:1, :]) * HEAD_DIM**-0.5).astype(BF16)
    qkv_ref[:, width : 2 * width] = nn(x, w_ref[:, width : 2 * width]).astype(BF16)
    qkv_ref[:, 2 * width : 3 * width] = (
        nn(x, w_ref[:, 2 * width : 3 * width]) + bias_ref[1:2, :]
    ).astype(BF16)
    pair = 2 * HEAD_DIM
    low = lax.broadcasted_iota(jnp.int32, (1, pair), 1) < HEAD_DIM
    for p in range(HEADS // 2):
        q2 = qkv_ref[:, p * pair : (p + 1) * pair]
        k2 = qkv_ref[:, width + p * pair : width + (p + 1) * pair]
        v2 = qkv_ref[:, 2 * width + p * pair : 2 * width + (p + 1) * pair]
        v2t = v2.T
        parts = []
        for h in range(2):
            kh = jnp.where(low if h == 0 else ~low, k2, jnp.zeros_like(k2))
            s = nt(kh, q2) + mask_ref[...]
            top = jnp.max(s, 0, keepdims=True)
            e = jnp.exp(s - top)
            total = jnp.sum(e, 0, keepdims=True)
            lse_ref[2 * p + h : 2 * p + h + 1, :] = top + jnp.log(total)
            ot = nn(v2t[h * HEAD_DIM : (h + 1) * HEAD_DIM, :], e.astype(BF16))
            parts.append(ot * (1.0 / total))
        o_ref[:, p * pair : (p + 1) * pair] = jnp.concatenate(parts, 0).T.astype(BF16)
    z = x.astype(F32) + (nn(o_ref[...], w_ref[:, 3 * width :]) + bias_ref[2:3, :])
    z_ref[...] = z
    y_ref[...] = (normalise(z)[0] * norm_ref[0:1, :] + norm_ref[1:2, :]).astype(BF16)


def feed_core(x, up_ref, down_ref, upb_ref, h_ref, d_ref, block=512):
    total = None
    for c in range(0, up_ref.shape[1], block):
        u = nn(x, up_ref[:, c : c + block]) + upb_ref[:, c : c + block]
        h, d = gelu_both(u)
        hb = h.astype(BF16)
        h_ref[:, c : c + block] = hb
        d_ref[:, c : c + block] = d.astype(BF16)
        part = nn(hb, down_ref[c : c + block, :])
        total = part if total is None else total + part
    return total


def feed_weights(at_ref, ups, downs, up_ref, down_ref, sem):
    half = down_ref.shape[0] // 2
    loads = [Choice(at_ref[0], ups, up_ref, sem.at[0])]
    loads += [
        Choice(at_ref[1 + h], downs, down_ref.at[pl.ds(h * half, half)], sem.at[1 + h]) for h in range(2)
    ]
    for one in loads:
        one.start()
    return loads


def feed_forward_kernel(
    at_ref, u0, u1, u2, u3, d0, d1, d2, d3, x_ref, upb_ref, downb_ref, norm_ref,
    y_ref, z_ref, h_ref, d_ref, up_ref, down_ref, sem,
):
    loads = feed_weights(at_ref, (u0, u1, u2, u3), (d0, d1, d2, d3), up_ref, down_ref, sem)
    x = x_ref[...]
    for one in loads:
        one.wait()
    f = feed_core(x, up_ref, down_ref, upb_ref, h_ref, d_ref)
    z = x.astype(F32) + (f + downb_ref[...])
    z_ref[...] = z
    y_ref[...] = (normalise(z)[0] * norm_ref[0:1, :] + norm_ref[1:2, :]).astype(BF16)


def feed_back_core(
    core, upstream, x, z, h_ref, d_ref, up_ref, down_ref, gain,
    keep_ref, send_ref, upb_ref, xt_ref, gx_acc,
):
    back, gain_grad, offset_grad = norm_back(upstream, z, gain)
    back_bf = back.astype(BF16)
    downb = jnp.sum(back_bf.astype(F32), 0, keepdims=True)
    gx_acc[...] = back
    xt_ref[...] = x.T
    width = x.shape[1]
    rows = width // 2
    blocks = up_ref.shape[1] // width
    for j in range(blocks):
        b = lax.rem(j + core * (blocks // 2), blocks)
        cols = pl.ds(pl.multiple_of(b * width, width), width)
        gu = (nt(back_bf, down_ref[cols, :]) * d_ref[:, cols].astype(F32)).astype(BF16)
        down_out = keep_ref if j < blocks // 2 else send_ref
        at = blocks * rows + (j % (blocks // 2)) * width
        down_out[at : at + width, :] = tn(h_ref[:, cols], back_bf).astype(BF16)
        mine = pl.ds(pl.multiple_of(core * rows, rows), rows)
        other = pl.ds(pl.multiple_of((1 - core) * rows, rows), rows)
        at = pl.ds(pl.multiple_of(b * rows, rows), rows)
        keep_ref[at, :] = nn(xt_ref[mine, :], gu).astype(BF16)
        send_ref[at, :] = nn(xt_ref[other, :], gu).astype(BF16)
        upb_ref[pl.ds(b, 1), :] = jnp.sum(gu.astype(F32), 0, keepdims=True)
        gx_acc[...] += nt(gu, up_ref[:, cols])
    return gain_grad, offset_grad, downb


def feed_back_kernel(
    at_ref, u0, u1, u2, u3, d0, d1, d2, d3, g_ref, x_ref, z_ref, h_ref, d_ref, norm_ref,
    gx_ref, keep_ref, send_ref, upb_ref, vec_ref, up_ref, down_ref, xt_ref, gx_acc, sem,
):
    loads = feed_weights(at_ref, (u0, u1, u2, u3), (d0, d1, d2, d3), up_ref, down_ref, sem)
    for one in loads:
        one.wait()
    gain_grad, offset_grad, downb = feed_back_core(
        at_ref[3], g_ref[...].astype(F32), x_ref[...], z_ref[...], h_ref, d_ref, up_ref, down_ref,
        norm_ref[0:1, :], keep_ref, send_ref, upb_ref, xt_ref, gx_acc,
    )
    gx_ref[...] = gx_acc[...].astype(BF16)
    vec_ref[...] = jnp.concatenate([gain_grad, offset_grad, downb], 0)


def last_feed_kernel(
    at_ref, u0, u1, u2, u3, d0, d1, d2, d3,
    x_ref, upb_ref, downb_ref, norm_ref, pm_ref, pb_ref, adj_ref,
    pred_ref, gpm_ref, gpb_ref, gx_ref, keep_ref, send_ref, gupb_ref, vec_ref,
    h_ref, d_ref, up_ref, down_ref, xt_ref, gx_acc, sem,
):
    loads = feed_weights(at_ref, (u0, u1, u2, u3), (d0, d1, d2, d3), up_ref, down_ref, sem)
    x = x_ref[...]
    for one in loads:
        one.wait()
    f = feed_core(x, up_ref, down_ref, upb_ref, h_ref, d_ref)
    z = x.astype(F32) + (f + downb_ref[...])
    y = (normalise(z)[0] * norm_ref[0:1, :] + norm_ref[1:2, :]).astype(BF16)
    pm = pm_ref[...]
    adj = adj_ref[...]
    pred_ref[...] = (nn(y, pm) + pb_ref[...]).astype(BF16)
    gpm_ref[...] = tn(adj, y)
    gpb_ref[...] = jnp.sum(adj.astype(F32), 0, keepdims=True)
    gain_grad, offset_grad, downb = feed_back_core(
        at_ref[3], nt(adj, pm), x, z, h_ref, d_ref, up_ref, down_ref,
        norm_ref[0:1, :], keep_ref, send_ref, gupb_ref, xt_ref, gx_acc,
    )
    gx_ref[...] = gx_acc[...].astype(BF16)
    vec_ref[...] = jnp.concatenate([gain_grad, offset_grad, downb], 0)


def attention_back_kernel(
    at_ref, w0, w1, w2, w3, g_ref, x_ref, z_ref, qkv_ref, o_ref, lse_ref, norm_ref, segc_ref, segr_ref,
    gx_ref, keep_ref, send_ref, vec_ref, mask_ref, gqkv_ref, go_ref, w_ref, xt_ref, sem,
):
    choice = Choice(at_ref[0], (w0, w1, w2, w3), w_ref, sem.at[0])
    choice.start()
    core = at_ref[1]
    width = x_ref.shape[1]
    rows = width // 2
    mine = pl.ds(pl.multiple_of(core * rows, rows), rows)
    other = pl.ds(pl.multiple_of((1 - core) * rows, rows), rows)
    back, gain_grad, offset_grad = norm_back(g_ref[...].astype(F32), z_ref[...], norm_ref[0:1, :])
    ga = back.astype(BF16)
    gab = jnp.sum(ga.astype(F32), 0, keepdims=True)
    xt_ref[...] = o_ref[...].T
    keep_ref[3 * rows : 4 * rows, :] = nn(xt_ref[mine, :], ga).astype(BF16)
    send_ref[3 * rows : 4 * rows, :] = nn(xt_ref[other, :], ga).astype(BF16)
    mask_ref[...] = same_window_bias(segc_ref[...], segr_ref[...])
    choice.wait()
    go_ref[...] = nt(ga, w_ref[:, 3 * width :]).astype(BF16)
    pair = 2 * HEAD_DIM
    low = lax.broadcasted_iota(jnp.int32, (1, pair), 1) < HEAD_DIM
    for p in range(HEADS // 2):
        q2 = qkv_ref[:, p * pair : (p + 1) * pair]
        k2 = qkv_ref[:, width + p * pair : width + (p + 1) * pair]
        v2 = qkv_ref[:, 2 * width + p * pair : 2 * width + (p + 1) * pair]
        go2 = go_ref[:, p * pair : (p + 1) * pair]
        o2 = o_ref[:, p * pair : (p + 1) * pair]
        k2t = k2.T
        prod = (go2.astype(F32) * o2.astype(F32)).T
        gq, gk, gv = [], None, None
        for h in range(2):
            own = low if h == 0 else ~low
            zero = jnp.zeros_like(k2)
            lanes = slice(h * HEAD_DIM, (h + 1) * HEAD_DIM)
            centred = jnp.sum(prod[lanes, :], 0, keepdims=True)
            s = nt(jnp.where(own, k2, zero), q2) + mask_ref[...]
            weights = jnp.exp(s - lse_ref[2 * p + h : 2 * p + h + 1, :])
            gp = nt(jnp.where(own, v2, zero), go2)
            gs = (weights * (gp - centred)).astype(BF16)
            gv_part = nn(weights.astype(BF16), jnp.where(own, go2, zero))
            gk_part = nn(gs, jnp.where(own, q2, zero))
            gv = gv_part if gv is None else gv + gv_part
            gk = gk_part if gk is None else gk + gk_part
            gq.append(nn(k2t[lanes, :], gs) * HEAD_DIM**-0.5)
        cols = slice(p * pair, (p + 1) * pair)
        gqkv_ref[:, cols] = jnp.concatenate(gq, 0).T.astype(BF16)
        gqkv_ref[:, width + p * pair : width + (p + 1) * pair] = gk.astype(BF16)
        gqkv_ref[:, 2 * width + p * pair : 2 * width + (p + 1) * pair] = gv.astype(BF16)
    xt_ref[...] = x_ref[...].T
    for b in range(3):
        part = gqkv_ref[:, b * width : (b + 1) * width]
        keep_ref[b * rows : (b + 1) * rows, :] = nn(xt_ref[mine, :], part).astype(BF16)
        send_ref[b * rows : (b + 1) * rows, :] = nn(xt_ref[other, :], part).astype(BF16)
    gqkv = gqkv_ref[...]
    gqb = jnp.sum(gqkv[:, :width].astype(F32), 0, keepdims=True)
    gvb = jnp.sum(gqkv[:, 2 * width :].astype(F32), 0, keepdims=True)
    gx_ref[...] = (back + nt(gqkv, w_ref[:, : 3 * width])).astype(BF16)
    vec_ref[...] = jnp.concatenate([gain_grad, offset_grad, gqb, gvb, gab], 0)


def padded_table(t_ref, look):
    table = t_ref[...]
    skip = look - table.shape[0]
    if skip:
        table = jnp.concatenate([jnp.zeros((skip, table.shape[1]), BF16), table], 0)
    return table, skip


def embed_kernel(tok_ref, cls_ref, t0_ref, t1_ref, t2_ref, off_ref, x_ref):
    tok = tok_ref[...]
    cls = cls_ref[...]
    total = None
    for g, t_ref in enumerate((t0_ref, t1_ref, t2_ref)):
        chosen = cls == g
        masked = jnp.where(chosen, tok, jnp.zeros_like(tok))
        table, _ = padded_table(t_ref, tok.shape[1])
        part = nn(masked, table) + jnp.where(chosen, off_ref[g : g + 1, :], 0.0)
        total = part if total is None else total + part
    x_ref[...] = total.astype(BF16)


def embed_back_kernel(
    core_ref, g_ref, tok_ref, cls_ref, t0_ref, t1_ref, t2_ref,
    gpm_ref, gpb_ref, vec0_ref, vec1_ref, vec2_ref, vec3_ref, upb0_ref, upb1_ref,
    series_ref, keep_ref, send_ref, all_ref,
):
    tok = tok_ref[...]
    cls = cls_ref[...]
    g = g_ref[...]
    tokt = tok.T
    series = None
    sums = []
    at = 0
    for i, t_ref in enumerate((t0_ref, t1_ref, t2_ref)):
        masked = jnp.where(cls == i, g, jnp.zeros_like(g))
        table, skip = padded_table(t_ref, tok.shape[1])
        part = nt(masked, table)
        series = part if series is None else series + part
        count = table.shape[0] - skip
        all_ref[at : at + count, :] = nn(tokt, masked)[skip:, :].astype(BF16)
        at += count
        sums.append(jnp.sum(masked.astype(F32), 0, keepdims=True))
    series_ref[...] = series
    all_ref[at : at + gpm_ref.shape[0], :] = gpm_ref[...].astype(BF16)
    width = g.shape[1]
    gpb = jnp.concatenate(
        [gpb_ref[...], jnp.zeros((1, width - gpb_ref.shape[1]), F32)], 1
    )
    rows = [gpb, *sums, vec0_ref[2:5, :], vec2_ref[2:5, :], upb0_ref[...], upb1_ref[...]]
    rows += [vec1_ref[2:3, :], vec3_ref[2:3, :]]
    vecs = (vec0_ref, vec1_ref, vec2_ref, vec3_ref)
    rows += [v[0:1, :] for v in vecs] + [v[1:2, :] for v in vecs]
    used = sum(r.shape[0] for r in rows)
    rows.append(jnp.zeros((SHARED_ROWS - VECTOR_ROW - used, width), F32))
    all_ref[VECTOR_ROW:SHARED_ROWS, :] = jnp.concatenate(rows, 0).astype(BF16)
    if all_ref.shape[0] > SHARED_ROWS:
        all_ref[SHARED_ROWS:, :] = jnp.zeros((all_ref.shape[0] - SHARED_ROWS, width), BF16)
    half = all_ref.shape[0] // 2
    core = core_ref[0]
    keep_ref[...] = all_ref[pl.ds(pl.multiple_of(core * half, half), half), :]
    send_ref[...] = all_ref[pl.ds(pl.multiple_of((1 - core) * half, half), half), :]


def shared_out_kernel(
    at_ref, mine_ref, other_ref,
    t0_ref, t1_ref, t2_ref, embb_ref, gain_ref, offset_ref, att_ref, up_ref, down_ref, pw_ref, pb_ref,
    all_ref,
):
    half = all_ref.shape[0] // 2
    core = at_ref[0]
    place = at_ref[1]
    all_ref[pl.ds(pl.multiple_of(core * half, half), half), :] = mine_ref[...].astype(F32)
    all_ref[pl.ds(pl.multiple_of((1 - core) * half, half), half), :] = other_ref[...].astype(F32)
    at = 0
    for out in (t0_ref, t1_ref, t2_ref):
        out[...] = all_ref[at : at + out.shape[0], :]
        at += out.shape[0]
    pw_ref[...] = all_ref[at : at + pw_ref.shape[1], :].T
    v = VECTOR_ROW
    width = all_ref.shape[1]
    pb_ref[...] = all_ref[v : v + 1, : pb_ref.shape[1]]
    embb_ref[...] = all_ref[v + 1 : v + 4, :]
    att_ref[0, :, :] = all_ref[v + 4 : v + 7, :]
    att_ref[1, :, :] = all_ref[v + 7 : v + 10, :]
    for l in range(2):
        for b in range(4):
            row = v + 10 + 4 * l + b
            up_ref[l : l + 1, b * width : (b + 1) * width] = all_ref[row : row + 1, :]
    down_ref[...] = all_ref[v + 18 : v + 20, :]
    gain_ref[...] = all_ref[pl.ds(v + 20 + place, 1), :]
    offset_ref[...] = all_ref[pl.ds(v + 24 + place, 1), :]


def entry_out_kernel(core_ref, att_ref, att_other_ref, up_ref, up_other_ref, out_ref):
    rows = out_ref.shape[0] // 2
    width = att_ref.shape[1]

    def write(low, high):
        for b in range(out_ref.shape[1] // width):
            cols = slice(b * width, (b + 1) * width)
            out_ref[:rows, cols] = low[b * rows : (b + 1) * rows, :].astype(F32)
            out_ref[rows:, cols] = high[b * rows : (b + 1) * rows, :].astype(F32)

    pl.when(core_ref[0] == 0)(lambda: write(att_ref, att_other_ref))
    pl.when(core_ref[0] == 1)(lambda: write(up_other_ref, up_ref))


def call(kernel, kinds, outs, scratch=(), vmem=32 << 20, flops=0, nbytes=0):
    spaces = {
        "s": pl.BlockSpec(memory_space=pltpu.SMEM),
        "a": pl.BlockSpec(memory_space=pl.ANY),
        "v": pl.BlockSpec(memory_space=pltpu.VMEM),
    }

    def run(*args):
        return pl.pallas_call(
            kernel,
            out_shape=[jax.ShapeDtypeStruct(s, d) for s, d in outs],
            in_specs=[spaces[k] for k in kinds],
            out_specs=[spaces["v"]] * len(outs),
            scratch_shapes=list(scratch),
            compiler_params=pltpu.CompilerParams(vmem_limit_bytes=vmem),
            cost_estimate=pl.CostEstimate(flops=flops, bytes_accessed=nbytes, transcendentals=0),
        )(*args)

    return run


def scalars(*values):
    return jnp.stack([jnp.asarray(v, jnp.int32) for v in values])


def attention_fwd(at, weights, x, bias, norm, segc, segr):
    n, d = x.shape
    return call(
        attention_forward_kernel,
        "saaaavvvvv",
        [((n, d), BF16), ((n, d), F32), ((n, 3 * d), BF16), ((n, d), BF16), ((HEADS, n), F32)],
        [pltpu.VMEM((n, n), F32), pltpu.VMEM(weights[0].shape, BF16), pltpu.SemaphoreType.DMA((1,))],
        flops=5_000_000_000,
    )(at, *weights, x, bias, norm, segc, segr)


def feed_scratch(up, down):
    return [
        pltpu.VMEM(up.shape, BF16),
        pltpu.VMEM((2 * down.shape[0], down.shape[1]), BF16),
    ]


def feed_fwd(at, ups, downs, x, upb, downb, norm):
    n, d = x.shape
    ff = ups[0].shape[1]
    return call(
        feed_forward_kernel,
        "saaaaaaaavvvv",
        [((n, d), BF16), ((n, d), F32), ((n, ff), BF16), ((n, ff), BF16)],
        feed_scratch(ups[0], downs[0]) + [pltpu.SemaphoreType.DMA((3,))],
        flops=5_000_000_000,
    )(at, *ups, *downs, x, upb, downb, norm)


def last_feed(at, ups, downs, x, upb, downb, norm, pm, pb, adj):
    n, d = x.shape
    ff = ups[0].shape[1]
    out = pm.shape[1]
    share = ff // d * (d // 2) + ff // 2
    return call(
        last_feed_kernel,
        "saaaaaaaavvvvvvv",
        [
            ((n, out), BF16), ((out, d), F32), ((1, out), F32), ((n, d), BF16),
            ((share, d), BF16), ((share, d), BF16), ((ff // d, d), F32), ((3, d), F32),
        ],
        [pltpu.VMEM((n, ff), BF16), pltpu.VMEM((n, ff), BF16)]
        + feed_scratch(ups[0], downs[0])
        + [pltpu.VMEM((d, n), BF16), pltpu.VMEM((n, d), F32), pltpu.SemaphoreType.DMA((3,))],
        flops=8_000_000_000,
    )(at, *ups, *downs, x, upb, downb, norm, pm, pb, adj)


def feed_bwd(at, ups, downs, g, x, z, h, dd, norm):
    n, d = x.shape
    ff = ups[0].shape[1]
    share = ff // d * (d // 2) + ff // 2
    return call(
        feed_back_kernel,
        "saaaaaaaavvvvvv",
        [((n, d), BF16), ((share, d), BF16), ((share, d), BF16), ((ff // d, d), F32), ((3, d), F32)],
        feed_scratch(ups[0], downs[0])
        + [pltpu.VMEM((d, n), BF16), pltpu.VMEM((n, d), F32), pltpu.SemaphoreType.DMA((3,))],
        flops=6_000_000_000,
    )(at, *ups, *downs, g, x, z, h, dd, norm)


def attention_bwd(at, weights, g, x, z, qkv, o, lse, norm, segc, segr):
    n, d = x.shape
    return call(
        attention_back_kernel,
        "saaaavvvvvvvvv",
        [((n, d), BF16), ((2 * d, d), BF16), ((2 * d, d), BF16), ((5, d), F32)],
        [
            pltpu.VMEM((n, n), F32), pltpu.VMEM((n, 3 * d), BF16), pltpu.VMEM((n, d), BF16),
            pltpu.VMEM(weights[0].shape, BF16), pltpu.VMEM((d, n), BF16), pltpu.SemaphoreType.DMA((1,)),
        ],
        flops=7_000_000_000,
    )(at, *weights, g, x, z, qkv, o, lse, norm, segc, segr)


def embed_fwd(tok, cls, t0, t1, t2, off):
    return call(embed_kernel, "vvvvvv", [((tok.shape[0], t0.shape[1]), BF16)], flops=1_500_000_000)(
        tok, cls, t0, t1, t2, off
    )[0]


def embed_bwd(core, g, tok, cls, tables, small, rows):
    d = g.shape[1]
    return call(
        embed_back_kernel,
        "svvvvvv" + "v" * len(small),
        [(tok.shape, F32), ((rows // 2, d), BF16), ((rows // 2, d), BF16)],
        [pltpu.VMEM((rows, d), BF16)],
        flops=2_000_000_000,
    )(core, g, tok, cls, *tables, *small)


def shared_out(at, mine, other, tables, horizon, ff):
    d = mine.shape[1]
    return call(
        shared_out_kernel,
        "svv",
        [(t.shape, F32) for t in tables]
        + [((3, d), F32), ((1, d), F32), ((1, d), F32), ((2, 3, d), F32), ((2, ff), F32), ((2, d), F32)]
        + [((d, horizon), F32), ((1, horizon), F32)],
        [pltpu.VMEM((2 * mine.shape[0], d), F32)],
        nbytes=4_000_000,
    )(at, mine, other)


def entry_out(core, att, att_other, up, up_other, shape):
    return call(entry_out_kernel, "svvvv", [(shape, F32)], nbytes=8_000_000)(
        core, att, att_other, up, up_other
    )[0]


def row_layout(variate_tallies, lookback_classes, row_len):
    window_end = jnp.cumsum(variate_tallies, -1)
    position = jnp.arange(row_len, dtype=jnp.int32)
    packed_fragment = jnp.sum(
        (position[None, :, None] >= window_end[:, None, :]).astype(jnp.int32), -1
    )
    windows = jnp.arange(variate_tallies.shape[-1], dtype=jnp.int32)
    picked = jnp.sum(
        jnp.where(
            packed_fragment[:, :, None] == windows[None, None, :], lookback_classes[:, None, :], 0
        ),
        -1,
    )
    return (packed_fragment, picked)


def move(array, axis, pairs):
    return lax.ppermute(array, axis, pairs)


def bits_of(axis, mask):
    place = lax.axis_index(axis)
    index = 0
    for position, m in enumerate(mask):
        index = index + ((place & m) // m) * (1 << position)
    return index


def xor_swap(array, dim, k, plane=None):
    axis, mask = dim
    flip = sum(m for position, m in enumerate(mask) if k >> position & 1)
    size = lax.axis_size(axis)
    if plane is None:
        return lax.ppermute(array, axis, [(i, i ^ flip) for i in range(size)])
    dp = lax.axis_size("dp")
    cells = [c for c in range(lax.axis_size("pipe")) if c // 2 == plane]
    return lax.ppermute(
        array, ("pipe", "dp"), [(c * dp + i, c * dp + (i ^ flip)) for c in cells for i in range(dp)]
    )


def combine_kernel(count, ways, g_ref, *refs):
    ins, outs = refs[:count], refs[count:]
    rows = outs[0].shape[0]
    step = 128 if rows % 128 == 0 else rows
    for k in range(ways):
        base = (g_ref[0] ^ k) * rows
        for r in range(0, rows, step):
            at = pl.ds(pl.multiple_of(base + r, 16), step)
            total = ins[0][at, :].astype(F32)
            for one in ins[1:]:
                total = total + one[at, :].astype(F32)
            outs[k][r : r + step, :] = total.astype(outs[k].dtype)


def combine(arrays, group, ways):
    rows, cols = arrays[0].shape
    return call(
        functools.partial(combine_kernel, len(arrays), ways),
        "s" + "v" * len(arrays),
        [((rows // ways, cols), BF16)] * ways,
        vmem=20 << 20,
        nbytes=rows * cols,
    )(scalars(group), *arrays)


def assemble_kernel(ways, g_ref, *refs):
    out = refs[ways]
    rows = refs[0].shape[0]
    for k in range(ways):
        base = pl.multiple_of((g_ref[0] ^ k) * rows, 16)
        out[pl.ds(base, rows), :] = refs[k][...].astype(out.dtype)


def assemble(arrays, group, dtype=BF16):
    ways = len(arrays)
    rows, cols = arrays[0].shape
    return call(
        functools.partial(assemble_kernel, ways),
        "s" + "v" * ways,
        [((rows * ways, cols), dtype)],
        vmem=20 << 20,
        nbytes=rows * ways * cols,
    )(scalars(group), *arrays)[0]


def dims_of(name):
    if name == "x":
        return [("pipe", (2,))]
    if name == "c":
        return [("pipe", (1,))]
    size = lax.axis_size("dp")
    if name == "y":
        return [("dp", (1,))]
    rest = []
    m = 2
    while m < size:
        rest.append(m)
        m *= 2
    return [("dp", tuple(rest[i : i + 2])) for i in range(0, len(rest), 2)]


def reduce_rows(arrays, order, target=None):
    plane = None
    for name in order:
        if name == "t":
            one = combine(arrays, 0, 1)[0] if len(arrays) > 1 else arrays[0]
            pairs = [(2 * (1 - target) + c, 2 * target + c) for c in range(2)]
            arrays = [one, lax.ppermute(one, "pipe", pairs)]
            plane = target
            continue
        if name == "b":
            one = combine(arrays, 0, 1)[0] if len(arrays) > 1 else arrays[0]
            arrays = [one, xor_swap(one, ("pipe", (2,)), 1)]
            continue
        for dim in dims_of(name):
            ways = 1 << len(dim[1])
            pieces = combine(arrays, bits_of(*dim), ways)
            arrays = [pieces[0]] + [xor_swap(pieces[k], dim, k, plane) for k in range(1, ways)]
    return combine(arrays, 0, 1)[0]


def gather_rows(piece, order, plane=None):
    for name in order:
        for dim in reversed(dims_of(name)):
            ways = 1 << len(dim[1])
            swap_plane = None if name == "x" else plane
            piece = assemble(
                [piece] + [xor_swap(piece, dim, k, swap_plane) for k in range(1, ways)], bits_of(*dim)
            )
    return piece


def all_sum(arrays, order, target=None):
    back = "".join(n for n in reversed(order) if n not in "tb")
    piece = reduce_rows(arrays, order, target)
    return gather_rows(piece, back, None if "x" in order else target)


ORDERS = {"feed1": "tyz", "att1": "yzt", "feed0": "xyz", "att0": "yzt", "shared": "yzb"}


def per_device(
    lookback_readings,
    prediction_adjoint,
    variate_tallies,
    lookback_classes,
    brief_lift_table,
    moderate_lift_table,
    distant_lift_table,
    lift_offsets,
    part_entry_arrays,
    part_shrink_lines,
    part_layernorm_scale,
    part_layernorm_offset,
    mixing_offsets,
    expand_offsets,
    shrink_offsets,
    prediction_matrix,
    prediction_offset,
):
    place = lax.axis_index("pipe")
    core, far = place & 1, place // 2
    tok = lookback_readings[0]
    adjoint = prediction_adjoint[0]
    count = tok.shape[0]
    tables = (brief_lift_table, moderate_lift_table, distant_lift_table)
    entry, shrink = part_entry_arrays[0], part_shrink_lines[0]

    cores = [(0, 1), (1, 0), (2, 3), (3, 2)]
    att_x = move(entry, "pipe", [(0, 2), (2, 0)])
    entry_c = move(entry, "pipe", cores)
    shrink_c = move(shrink, "pipe", cores)
    norm = jnp.concatenate([part_layernorm_scale, part_layernorm_offset], 0)[None]
    norm = assemble_norm(norm, place)
    att_xc = move(att_x, "pipe", [(0, 1), (2, 3)])
    entry_f, att_x = lax.optimization_barrier((entry, att_x))
    up_x = move(entry_f, "pipe", [(1, 3), (3, 1)])
    up_xc = move(up_x, "pipe", [(1, 0), (3, 2)])
    shrink_x = spread(shrink)
    shrink_xc = move(shrink_x, "pipe", cores)
    atts = (entry, entry_c, att_x, att_xc)
    ups = (entry, entry_c, up_x, up_xc)
    downs = (shrink, shrink_c, shrink_x, shrink_xc)

    def att_at(layer):
        return scalars(2 * (far ^ layer) + core, core)

    def feed_at(layer):
        away = 2 * (far ^ layer)
        return scalars(away + 1 - core, away + core, away + 1 - core, core)

    tallies = lax.dynamic_index_in_dim(variate_tallies, place, 0, False)
    classes = lax.dynamic_index_in_dim(lookback_classes, place, 0, False)
    fragment, picked = row_layout(tallies, classes, count)
    segc, segr = fragment.reshape(-1, 1), fragment.reshape(1, -1)
    cls = picked.reshape(-1, 1)

    x0 = embed_fwd(tok, cls, *tables, lift_offsets)
    x1, z0, qkv0, o0, lse0 = attention_fwd(
        att_at(0), atts, x0, mixing_offsets[0], norm[0], segc, segr
    )
    x2, z1, h1, d1 = feed_fwd(
        feed_at(0), ups, downs, x1, expand_offsets[0:1], shrink_offsets[0:1], norm[1]
    )
    x3, z2, qkv2, o2, lse2 = attention_fwd(
        att_at(1), atts, x2, mixing_offsets[1], norm[2], segc, segr
    )
    prediction, gpm, gpb, g, keep3, send3, upb1, vec3 = last_feed(
        feed_at(1), ups, downs, x3, expand_offsets[1:2], shrink_offsets[1:2], norm[3],
        prediction_matrix, prediction_offset[None], adjoint,
    )
    g, keep2, send2, vec2 = attention_bwd(
        att_at(1), atts, g, x2, z2, qkv2, o2, lse2, norm[2], segc, segr
    )
    g, keep1, send1, upb0, vec1 = feed_bwd(feed_at(0), ups, downs, g, x1, z1, h1, d1, norm[1])
    g, keep0, send0, vec0 = attention_bwd(
        att_at(0), atts, g, x0, z0, qkv0, o0, lse0, norm[0], segc, segr
    )
    shared_rows = max(SHARED_ROWS, 32 * lax.axis_size("dp"))
    series, keeps, sends = embed_bwd(
        scalars(core), g, tok, cls, tables, (gpm, gpb, vec0, vec1, vec2, vec3, upb0, upb1), shared_rows
    )

    def chunk(keep, send, name, target):
        return all_sum([keep, move(send, "pipe", cores)], ORDERS[name], target)

    feeds = [chunk(keep1, send1, "feed0", 0), chunk(keep3, send3, "feed1", 1)]
    attns = [chunk(keep0, send0, "att0", 0), chunk(keep2, send2, "att1", 1)]
    feed = jnp.where(far == 0, feeds[0], feeds[1])
    att = jnp.where(far == 0, attns[0], attns[1])
    shared = chunk(keeps, sends, "shared", None)
    shared_other = move(shared, "pipe", cores)
    rows = entry.shape[0] * entry.shape[1] // shrink.shape[1] // 2
    up, down_grad = feed[:rows], feed[rows:].astype(F32)
    up_other = move(up, "pipe", [(0, 1), (2, 3)])
    att_other = move(att, "pipe", [(1, 0), (3, 2)])
    entry_grad = entry_out(scalars(core), att, att_other, up, up_other, entry.shape)
    t0, t1, t2, embb, gain, offset, attb, upb, downb, pw, pb = shared_out(
        scalars(core, place), shared, shared_other, tables, prediction_matrix.shape[1], entry.shape[1]
    )
    return (
        prediction[None],
        series[None],
        t0,
        t1,
        t2,
        embb,
        entry_grad[None],
        down_grad[None],
        gain,
        offset,
        attb,
        upb,
        downb,
        pw,
        pb[0],
    )


def assemble_norm(own, place):
    cores = [(0, 1), (1, 0), (2, 3), (3, 2)]
    other = lax.ppermute(own, "pipe", cores)
    chip = jnp.where(place & 1 == 0, jnp.concatenate([own, other]), jnp.concatenate([other, own]))
    away = xor_swap(chip, ("pipe", (2,)), 1)
    return jnp.where(place // 2 == 0, jnp.concatenate([chip, away]), jnp.concatenate([away, chip]))


def spread(array):
    size = lax.axis_size("dp")
    rows = array.shape[0] // size
    share = lax.dynamic_slice_in_dim(array, bits_over_dp() * rows, rows, 0)
    return gather_rows(xor_swap(share, ("pipe", (2,)), 1), "zy")


def bits_over_dp():
    index = 0
    for name in "yz":
        for dim in dims_of(name):
            index = index * (1 << len(dim[1])) + bits_of(*dim)
    return index


def solution(mesh):
    placed = (
        P("pipe", "dp", None),
        P("pipe", "dp", None),
        P(None, "dp", None),
        P(None, "dp", None),
        P(),
        P(),
        P(),
        P(),
        P("pipe", None, None),
        P("pipe", None, None),
        P("pipe", None),
        P("pipe", None),
        P(),
        P(),
        P(),
        P(),
        P(),
    )
    return jax.shard_map(
        per_device,
        mesh=mesh,
        in_specs=placed,
        out_specs=(
            P("pipe", "dp", None),
            P("pipe", "dp", None),
            P(),
            P(),
            P(),
            P(),
            P("pipe", None, None),
            P("pipe", None, None),
            P("pipe", None),
            P("pipe", None),
            P(),
            P(),
            P(),
            P(),
            P(),
        ),
        check_vma=False,
    )
```

```python
import functools

import jax
import jax.numpy as jnp
from jax import lax
from jax.experimental import pallas as pl
from jax.experimental.pallas import tpu as pltpu
from jax.sharding import PartitionSpec as P

HEADS = 8
HEAD_DIM = 64
F32 = jnp.float32
BF16 = jnp.bfloat16
VECTOR_ROW = 624
VECTORS = 16


def nn(a, b):
    return lax.dot_general(a, b, (((1,), (0,)), ((), ())), preferred_element_type=F32)


def nt(a, b):
    return lax.dot_general(a, b, (((1,), (1,)), ((), ())), preferred_element_type=F32)


def tn(a, b):
    return lax.dot_general(a, b, (((0,), (0,)), ((), ())), preferred_element_type=F32)


def column_sum(a):
    return jnp.sum(a.astype(F32), 0, keepdims=True)


def normalise(z):
    centre = z - jnp.mean(z, -1, keepdims=True)
    inverse = lax.rsqrt(jnp.mean(centre * centre, -1, keepdims=True) + 1e-05)
    return centre * inverse, inverse


def norm_back(upstream, z, gain):
    normed, inverse = normalise(z)
    gain_grad = jnp.sum(upstream * normed, 0, keepdims=True)
    offset_grad = jnp.sum(upstream, 0, keepdims=True)
    scaled = upstream * gain
    back = inverse * (
        scaled
        - jnp.mean(scaled, -1, keepdims=True)
        - normed * jnp.mean(scaled * normed, -1, keepdims=True)
    )
    return back, gain_grad, offset_grad


def gelu_both(u):
    bell = jnp.exp(u * u * -0.5)
    t = 1.0 / (1.0 + (0.3275911 * 0.5**0.5) * jnp.abs(u))
    poly = t * (
        0.127414796
        + t * (-0.142248368 + t * (0.7107068705 + t * (-0.7265760135 + t * 0.5307027145)))
    )
    half = poly * bell
    phi = jnp.where(u >= 0, 1.0 - half, half)
    return u * phi, phi + u * bell * 0.3989422804014327


def same_window_bias(seg_col, seg_row):
    return jnp.where(seg_col == seg_row, 0.0, -1e30).astype(F32)


class Choice:
    def __init__(self, index, sources, place, sem):
        self.index = index
        self.copies = [pltpu.make_async_copy(s, place, sem) for s in sources]

    def start(self):
        for k, copy in enumerate(self.copies):
            pl.when(self.index == k)(copy.start)

    def wait(self):
        for k, copy in enumerate(self.copies):
            pl.when(self.index == k)(copy.wait)


def weight_loads(core, entry, other, shrink, shrink_other, att_ref, up_ref, down_ref, sem):
    loads = []
    if att_ref is not None:
        loads.append(Choice(core, (entry, other), att_ref, sem.at[0]))
    if up_ref is not None:
        loads.append(Choice(1 - core, (entry, other), up_ref, sem.at[1]))
        half = down_ref.shape[0] // 2
        low, high = down_ref.at[pl.ds(0, half)], down_ref.at[pl.ds(half, half)]
        loads.append(Choice(core, (shrink, shrink_other), low, sem.at[2]))
        loads.append(Choice(1 - core, (shrink, shrink_other), high, sem.at[3]))
    for one in loads:
        one.start()
    return loads


def chosen_norms(core, own_ref, other_ref):
    own, other = own_ref[...], other_ref[...]
    first = core == 0
    return jnp.where(first, own, other), jnp.where(first, other, own)


def attention_core(x, w_ref, bias_ref, norm, mask_ref, qkv_ref, o_ref, lse_ref, z_ref):
    width = x.shape[1]
    qkv_ref[:, :width] = ((nn(x, w_ref[:, :width]) + bias_ref[0:1, :]) * HEAD_DIM**-0.5).astype(BF16)
    qkv_ref[:, width : 2 * width] = nn(x, w_ref[:, width : 2 * width]).astype(BF16)
    qkv_ref[:, 2 * width : 3 * width] = (
        nn(x, w_ref[:, 2 * width : 3 * width]) + bias_ref[1:2, :]
    ).astype(BF16)
    pair = 2 * HEAD_DIM
    low = lax.broadcasted_iota(jnp.int32, (1, pair), 1) < HEAD_DIM
    for p in range(HEADS // 2):
        q2 = qkv_ref[:, p * pair : (p + 1) * pair]
        k2 = qkv_ref[:, width + p * pair : width + (p + 1) * pair]
        v2 = qkv_ref[:, 2 * width + p * pair : 2 * width + (p + 1) * pair]
        v2t = v2.T
        parts = []
        for h in range(2):
            kh = jnp.where(low if h == 0 else ~low, k2, jnp.zeros_like(k2))
            s = nt(kh, q2) + mask_ref[...]
            top = jnp.max(s, 0, keepdims=True)
            e = jnp.exp(s - top)
            total = jnp.sum(e, 0, keepdims=True)
            lse_ref[2 * p + h : 2 * p + h + 1, :] = top + jnp.log(total)
            ot = nn(v2t[h * HEAD_DIM : (h + 1) * HEAD_DIM, :], e.astype(BF16))
            parts.append(ot * (1.0 / total))
        o_ref[:, p * pair : (p + 1) * pair] = jnp.concatenate(parts, 0).T.astype(BF16)
    z = x.astype(F32) + (nn(o_ref[...], w_ref[:, 3 * width :]) + bias_ref[2:3, :])
    z_ref[...] = z
    return (normalise(z)[0] * norm[0:1, :] + norm[1:2, :]).astype(BF16)


def feed_core(x, up_ref, down_ref, upb_ref, downb_ref, norm, h_ref, d_ref, z_ref, block=512):
    total = None
    for c in range(0, up_ref.shape[1], block):
        u = nn(x, up_ref[:, c : c + block]) + upb_ref[:, c : c + block]
        h, d = gelu_both(u)
        hb = h.astype(BF16)
        h_ref[:, c : c + block] = hb
        d_ref[:, c : c + block] = d.astype(BF16)
        part = nn(hb, down_ref[c : c + block, :])
        total = part if total is None else total + part
    z = x.astype(F32) + (total + downb_ref[...])
    z_ref[...] = z
    return (normalise(z)[0] * norm[0:1, :] + norm[1:2, :]).astype(BF16)


def feed_back_chain(upstream, z_ref, d_ref, up_ref, down_ref, norm, gu_ref, gf_ref, vec_ref, gx_acc):
    back, gain_grad, offset_grad = norm_back(upstream, z_ref[...], norm[0:1, :])
    gf_ref[...] = back.astype(BF16)
    gx_acc[...] = back
    width = back.shape[1]
    for b in range(up_ref.shape[1] // width):
        cols = slice(b * width, (b + 1) * width)
        gu = (nt(gf_ref[...], down_ref[cols, :]) * d_ref[:, cols].astype(F32)).astype(BF16)
        gu_ref[:, cols] = gu
        vec_ref[7 + b : 8 + b, :] = column_sum(gu)
        gx_acc[...] += nt(gu, up_ref[:, cols])
    vec_ref[11:12, :] = column_sum(gf_ref[...])
    vec_ref[14:15, :] = gain_grad
    vec_ref[15:16, :] = offset_grad


def attention_back_chain(
    upstream, z_ref, qkv_ref, o_ref, lse_ref, w_ref, norm, mask_ref,
    gqkv_ref, ga_ref, go_ref, vec_ref, gx_acc,
):
    back, gain_grad, offset_grad = norm_back(upstream, z_ref[...], norm[0:1, :])
    width = back.shape[1]
    ga_ref[...] = back.astype(BF16)
    gx_acc[...] = back
    vec_ref[6:7, :] = column_sum(ga_ref[...])
    vec_ref[12:13, :] = gain_grad
    vec_ref[13:14, :] = offset_grad
    go_ref[...] = nt(ga_ref[...], w_ref[:, 3 * width :]).astype(BF16)
    pair = 2 * HEAD_DIM
    low = lax.broadcasted_iota(jnp.int32, (1, pair), 1) < HEAD_DIM
    for p in range(HEADS // 2):
        q2 = qkv_ref[:, p * pair : (p + 1) * pair]
        k2 = qkv_ref[:, width + p * pair : width + (p + 1) * pair]
        v2 = qkv_ref[:, 2 * width + p * pair : 2 * width + (p + 1) * pair]
        go2 = go_ref[:, p * pair : (p + 1) * pair]
        o2 = o_ref[:, p * pair : (p + 1) * pair]
        k2t = k2.T
        prod = (go2.astype(F32) * o2.astype(F32)).T
        gq, gk, gv = [], None, None
        for h in range(2):
            own = low if h == 0 else ~low
            zero = jnp.zeros_like(k2)
            lanes = slice(h * HEAD_DIM, (h + 1) * HEAD_DIM)
            centred = jnp.sum(prod[lanes, :], 0, keepdims=True)
            s = nt(jnp.where(own, k2, zero), q2) + mask_ref[...]
            weights = jnp.exp(s - lse_ref[2 * p + h : 2 * p + h + 1, :])
            gp = nt(jnp.where(own, v2, zero), go2)
            gs = (weights * (gp - centred)).astype(BF16)
            gv_part = nn(weights.astype(BF16), jnp.where(own, go2, zero))
            gk_part = nn(gs, jnp.where(own, q2, zero))
            gv = gv_part if gv is None else gv + gv_part
            gk = gk_part if gk is None else gk + gk_part
            gq.append(nn(k2t[lanes, :], gs) * HEAD_DIM**-0.5)
        cols = slice(p * pair, (p + 1) * pair)
        gqkv_ref[:, cols] = jnp.concatenate(gq, 0).T.astype(BF16)
        gqkv_ref[:, width + p * pair : width + (p + 1) * pair] = gk.astype(BF16)
        gqkv_ref[:, 2 * width + p * pair : 2 * width + (p + 1) * pair] = gv.astype(BF16)
    gx_acc[...] += nt(gqkv_ref[...], w_ref[:, : 3 * width])
    vec_ref[4:5, :] = column_sum(gqkv_ref[:, :width])
    vec_ref[5:6, :] = column_sum(gqkv_ref[:, 2 * width :])


def shares(core, rows):
    mine = pl.ds(pl.multiple_of(core * rows, rows), rows)
    other = pl.ds(pl.multiple_of((1 - core) * rows, rows), rows)
    return mine, other


def feed_weight_grads(core, rows_of, prior, keep_ref, send_ref, xt_ref):
    width = rows_of[0][0].shape[1]
    half = width // 2
    blocks = rows_of[0][1].shape[1] // width
    for i, (x, _, _, _) in enumerate(rows_of):
        xt_ref[i] = x[...].T
    mine, other = shares(core, half)

    def put(out, index, at, size, value):
        if prior is not None:
            value = value + prior[index][at, :].astype(F32)
        out[at, :] = value.astype(BF16)

    for j in range(blocks):
        b = lax.rem(j + core * (blocks // 2), blocks)
        cols = pl.ds(pl.multiple_of(b * width, width), width)
        index = j // (blocks // 2)
        at = blocks * half + (j % (blocks // 2)) * width
        value = sum(tn(h[:, cols], gf[...]) for _, h, _, gf in rows_of)
        put((keep_ref, send_ref)[index], index, slice(at, at + width), width, value)
        at = pl.ds(pl.multiple_of(b * half, half), half)
        for index, (out, part) in enumerate(((keep_ref, mine), (send_ref, other))):
            value = sum(nn(xt_ref[i, part, :], gu[:, cols]) for i, (_, _, gu, _) in enumerate(rows_of))
            put(out, index, at, half, value)


def attention_weight_grads(core, rows_of, prior, keep_ref, send_ref, xt_ref, ot_ref):
    width = rows_of[0][0].shape[1]
    half = width // 2
    mine, other = shares(core, half)

    def put(out, index, b, value):
        at = slice(b * half, (b + 1) * half)
        if prior is not None:
            value = value + prior[index][at, :].astype(F32)
        out[at, :] = value.astype(BF16)

    for i, (x, _, _, _) in enumerate(rows_of):
        xt_ref[i] = x[...].T
    for b in range(3):
        for index, (out, part) in enumerate(((keep_ref, mine), (send_ref, other))):
            put(out, index, b, sum(
                nn(xt_ref[i, part, :], gqkv[:, b * width : (b + 1) * width])
                for i, (_, gqkv, _, _) in enumerate(rows_of)
            ))
    for i, (_, _, o, _) in enumerate(rows_of):
        ot_ref[i] = o[...].T
    for index, (out, part) in enumerate(((keep_ref, mine), (send_ref, other))):
        put(out, index, 3, sum(
            nn(ot_ref[i, part, :], ga[...]) for i, (_, _, _, ga) in enumerate(rows_of)
        ))


def padded_table(t_ref, look):
    table = t_ref[...]
    skip = look - table.shape[0]
    if skip:
        table = jnp.concatenate([jnp.zeros((skip, table.shape[1]), BF16), table], 0)
    return table, skip


def embed(tok, cls, tables, off_ref):
    total = None
    for g, t_ref in enumerate(tables):
        chosen = cls == g
        masked = jnp.where(chosen, tok, jnp.zeros_like(tok))
        table, _ = padded_table(t_ref, tok.shape[1])
        part = nn(masked, table) + jnp.where(chosen, off_ref[g : g + 1, :], 0.0)
        total = part if total is None else total + part
    return total.astype(BF16)


def first_layer_kernel(
    at, entry, other, shrink, shrink_other,
    tok_ref, cls_ref, t0_ref, t1_ref, t2_ref, off_ref, bias_ref, upb_ref, downb_ref,
    norm_ref, norm_other_ref, segc_ref, segr_ref,
    x2_ref, x0_ref, z0_ref, qkv_ref, o_ref, lse_ref, x1_ref, z1_ref, h_ref, d_ref,
    mask_ref, att_ref, up_ref, down_ref, sem,
):
    @pl.when(at[1] == 0)
    def _():
        core = at[0]
        loads = weight_loads(
            core, entry, other, shrink, shrink_other, att_ref, up_ref, down_ref, sem
        )
        x0_ref[...] = embed(tok_ref[...], cls_ref[...], (t0_ref, t1_ref, t2_ref), off_ref)
        mask_ref[...] = same_window_bias(segc_ref[...], segr_ref[...])
        norm_att, norm_feed = chosen_norms(core, norm_ref, norm_other_ref)
        loads[0].wait()
        x1_ref[...] = attention_core(
            x0_ref[...], att_ref, bias_ref, norm_att, mask_ref, qkv_ref, o_ref, lse_ref, z0_ref
        )
        for one in loads[1:]:
            one.wait()
        x2_ref[...] = feed_core(
            x1_ref[...], up_ref, down_ref, upb_ref, downb_ref, norm_feed, h_ref, d_ref, z1_ref
        )


def second_layer_kernel(
    at, entry, other, shrink, shrink_other,
    x2_ref, adj_ref, pm_ref, pb_ref, bias_ref, upb_ref, downb_ref,
    norm_ref, norm_other_ref, segc_ref, segr_ref,
    g_ref, pred_ref, gqkv_ref, o_ref, ga_ref, x3_ref, gu_ref, h_ref, gf_ref, vec_ref, gpm_ref,
    mask_ref, att_ref, up_ref, down_ref, qkv_ref, lse_ref, z2_ref, z3_ref, d_ref, gx_acc, go_ref, sem,
):
    @pl.when(at[1] == 1)
    def _():
        core = at[0]
        loads = weight_loads(
            core, entry, other, shrink, shrink_other, att_ref, up_ref, down_ref, sem
        )
        mask_ref[...] = same_window_bias(segc_ref[...], segr_ref[...])
        norm_att, norm_feed = chosen_norms(core, norm_ref, norm_other_ref)
        loads[0].wait()
        x3_ref[...] = attention_core(
            x2_ref[...], att_ref, bias_ref, norm_att, mask_ref, qkv_ref, o_ref, lse_ref, z2_ref
        )
        for one in loads[1:]:
            one.wait()
        y = feed_core(
            x3_ref[...], up_ref, down_ref, upb_ref, downb_ref, norm_feed, h_ref, d_ref, z3_ref
        )
        pm, adj = pm_ref[...], adj_ref[...]
        pred_ref[...] = (nn(y, pm) + pb_ref[...]).astype(BF16)
        gpm_ref[...] = tn(adj, y)
        width = y.shape[1]
        gpb = column_sum(adj)
        vec_ref[0:1, :] = jnp.concatenate([gpb, jnp.zeros((1, width - gpb.shape[1]), F32)], 1)
        vec_ref[1:4, :] = jnp.zeros((3, width), F32)
        feed_back_chain(
            nt(adj, pm), z3_ref, d_ref, up_ref, down_ref, norm_feed, gu_ref, gf_ref, vec_ref, gx_acc
        )
        attention_back_chain(
            gx_acc[...].astype(BF16).astype(F32), z2_ref, qkv_ref, o_ref, lse_ref, att_ref, norm_att,
            mask_ref, gqkv_ref, ga_ref, go_ref, vec_ref, gx_acc,
        )
        g_ref[...] = gx_acc[...].astype(BF16)


def second_weights_kernel(
    at, *refs,
):
    rows = refs[:10], refs[10:20]
    keepf, sendf, keepa, senda, shared_ref, xt_ref, xt2_ref, ot_ref = refs[20:]

    @pl.when(at[1] == 1)
    def _():
        core = at[0]
        feed_weight_grads(
            core, [(r[4], r[6], r[5], r[7]) for r in rows], None, keepf, sendf, xt_ref
        )
        attention_weight_grads(core, [(r[0], r[1], r[2], r[3]) for r in rows], None, keepa, senda, xt2_ref, ot_ref)
        horizon = rows[0][9].shape[0]
        shared_ref[...] = jnp.zeros(shared_ref.shape, F32)
        shared_ref[:horizon, :] = rows[0][9][...] + rows[1][9][...]
        shared_ref[VECTOR_ROW : VECTOR_ROW + VECTORS, :] = rows[0][8][...] + rows[1][8][...]


def first_feed_back_kernel(
    second, at, entry, other, shrink, shrink_other, *refs,
):
    g_ref, x1_ref, z1_ref, h_ref, d_ref, norm_ref, norm_other_ref = refs[:7]
    refs = refs[7:]
    if second:
        keep_in, send_in, keep_far, send_far = refs[:4]
        refs = refs[4:]
    gx_ref, keep_ref, send_ref, vec_ref, up_ref, down_ref, gu_ref, gf_ref, gx_acc, xt_ref, sem = refs

    @pl.when(at[1] == 0)
    def _():
        core = at[0]
        loads = weight_loads(core, entry, other, shrink, shrink_other, None, up_ref, down_ref, sem)
        _, norm_feed = chosen_norms(core, norm_ref, norm_other_ref)
        for one in loads:
            one.wait()
        vec_ref[...] = jnp.zeros(vec_ref.shape, F32)
        feed_back_chain(
            g_ref[...].astype(F32), z1_ref, d_ref, up_ref, down_ref, norm_feed,
            gu_ref, gf_ref, vec_ref, gx_acc,
        )
        gx_ref[...] = gx_acc[...].astype(BF16)
        feed_weight_grads(
            core, [(x1_ref, h_ref, gu_ref, gf_ref)], (keep_in, send_in) if second else None,
            keep_ref, send_ref, xt_ref,
        )

    if second:
        @pl.when(at[1] == 1)
        def _():
            keep_ref[...] = keep_far[...]
            send_ref[...] = send_far[...]


def first_attention_back_kernel(
    second, at, entry, other, *refs,
):
    (g_ref, x0_ref, z0_ref, qkv_ref, o_ref, lse_ref, norm_ref, norm_other_ref, segc_ref, segr_ref,
     tok_ref, cls_ref, t0_ref, t1_ref, t2_ref, vec_in) = refs[:16]
    refs = refs[16:]
    if second:
        keep_in, send_in, shared_in, keep_far, send_far, shared_far = refs[:6]
        series_ref, keep_ref, send_ref, skeep_ref, ssend_ref = refs[6:11]
        refs = refs[11:]
    else:
        series_ref, keep_ref, send_ref, shared_ref = refs[:4]
        refs = refs[4:]
    mask_ref, att_ref, gqkv_ref, ga_ref, go_ref, gx_acc, xt_ref, ot_ref, vec_ref, acc_ref, sem = refs

    def split(total):
        half = skeep_ref.shape[0]
        mine, theirs = shares(at[0], half)
        acc_ref[...] = total
        skeep_ref[...] = acc_ref[mine, :].astype(BF16)
        ssend_ref[...] = acc_ref[theirs, :].astype(BF16)

    @pl.when(at[1] == 0)
    def _():
        core = at[0]
        loads = weight_loads(core, entry, other, None, None, att_ref, None, None, sem)
        norm_att, _ = chosen_norms(core, norm_ref, norm_other_ref)
        mask_ref[...] = same_window_bias(segc_ref[...], segr_ref[...])
        vec_ref[...] = vec_in[...]
        loads[0].wait()
        attention_back_chain(
            g_ref[...].astype(F32), z0_ref, qkv_ref, o_ref, lse_ref, att_ref, norm_att,
            mask_ref, gqkv_ref, ga_ref, go_ref, vec_ref, gx_acc,
        )
        attention_weight_grads(
            core, [(x0_ref, gqkv_ref, o_ref, ga_ref)], (keep_in, send_in) if second else None,
            keep_ref, send_ref, xt_ref, ot_ref,
        )
        g = gx_acc[...].astype(BF16)
        tok, cls = tok_ref[...], cls_ref[...]
        look = tok.shape[1]
        tokt = tok.T
        series = None
        at_row = 0
        out = acc_ref
        for i, t_ref in enumerate((t0_ref, t1_ref, t2_ref)):
            masked = jnp.where(cls == i, g, jnp.zeros_like(g))
            table, skip = padded_table(t_ref, look)
            part = nt(masked, table)
            series = part if series is None else series + part
            count = look - skip
            out[at_row : at_row + count, :] = nn(tokt, masked)[skip:, :]
            at_row += count
            vec_ref[1 + i : 2 + i, :] = column_sum(masked)
        series_ref[...] = series.astype(series_ref.dtype)
        out[VECTOR_ROW : VECTOR_ROW + VECTORS, :] = vec_ref[...]
        rest = VECTOR_ROW + VECTORS
        out[rest:, :] = jnp.zeros((out.shape[0] - rest, out.shape[1]), F32)
        if second:
            split(acc_ref[...] + shared_in[...])
        else:
            shared_ref[...] = acc_ref[...]

    if second:
        @pl.when(at[1] == 1)
        def _():
            keep_ref[...] = keep_far[...]
            send_ref[...] = send_far[...]
            split(shared_far[...])


def shared_out_kernel(
    at, mine_ref, other_ref,
    t0_ref, t1_ref, t2_ref, embb_ref, gain_ref, offset_ref, att_ref, up_ref, down_ref, pw_ref, pb_ref,
    all_ref,
):
    core, far = at[0], at[1]
    half = mine_ref.shape[0] // 2
    size = at.shape[0] - 2
    piece = half // size
    for who, source in ((core, mine_ref), (1 - core, other_ref)):
        for b in range(size):
            to = pl.ds(pl.multiple_of(who * half + b * piece, 16), piece)
            all_ref[far, to, :] = source[2 * b * piece : (2 * b + 1) * piece, :].astype(F32)
            all_ref[1 - far, to, :] = source[(2 * b + 1) * piece : (2 * b + 2) * piece, :].astype(F32)
    row = 0
    for out in (t0_ref, t1_ref, t2_ref):
        out[...] = all_ref[0, row : row + out.shape[0], :]
        row += out.shape[0]
    pw_ref[...] = all_ref[1, : pw_ref.shape[1], :].T
    v = VECTOR_ROW
    width = all_ref.shape[2]
    pb_ref[...] = all_ref[1, v : v + 1, : pb_ref.shape[1]]
    embb_ref[...] = all_ref[0, v + 1 : v + 4, :]
    for l in range(2):
        att_ref[l, :, :] = all_ref[l, v + 4 : v + 7, :]
        for b in range(4):
            up_ref[l : l + 1, b * width : (b + 1) * width] = all_ref[l, v + 7 + b : v + 8 + b, :]
        down_ref[l : l + 1, :] = all_ref[l, v + 11 : v + 12, :]
    gain_ref[...] = all_ref[far, pl.ds(v + 12 + 2 * core, 1), :]
    offset_ref[...] = all_ref[far, pl.ds(v + 13 + 2 * core, 1), :]


def entry_out_kernel(at, att_ref, att_other_ref, up_ref, up_other_ref, out_ref):
    rows = out_ref.shape[0] // 2
    width = att_ref.shape[1]

    def write(low, high):
        for b in range(out_ref.shape[1] // width):
            cols = slice(b * width, (b + 1) * width)
            out_ref[:rows, cols] = low[b * rows : (b + 1) * rows, :].astype(F32)
            out_ref[rows:, cols] = high[b * rows : (b + 1) * rows, :].astype(F32)

    pl.when(at[0] == 0)(lambda: write(att_ref, att_other_ref))
    pl.when(at[0] == 1)(lambda: write(up_other_ref, up_ref))


def call(kernel, kinds, outs, scratch=(), vmem=40 << 20, flops=0, nbytes=0):
    spaces = {
        "s": pl.BlockSpec(memory_space=pltpu.SMEM),
        "a": pl.BlockSpec(memory_space=pl.ANY),
        "v": pl.BlockSpec(memory_space=pltpu.VMEM),
    }

    def run(*args):
        return pl.pallas_call(
            kernel,
            out_shape=[jax.ShapeDtypeStruct(s, d) for s, d in outs],
            in_specs=[spaces[k] for k in kinds],
            out_specs=[spaces["v"]] * len(outs),
            scratch_shapes=[s if not isinstance(s, tuple) else pltpu.VMEM(*s) for s in scratch],
            compiler_params=pltpu.CompilerParams(vmem_limit_bytes=vmem),
            cost_estimate=pl.CostEstimate(flops=flops, bytes_accessed=nbytes, transcendentals=0),
        )(*args)

    return run


def scalars(*values):
    return jnp.stack([jnp.asarray(v, jnp.int32) for v in values])


def first_layer(at, weights, tok, cls, tables, off, bias, upb, downb, norms, segs):
    n, d, ff = tok.shape[0], off.shape[1], upb.shape[1]
    return call(
        first_layer_kernel,
        "saaaa" + "v" * 13,
        [
            ((n, d), BF16), ((n, d), BF16), ((n, d), F32), ((n, 3 * d), BF16), ((n, d), BF16),
            ((HEADS, n), F32), ((n, d), BF16), ((n, d), F32), ((n, ff), BF16), ((n, ff), BF16),
        ],
        [((n, n), F32), ((d, ff), BF16), ((d, ff), BF16), ((ff, d), BF16), pltpu.SemaphoreType.DMA((4,))],
        flops=10_000_000_000,
    )(at, *weights, tok, cls, *tables, off, bias, upb, downb, *norms, *segs)


def second_layer(at, weights, x2, adj, pm, pb, bias, upb, downb, norms, segs):
    n, d = x2.shape
    ff, out = upb.shape[1], pm.shape[1]
    return call(
        second_layer_kernel,
        "saaaa" + "v" * 11,
        [
            ((n, d), BF16), ((n, out), BF16), ((n, 3 * d), BF16), ((n, d), BF16), ((n, d), BF16),
            ((n, d), BF16), ((n, ff), BF16), ((n, ff), BF16), ((n, d), BF16), ((VECTORS, d), F32),
            ((out, d), F32),
        ],
        [
            ((n, n), F32), ((d, ff), BF16), ((d, ff), BF16), ((ff, d), BF16), ((n, 3 * d), BF16),
            ((HEADS, n), F32), ((n, d), F32), ((n, d), F32), ((n, ff), BF16), ((n, d), F32),
            ((n, d), BF16), pltpu.SemaphoreType.DMA((4,)),
        ],
        flops=16_000_000_000,
    )(at, *weights, x2, adj, pm, pb, bias, upb, downb, *norms, *segs)


def share_shapes(d, ff):
    return [((ff // d * (d // 2) + ff // 2, d), BF16)] * 2, [((2 * d, d), BF16)] * 2


def second_weights(at, rows, shared_rows):
    n, d = rows[0][0].shape
    ff = rows[0][5].shape[1]
    feed, att = share_shapes(d, ff)
    return call(
        second_weights_kernel,
        "s" + "v" * 20,
        feed + att + [((shared_rows, d), F32)],
        [((2, d, n), BF16)] * 3,
        flops=6_000_000_000,
    )(at, *rows[0], *rows[1])


def first_feed_back(at, weights, g, x1, z1, h, dd, norms, prior=()):
    n, d = x1.shape
    ff = h.shape[1]
    feed, _ = share_shapes(d, ff)
    return call(
        functools.partial(first_feed_back_kernel, bool(prior)),
        "saaaa" + "v" * (7 + len(prior)),
        [((n, d), BF16)] + feed + [((VECTORS, d), F32)],
        [
            ((d, ff), BF16), ((ff, d), BF16), ((n, ff), BF16), ((n, d), BF16), ((n, d), F32),
            ((1, d, n), BF16), pltpu.SemaphoreType.DMA((4,)),
        ],
        flops=7_000_000_000,
    )(at, *weights, g, x1, z1, h, dd, *norms, *prior)


def first_attention_back(
    at, weights, g, x0, z0, qkv, o, lse, norms, segs, tok, cls, tables, vec, shared_rows, prior=()
):
    n, d = x0.shape
    _, att = share_shapes(d, 4 * d)
    if prior:
        outs = [(tok.shape, BF16)] + att + [((shared_rows // 2, d), BF16)] * 2
    else:
        outs = [(tok.shape, F32)] + att + [((shared_rows, d), F32)]
    return call(
        functools.partial(first_attention_back_kernel, bool(prior)),
        "saa" + "v" * (16 + len(prior)),
        outs,
        [
            ((n, n), F32), ((d, 4 * d), BF16), ((n, 3 * d), BF16), ((n, d), BF16), ((n, d), BF16),
            ((n, d), F32), ((1, d, n), BF16), ((1, d, n), BF16), ((VECTORS, d), F32),
            ((shared_rows, d), F32),
            pltpu.SemaphoreType.DMA((4,)),
        ],
        flops=9_000_000_000,
    )(at, *weights[:2], g, x0, z0, qkv, o, lse, *norms, *segs, tok, cls, *tables, vec, *prior)


def shared_out(core, far, size, mine, other, tables, horizon, ff):
    d = mine.shape[1]
    return call(
        shared_out_kernel,
        "svv",
        [(t.shape, F32) for t in tables]
        + [((3, d), F32), ((1, d), F32), ((1, d), F32), ((2, 3, d), F32), ((2, ff), F32), ((2, d), F32)]
        + [((d, horizon), F32), ((1, horizon), F32)],
        [((2, mine.shape[0], d), F32)],
        nbytes=4_000_000,
    )(scalars(core, far, *([0] * size)), mine, other)


def entry_out(at, att, att_other, up, up_other, shape):
    return call(entry_out_kernel, "svvvv", [(shape, F32)], nbytes=8_000_000)(
        at, att, att_other, up, up_other
    )[0]


def row_layout(variate_tallies, lookback_classes, row_len):
    window_end = jnp.cumsum(variate_tallies, -1)
    position = jnp.arange(row_len, dtype=jnp.int32)
    packed_fragment = jnp.sum(
        (position[None, :, None] >= window_end[:, None, :]).astype(jnp.int32), -1
    )
    windows = jnp.arange(variate_tallies.shape[-1], dtype=jnp.int32)
    picked = jnp.sum(
        jnp.where(
            packed_fragment[:, :, None] == windows[None, None, :], lookback_classes[:, None, :], 0
        ),
        -1,
    )
    return (packed_fragment, picked)


CORES = [(0, 1), (1, 0), (2, 3), (3, 2)]
TO_NEAR = [(2, 0), (3, 1)]
TO_FAR = [(0, 2), (1, 3)]


def move(array, pairs):
    return lax.ppermute(array, "pipe", pairs)


def bits_of(axis, mask):
    place = lax.axis_index(axis)
    index = 0
    for position, m in enumerate(mask):
        index = index + ((place & m) // m) * (1 << position)
    return index


def xor_swap(array, dim, k):
    axis, mask = dim
    flip = sum(m for position, m in enumerate(mask) if k >> position & 1)
    return lax.ppermute(array, axis, [(i, i ^ flip) for i in range(lax.axis_size(axis))])


def combine_kernel(count, ways, g_ref, *refs):
    ins, outs = refs[:count], refs[count:]
    rows = outs[0].shape[0]
    step = 128 if rows % 128 == 0 else rows
    for k in range(ways):
        base = (g_ref[0] ^ k) * rows
        for r in range(0, rows, step):
            at = pl.ds(pl.multiple_of(base + r, 16), step)
            total = ins[0][at, :].astype(F32)
            for one in ins[1:]:
                total = total + one[at, :].astype(F32)
            outs[k][r : r + step, :] = total.astype(outs[k].dtype)


def combine(arrays, group, ways):
    rows, cols = arrays[0].shape
    return call(
        functools.partial(combine_kernel, len(arrays), ways),
        "s" + "v" * len(arrays),
        [((rows // ways, cols), BF16)] * ways,
        vmem=20 << 20,
        nbytes=rows * cols,
    )(scalars(group), *arrays)


def assemble_kernel(ways, g_ref, *refs):
    out = refs[ways]
    rows = refs[0].shape[0]
    for k in range(ways):
        base = pl.multiple_of((g_ref[0] ^ k) * rows, 16)
        out[pl.ds(base, rows), :] = refs[k][...].astype(out.dtype)


def assemble(arrays, group, dtype=BF16):
    ways = len(arrays)
    rows, cols = arrays[0].shape
    return call(
        functools.partial(assemble_kernel, ways),
        "s" + "v" * ways,
        [((rows * ways, cols), dtype)],
        vmem=20 << 20,
        nbytes=rows * ways * cols,
    )(scalars(group), *arrays)[0]


def dims_of(name):
    size = lax.axis_size("dp")
    if name == "y":
        return [("dp", (1,))]
    rest = []
    m = 2
    while m < size:
        rest.append(m)
        m *= 2
    return [("dp", tuple(rest[i : i + 2])) for i in range(0, len(rest), 2)]


def reduce_rows(arrays, order):
    for name in order:
        for dim in dims_of(name):
            ways = 1 << len(dim[1])
            pieces = combine(arrays, bits_of(*dim), ways)
            arrays = [pieces[0]] + [xor_swap(pieces[k], dim, k) for k in range(1, ways)]
    return combine(arrays, 0, 1)[0]


def gather_rows(piece, order):
    for name in reversed(order):
        for dim in reversed(dims_of(name)):
            ways = 1 << len(dim[1])
            piece = assemble(
                [piece] + [xor_swap(piece, dim, k) for k in range(1, ways)], bits_of(*dim)
            )
    return piece


def per_device(
    lookback_readings,
    prediction_adjoint,
    variate_tallies,
    lookback_classes,
    brief_lift_table,
    moderate_lift_table,
    distant_lift_table,
    lift_offsets,
    part_entry_arrays,
    part_shrink_lines,
    part_layernorm_scale,
    part_layernorm_offset,
    mixing_offsets,
    expand_offsets,
    shrink_offsets,
    prediction_matrix,
    prediction_offset,
):
    place = lax.axis_index("pipe")
    core, far = place & 1, place // 2
    at = scalars(core, far)
    tok, adjoint = lookback_readings[0], prediction_adjoint[0]
    tables = (brief_lift_table, moderate_lift_table, distant_lift_table)
    entry, shrink = part_entry_arrays[0], part_shrink_lines[0]
    norm = jnp.concatenate([part_layernorm_scale, part_layernorm_offset], 0)

    weights = (entry, move(entry, CORES), shrink, move(shrink, CORES))
    norms = (norm, move(norm, CORES))
    toks = (tok, move(tok, TO_NEAR))
    adjoints = (move(adjoint, TO_FAR), adjoint)

    fragments, classes = row_layout(
        variate_tallies[:, 0], lookback_classes[:, 0], tok.shape[0]
    )
    segs, clss = [], []
    for r in range(2):
        fragment = lax.dynamic_index_in_dim(fragments, core + 2 * r, 0, False)
        segs.append((fragment.reshape(-1, 1), fragment.reshape(1, -1)))
        clss.append(lax.dynamic_index_in_dim(classes, core + 2 * r, 0, False).reshape(-1, 1))

    first = []
    arrived = []
    for r in range(2):
        out = first_layer(
            at, weights, toks[r], clss[r], tables, lift_offsets, mixing_offsets[0],
            expand_offsets[0:1], shrink_offsets[0:1], norms, segs[r],
        )
        first.append(out[1:])
        arrived.append(move(out[0], TO_FAR))
    second = []
    returned = []
    predictions = []
    for r in range(2):
        g, prediction, *rest = second_layer(
            at, weights, arrived[r], adjoints[r], prediction_matrix, prediction_offset[None],
            mixing_offsets[1], expand_offsets[1:2], shrink_offsets[1:2], norms, segs[r],
        )
        returned.append(move(g, TO_NEAR))
        predictions.append(prediction)
        second.append((arrived[r], *rest))
    shared_rows = max(768, 32 * lax.axis_size("dp"))
    keepf_far, sendf_far, keepa_far, senda_far, shared_far = second_weights(at, second, shared_rows)

    feed, att, series, shared = (), (), [], ()
    for r in range(2):
        x0, z0, qkv, o, lse, x1, z1, h, d = first[r]
        prior = (*feed, keepf_far, sendf_far) if r else ()
        g, *feed, vec = first_feed_back(at, weights, returned[r], x1, z1, h, d, norms, prior)
        if r:
            feed_got = move(feed[1], CORES)
        prior = (*att, shared[0], keepa_far, senda_far, shared_far) if r else ()
        series_row, *rest = first_attention_back(
            at, weights, g, x0, z0, qkv, o, lse, norms, segs[r], toks[r], clss[r], tables, vec,
            shared_rows, prior,
        )
        series.append(series_row)
        att, shared = rest[:2], rest[2:]

    prediction = jnp.where(far == 0, move(predictions[0], TO_NEAR), predictions[1])
    series_grad = jnp.where(far == 0, series[0], move(series[1], TO_FAR).astype(F32))

    feed_piece = gather_rows(reduce_rows([feed[0], feed_got], "yz"), "yz")
    att_piece = gather_rows(reduce_rows([att[0], move(att[1], CORES)], "zy"), "zy")
    shared_piece = reduce_rows([shared[0], move(shared[1], CORES)], "yz")
    shared_piece = assemble([shared_piece, lax.ppermute(shared_piece, "pipe", TO_FAR + TO_NEAR)], 0)
    shared_mine = gather_rows(shared_piece, "yz")
    shared_other = move(shared_mine, CORES)

    rows = entry.shape[0] * entry.shape[1] // shrink.shape[1] // 2
    up, down_grad = feed_piece[:rows], feed_piece[rows:].astype(F32)
    up_other = move(up, [(0, 1), (2, 3)])
    att_other = move(att_piece, [(1, 0), (3, 2)])
    entry_grad = entry_out(at, att_piece, att_other, up, up_other, entry.shape)
    t0, t1, t2, embb, gain, offset, attb, upb, downb, pw, pb = shared_out(
        core, far, lax.axis_size("dp"), shared_mine, shared_other, tables,
        prediction_matrix.shape[1], entry.shape[1],
    )
    return (
        prediction[None],
        series_grad[None],
        t0,
        t1,
        t2,
        embb,
        entry_grad[None],
        down_grad[None],
        gain,
        offset,
        attb,
        upb,
        downb,
        pw,
        pb[0],
    )


def solution(mesh):
    placed = (
        P("pipe", "dp", None),
        P("pipe", "dp", None),
        P(None, "dp", None),
        P(None, "dp", None),
        P(),
        P(),
        P(),
        P(),
        P("pipe", None, None),
        P("pipe", None, None),
        P("pipe", None),
        P("pipe", None),
        P(),
        P(),
        P(),
        P(),
        P(),
    )
    return jax.shard_map(
        per_device,
        mesh=mesh,
        in_specs=placed,
        out_specs=(
            P("pipe", "dp", None),
            P("pipe", "dp", None),
            P(),
            P(),
            P(),
            P(),
            P("pipe", None, None),
            P("pipe", None, None),
            P("pipe", None),
            P("pipe", None),
            P(),
            P(),
            P(),
            P(),
            P(),
        ),
        check_vma=False,
    )
```

```python
import functools

import jax
import jax.numpy as jnp
from jax import lax
from jax.experimental import pallas as pl
from jax.experimental.pallas import tpu as pltpu
from jax.sharding import PartitionSpec as P

HEADS = 8
HEAD_DIM = 64
F32 = jnp.float32
BF16 = jnp.bfloat16
VECTOR_ROW = 624
VECTORS = 16


def nn(a, b):
    return lax.dot_general(a, b, (((1,), (0,)), ((), ())), preferred_element_type=F32)


def nt(a, b):
    return lax.dot_general(a, b, (((1,), (1,)), ((), ())), preferred_element_type=F32)


def tn(a, b):
    return lax.dot_general(a, b, (((0,), (0,)), ((), ())), preferred_element_type=F32)


def column_sum(a):
    return jnp.sum(a.astype(F32), 0, keepdims=True)


def normalise(z):
    centre = z - jnp.mean(z, -1, keepdims=True)
    inverse = lax.rsqrt(jnp.mean(centre * centre, -1, keepdims=True) + 1e-05)
    return centre * inverse, inverse


def norm_back(upstream, z, gain):
    normed, inverse = normalise(z)
    gain_grad = jnp.sum(upstream * normed, 0, keepdims=True)
    offset_grad = jnp.sum(upstream, 0, keepdims=True)
    scaled = upstream * gain
    back = inverse * (
        scaled
        - jnp.mean(scaled, -1, keepdims=True)
        - normed * jnp.mean(scaled * normed, -1, keepdims=True)
    )
    return back, gain_grad, offset_grad


def gelu_both(u):
    bell = jnp.exp(u * u * -0.5)
    t = 1.0 / (1.0 + (0.3275911 * 0.5**0.5) * jnp.abs(u))
    poly = t * (
        0.127414796
        + t * (-0.142248368 + t * (0.7107068705 + t * (-0.7265760135 + t * 0.5307027145)))
    )
    half = poly * bell
    phi = jnp.where(u >= 0, 1.0 - half, half)
    return u * phi, phi + u * bell * 0.3989422804014327


def same_window_bias(seg_col, seg_row):
    return jnp.where(seg_col == seg_row, 0.0, -1e30).astype(F32)


class Choice:
    def __init__(self, index, sources, place, sem):
        self.index = index
        self.copies = [pltpu.make_async_copy(s, place, sem) for s in sources]

    def start(self):
        for k, copy in enumerate(self.copies):
            pl.when(self.index == k)(copy.start)

    def wait(self):
        for k, copy in enumerate(self.copies):
            pl.when(self.index == k)(copy.wait)


def weight_loads(core, entry, other, shrink, shrink_other, att_ref, up_ref, down_ref, sem):
    loads = []
    if att_ref is not None:
        loads.append(Choice(core, (entry, other), att_ref, sem.at[0]))
    if up_ref is not None:
        loads.append(Choice(1 - core, (entry, other), up_ref, sem.at[1]))
        half = down_ref.shape[0] // 2
        low, high = down_ref.at[pl.ds(0, half)], down_ref.at[pl.ds(half, half)]
        loads.append(Choice(core, (shrink, shrink_other), low, sem.at[2]))
        loads.append(Choice(1 - core, (shrink, shrink_other), high, sem.at[3]))
    for one in loads:
        one.start()
    return loads


def chosen_norms(core, own_ref, other_ref):
    own, other = own_ref[...], other_ref[...]
    first = core == 0
    return jnp.where(first, own, other), jnp.where(first, other, own)


class Moves:
    def __init__(self, sem):
        self.sem = sem
        self.started = []

    def start(self, source, target):
        copy = pltpu.make_async_copy(source, target, self.sem.at[len(self.started)])
        copy.start()
        self.started.append(copy)
        return copy


class Small:
    def __init__(self, pairs, sem):
        self.copies = [pltpu.make_async_copy(s, t, sem.at[i]) for i, (s, t) in enumerate(pairs)]

    def start(self):
        for copy in self.copies:
            copy.start()

    def wait(self):
        for copy in self.copies:
            copy.wait()


def row_windows(tallies, classes, micro, count):
    windows = 4
    ends, total = [], 0
    for w in range(windows - 1):
        total = total + tallies[micro, 0, w]
        ends.append(total)
    out = []
    for shape, axis in (((count, 1), 0), ((1, count), 1)):
        position = lax.broadcasted_iota(jnp.int32, shape, axis)
        window = sum((position >= end).astype(jnp.int32) for end in ends)
        group = jnp.full(shape, classes[micro, 0, 0], jnp.int32)
        for w in range(1, windows):
            group = jnp.where(window == w, classes[micro, 0, w], group)
        out.append((window, group))
    return out


def attention_core(x, w_ref, biases, norm, mask_ref, qkv_ref, o_ref, lse_ref, z_ref):
    width = x.shape[1]
    qkv_ref[:, :width] = ((nn(x, w_ref[:, :width]) + biases[0]) * HEAD_DIM**-0.5).astype(BF16)
    qkv_ref[:, width : 2 * width] = nn(x, w_ref[:, width : 2 * width]).astype(BF16)
    qkv_ref[:, 2 * width : 3 * width] = (
        nn(x, w_ref[:, 2 * width : 3 * width]) + biases[1]
    ).astype(BF16)
    pair = 2 * HEAD_DIM
    low = lax.broadcasted_iota(jnp.int32, (1, pair), 1) < HEAD_DIM
    for p in range(HEADS // 2):
        q2 = qkv_ref[:, p * pair : (p + 1) * pair]
        k2 = qkv_ref[:, width + p * pair : width + (p + 1) * pair]
        v2 = qkv_ref[:, 2 * width + p * pair : 2 * width + (p + 1) * pair]
        v2t = v2.T
        parts = []
        for h in range(2):
            kh = jnp.where(low if h == 0 else ~low, k2, jnp.zeros_like(k2))
            s = nt(kh, q2) + mask_ref[...]
            top = jnp.max(s, 0, keepdims=True)
            e = jnp.exp(s - top)
            total = jnp.sum(e, 0, keepdims=True)
            lse_ref[2 * p + h : 2 * p + h + 1, :] = top + jnp.log(total)
            ot = nn(v2t[h * HEAD_DIM : (h + 1) * HEAD_DIM, :], e.astype(BF16))
            parts.append(ot * (1.0 / total))
        o_ref[:, p * pair : (p + 1) * pair] = jnp.concatenate(parts, 0).T.astype(BF16)
    z = x.astype(F32) + (nn(o_ref[...], w_ref[:, 3 * width :]) + biases[2])
    z_ref[...] = z
    return (normalise(z)[0] * norm[0:1, :] + norm[1:2, :]).astype(BF16)


def feed_core(x, up_ref, down_ref, upb, downb, norm, h_ref, d_ref, z_ref, done=None, block=512):
    total = None
    for c in range(0, up_ref.shape[1], block):
        u = nn(x, up_ref[:, c : c + block]) + upb[:, c : c + block]
        h, d = gelu_both(u)
        hb = h.astype(BF16)
        h_ref[:, c : c + block] = hb
        d_ref[:, c : c + block] = d.astype(BF16)
        if done is not None:
            done(slice(c, c + block))
        part = nn(hb, down_ref[c : c + block, :])
        total = part if total is None else total + part
    z = x.astype(F32) + (total + downb)
    z_ref[...] = z
    return (normalise(z)[0] * norm[0:1, :] + norm[1:2, :]).astype(BF16)


def feed_back_chain(upstream, z_ref, d_ref, up_ref, down_ref, norm, gu_ref, gf_ref, vec_ref, gx_acc, done=None):
    back, gain_grad, offset_grad = norm_back(upstream, z_ref[...], norm[0:1, :])
    gf_ref[...] = back.astype(BF16)
    gx_acc[...] = back
    width = back.shape[1]
    for b in range(up_ref.shape[1] // width):
        cols = slice(b * width, (b + 1) * width)
        gu = (nt(gf_ref[...], down_ref[cols, :]) * d_ref[:, cols].astype(F32)).astype(BF16)
        gu_ref[:, cols] = gu
        if done is not None:
            done(cols)
        vec_ref[7 + b : 8 + b, :] = column_sum(gu)
        gx_acc[...] += nt(gu, up_ref[:, cols])
    vec_ref[11:12, :] = column_sum(gf_ref[...])
    vec_ref[14:15, :] = gain_grad
    vec_ref[15:16, :] = offset_grad


def attention_back_chain(
    upstream, z_ref, qkv_ref, o_ref, lse_ref, w_ref, norm, mask_ref,
    gqkv_ref, ga_ref, go_ref, vec_ref, gx_acc,
):
    back, gain_grad, offset_grad = norm_back(upstream, z_ref[...], norm[0:1, :])
    width = back.shape[1]
    ga_ref[...] = back.astype(BF16)
    gx_acc[...] = back
    vec_ref[6:7, :] = column_sum(ga_ref[...])
    vec_ref[12:13, :] = gain_grad
    vec_ref[13:14, :] = offset_grad
    go_ref[...] = nt(ga_ref[...], w_ref[:, 3 * width :]).astype(BF16)
    pair = 2 * HEAD_DIM
    low = lax.broadcasted_iota(jnp.int32, (1, pair), 1) < HEAD_DIM
    for p in range(HEADS // 2):
        q2 = qkv_ref[:, p * pair : (p + 1) * pair]
        k2 = qkv_ref[:, width + p * pair : width + (p + 1) * pair]
        v2 = qkv_ref[:, 2 * width + p * pair : 2 * width + (p + 1) * pair]
        go2 = go_ref[:, p * pair : (p + 1) * pair]
        o2 = o_ref[:, p * pair : (p + 1) * pair]
        k2t = k2.T
        prod = (go2.astype(F32) * o2.astype(F32)).T
        gq, gk, gv = [], None, None
        for h in range(2):
            own = low if h == 0 else ~low
            zero = jnp.zeros_like(k2)
            lanes = slice(h * HEAD_DIM, (h + 1) * HEAD_DIM)
            centred = jnp.sum(prod[lanes, :], 0, keepdims=True)
            s = nt(jnp.where(own, k2, zero), q2) + mask_ref[...]
            weights = jnp.exp(s - lse_ref[2 * p + h : 2 * p + h + 1, :])
            gp = nt(jnp.where(own, v2, zero), go2)
            gs = (weights * (gp - centred)).astype(BF16)
            gv_part = nn(weights.astype(BF16), jnp.where(own, go2, zero))
            gk_part = nn(gs, jnp.where(own, q2, zero))
            gv = gv_part if gv is None else gv + gv_part
            gk = gk_part if gk is None else gk + gk_part
            gq.append(nn(k2t[lanes, :], gs) * HEAD_DIM**-0.5)
        cols = slice(p * pair, (p + 1) * pair)
        gqkv_ref[:, cols] = jnp.concatenate(gq, 0).T.astype(BF16)
        gqkv_ref[:, width + p * pair : width + (p + 1) * pair] = gk.astype(BF16)
        gqkv_ref[:, 2 * width + p * pair : 2 * width + (p + 1) * pair] = gv.astype(BF16)
    gx_acc[...] += nt(gqkv_ref[...], w_ref[:, : 3 * width])
    vec_ref[4:5, :] = column_sum(gqkv_ref[:, :width])
    vec_ref[5:6, :] = column_sum(gqkv_ref[:, 2 * width :])


def shares(core, rows):
    mine = pl.ds(pl.multiple_of(core * rows, rows), rows)
    other = pl.ds(pl.multiple_of((1 - core) * rows, rows), rows)
    return mine, other


def feed_weight_grads(core, rows_of, prior, outs, xt_ref):
    width = rows_of[0][0].shape[1]
    half = width // 2
    blocks = rows_of[0][1].shape[1] // width
    for i, (x, _, _, _) in enumerate(rows_of):
        xt_ref[i] = x[...].T
    parts = shares(core, half)

    def put(index, at, value):
        if prior is not None:
            value = value + prior[index][at, :].astype(F32)
        outs[index][at, :] = value.astype(BF16)

    for j in range(blocks):
        b = lax.rem(j + core * (blocks // 2), blocks)
        cols = pl.ds(pl.multiple_of(b * width, width), width)
        at = (j % (blocks // 2)) * width
        value = sum(tn(h[:, cols], gf[...]) for _, h, _, gf in rows_of)
        put(2 + j // (blocks // 2), slice(at, at + width), value)
        at = pl.ds(pl.multiple_of(b * half, half), half)
        for index, part in enumerate(parts):
            put(index, at, sum(nn(xt_ref[i, part, :], gu[:, cols]) for i, (_, _, gu, _) in enumerate(rows_of)))


def attention_weight_grads(core, rows_of, prior, outs, xt_ref, ot_ref):
    width = rows_of[0][0].shape[1]
    half = width // 2
    parts = shares(core, half)

    def put(index, b, value):
        at = slice(b * half, (b + 1) * half)
        if prior is not None:
            value = value + prior[index][at, :].astype(F32)
        outs[index][at, :] = value.astype(BF16)

    for i, (_, _, o, _) in enumerate(rows_of):
        ot_ref[i] = o[...].T
    for index, part in enumerate(parts):
        put(index, 3, sum(nn(ot_ref[i, part, :], ga[...]) for i, (_, _, _, ga) in enumerate(rows_of)))
    for i, (x, _, _, _) in enumerate(rows_of):
        xt_ref[i] = x[...].T
    for b in range(3):
        for index, part in enumerate(parts):
            put(index, b, sum(
                nn(xt_ref[i, part, :], gqkv[:, b * width : (b + 1) * width])
                for i, (_, gqkv, _, _) in enumerate(rows_of)
            ))


def embed(tok, group_col, group_row, tables, off_ref):
    look = tok.shape[0]
    total = None
    for g, t_ref in enumerate(tables):
        skip = look - t_ref.shape[0]
        masked = jnp.where(group_row == g, tok[skip:, :], jnp.zeros((1, 1), BF16))
        part = tn(masked, t_ref[...]) + jnp.where(group_col == g, off_ref[g : g + 1, :], 0.0)
        total = part if total is None else total + part
    return total.astype(BF16)


def first_layer_kernel(
    row, small, at, tallies, classes, entry, other, shrink, shrink_other,
    tok_ref, t0_ref, t1_ref, t2_ref, off_ref, bias_ref, upb_ref, downb_ref, norm_ref, norm_other_ref,
    x2_ref, x0_out, z0_out, qkv_out, o_out, lse_out, x1_out, z1_out, h_out, d_out,
    x0_ref, z0_ref, qkv_ref, o_ref, lse_ref, x1_ref, z1_ref, h_ref, d_ref,
    mask_ref, att_ref, up_ref, down_ref, sem, out_sem,
):
    @pl.when(at[1] == 0)
    def _():
        core = at[0]
        small.start()
        loads = weight_loads(
            core, entry, other, shrink, shrink_other, att_ref, up_ref, down_ref, sem
        )
        out = Moves(out_sem)
        (wc, gc), (wr, gr) = row_windows(tallies, classes, core + 2 * row, x0_ref.shape[0])
        mask_ref[...] = same_window_bias(wc, wr)
        small.wait()
        x0_ref[...] = embed(tok_ref[...], gc, gr, (t0_ref, t1_ref, t2_ref), off_ref)
        out.start(x0_ref, x0_out)
        norm_att, norm_feed = chosen_norms(core, norm_ref, norm_other_ref)
        loads[0].wait()
        x1_ref[...] = attention_core(
            x0_ref[...], att_ref, [bias_ref[i, 0:1, :] for i in range(3)], norm_att, mask_ref,
            qkv_ref, o_ref, lse_ref, z0_ref,
        )
        for source, target in (
            (qkv_ref, qkv_out), (o_ref, o_out), (lse_ref, lse_out), (z0_ref, z0_out), (x1_ref, x1_out)
        ):
            out.start(source, target)
        for one in loads[1:]:
            one.wait()

        def done(cols):
            out.start(h_ref.at[:, cols], h_out.at[:, cols])
            out.start(d_ref.at[:, cols], d_out.at[:, cols])

        x2_ref[...] = feed_core(
            x1_ref[...], up_ref, down_ref, upb_ref[0:1, :], downb_ref[0:1, :], norm_feed,
            h_ref, d_ref, z1_ref, done,
        )
        out.start(z1_ref, z1_out)
        for copy in out.started:
            copy.wait()


def second_layer_kernel(
    row, small, at, tallies, classes, entry, other, shrink, shrink_other,
    x2_ref, adj_ref, pm_ref, pb_ref, bias_ref, upb_ref, downb_ref, norm_ref, norm_other_ref,
    g_ref, pred_ref, x2_out, gqkv_out, o_out, ga_out, x3_out, gu_out, h_out, gf_out, vec_out, gpm_out,
    gqkv_ref, o_ref, ga_ref, x3_ref, gu_ref, h_ref, gf_ref, vec_ref, gpm_ref,
    mask_ref, att_ref, up_ref, down_ref, qkv_ref, lse_ref, z2_ref, z3_ref, d_ref, gx_acc, go_ref,
    sem, out_sem,
):
    @pl.when(at[1] == 1)
    def _():
        core = at[0]
        small.start()
        loads = weight_loads(
            core, entry, other, shrink, shrink_other, att_ref, up_ref, down_ref, sem
        )
        out = Moves(out_sem)
        out.start(x2_ref, x2_out)
        (wc, _), (wr, _) = row_windows(tallies, classes, core + 2 * row, x2_ref.shape[0])
        mask_ref[...] = same_window_bias(wc, wr)
        small.wait()
        norm_att, norm_feed = chosen_norms(core, norm_ref, norm_other_ref)
        loads[0].wait()
        x3_ref[...] = attention_core(
            x2_ref[...], att_ref, [bias_ref[i, 1:2, :] for i in range(3)], norm_att, mask_ref,
            qkv_ref, o_ref, lse_ref, z2_ref,
        )
        out.start(o_ref, o_out)
        out.start(x3_ref, x3_out)
        for one in loads[1:]:
            one.wait()
        y = feed_core(
            x3_ref[...], up_ref, down_ref, upb_ref[1:2, :], downb_ref[1:2, :], norm_feed,
            h_ref, d_ref, z3_ref, lambda cols: out.start(h_ref.at[:, cols], h_out.at[:, cols]),
        )
        pm, adj = pm_ref[...], adj_ref[...]
        pred_ref[...] = (nt(pm, y) + pb_ref[...].T).astype(BF16)
        gpm_ref[...] = nn(adj, y)
        out.start(gpm_ref, gpm_out)
        width = y.shape[1]
        horizon = adj.shape[0]
        gpb = jnp.sum(adj.astype(F32), 1, keepdims=True).T
        vec_ref[0:1, :] = jnp.concatenate([gpb, jnp.zeros((1, width - horizon), F32)], 1)
        vec_ref[1:4, :] = jnp.zeros((3, width), F32)
        feed_back_chain(
            tn(adj, pm), z3_ref, d_ref, up_ref, down_ref, norm_feed, gu_ref, gf_ref, vec_ref, gx_acc,
            lambda cols: out.start(gu_ref.at[:, cols], gu_out.at[:, cols]),
        )
        out.start(gf_ref, gf_out)
        attention_back_chain(
            gx_acc[...].astype(BF16).astype(F32), z2_ref, qkv_ref, o_ref, lse_ref, att_ref, norm_att,
            mask_ref, gqkv_ref, ga_ref, go_ref, vec_ref, gx_acc,
        )
        g_ref[...] = gx_acc[...].astype(BF16)
        out.start(ga_ref, ga_out)
        out.start(gqkv_ref, gqkv_out)
        out.start(vec_ref, vec_out)
        for copy in out.started:
            copy.wait()


def second_weights_kernel(at, *refs):
    sources, refs = refs[:20], refs[20:]
    outs, refs = refs[:7], refs[7:]
    held, refs = refs[:20], refs[20:]
    made, (xt_ref, xt2_ref, ot_ref, sem, out_sem) = refs[:7], refs[7:]

    @pl.when(at[1] == 1)
    def _():
        core = at[0]
        loads = Moves(sem)
        for i in range(10):
            for r in range(2):
                loads.start(sources[10 * r + i], held[10 * r + i])
        out = Moves(out_sem)
        rows = held[:10], held[10:]
        for copy in loads.started[:8]:
            copy.wait()
        feed_weight_grads(core, [r[:4] for r in rows], None, made[:4], xt_ref)
        for i in range(4):
            out.start(made[i], outs[i])
        for copy in loads.started[8:]:
            copy.wait()
        attention_weight_grads(core, [r[4:8] for r in rows], None, made[4:6], xt2_ref, ot_ref)
        horizon = rows[0][9].shape[0]
        shared_ref = made[6]
        shared_ref[...] = jnp.zeros(shared_ref.shape, F32)
        shared_ref[:horizon, :] = rows[0][9][...] + rows[1][9][...]
        shared_ref[VECTOR_ROW : VECTOR_ROW + VECTORS, :] = rows[0][8][...] + rows[1][8][...]
        for i in range(4, 7):
            out.start(made[i], outs[i])
        for copy in out.started:
            copy.wait()


def first_feed_back_kernel(second, small, at, entry, other, shrink, shrink_other, *refs):
    z1_in, d_in, x1_in, h_in = refs[:4]
    refs = refs[4:]
    prior, far_in = (refs[:4], refs[4:8]) if second else (None, None)
    refs = refs[8:] if second else refs
    g_ref, norm_ref, norm_other_ref, gx_ref, vec_ref = refs[:5]
    outs, refs = refs[5:9], refs[9:]
    if second:
        held, refs = refs[:4], refs[4:]
    else:
        made, refs = refs[:4], refs[4:]
    z1_ref, d_ref, x1_ref, h_ref, up_ref, down_ref, gu_ref, gf_ref, gx_acc, xt_ref, sem, in_sem = refs

    @pl.when(at[1] == 0)
    def _():
        core = at[0]
        loads = Moves(in_sem)
        small.start()
        loads.start(z1_in, z1_ref)
        loads.start(d_in, d_ref)
        weights = weight_loads(core, entry, other, shrink, shrink_other, None, up_ref, down_ref, sem)
        loads.start(x1_in, x1_ref)
        loads.start(h_in, h_ref)
        if second:
            for source, target in zip(prior, held):
                loads.start(source, target)
        small.wait()
        _, norm_feed = chosen_norms(core, norm_ref, norm_other_ref)
        vec_ref[...] = jnp.zeros(vec_ref.shape, F32)
        for copy in loads.started[:2]:
            copy.wait()
        for one in weights:
            one.wait()
        feed_back_chain(
            g_ref[...].astype(F32), z1_ref, d_ref, up_ref, down_ref, norm_feed,
            gu_ref, gf_ref, vec_ref, gx_acc,
        )
        gx_ref[...] = gx_acc[...].astype(BF16)
        for copy in loads.started[2:]:
            copy.wait()
        feed_weight_grads(
            core, [(x1_ref, h_ref, gu_ref, gf_ref)], held if second else None,
            outs if second else made, xt_ref,
        )
        if not second:
            out = Moves(in_sem)
            for source, target in zip(made, outs):
                out.start(source, target)
            for copy in out.started:
                copy.wait()

    if second:
        @pl.when(at[1] == 1)
        def _():
            loads = Moves(in_sem)
            for source, target in zip(far_in, outs):
                loads.start(source, target)
            for copy in loads.started:
                copy.wait()


def first_attention_back_kernel(second, row, small, at, tallies, classes, entry, other, *refs):
    z0_in, o_in, qkv_in, lse_in, x0_in, tok_in = refs[:6]
    refs = refs[6:]
    prior, far_in = (refs[:3], refs[3:6]) if second else (None, None)
    refs = refs[6:] if second else refs
    g_ref, norm_ref, norm_other_ref, t0_ref, t1_ref, t2_ref, vec_in = refs[:7]
    refs = refs[8:]
    if second:
        (series_ref, keep_ref, send_ref, skeep_ref, ssend_ref), refs = refs[:5], refs[5:]
        held, refs = refs[:3], refs[3:]
        made = (keep_ref, send_ref)
    else:
        outs, refs = refs[:4], refs[4:]
        (series_ref, *made), refs = refs[:3], refs[3:]
    (z0_ref, o_ref, qkv_ref, lse_ref, x0_ref, tok_ref, mask_ref, att_ref, gqkv_ref, ga_ref, go_ref,
     gx_acc, xt_ref, ot_ref, vec_ref, acc_ref, sem, in_sem) = refs

    def split(total):
        half = skeep_ref.shape[0]
        mine, theirs = shares(at[0], half)
        total_ref = held[2]
        total_ref[...] = total
        skeep_ref[...] = total_ref[mine, :].astype(BF16)
        ssend_ref[...] = total_ref[theirs, :].astype(BF16)

    @pl.when(at[1] == 0)
    def _():
        core = at[0]
        loads = Moves(in_sem)
        small.start()
        loads.start(z0_in, z0_ref)
        weights = weight_loads(core, entry, other, None, None, att_ref, None, None, sem)
        loads.start(o_in, o_ref)
        loads.start(qkv_in, qkv_ref)
        loads.start(lse_in, lse_ref)
        loads.start(x0_in, x0_ref)
        loads.start(tok_in, tok_ref)
        if second:
            for source, target in zip(prior, held):
                loads.start(source, target)
        small.wait()
        norm_att, _ = chosen_norms(core, norm_ref, norm_other_ref)
        (wc, _), (wr, gr) = row_windows(tallies, classes, core + 2 * row, x0_ref.shape[0])
        mask_ref[...] = same_window_bias(wc, wr)
        vec_ref[...] = vec_in[...]
        weights[0].wait()
        for copy in loads.started:
            copy.wait()
        attention_back_chain(
            g_ref[...].astype(F32), z0_ref, qkv_ref, o_ref, lse_ref, att_ref, norm_att,
            mask_ref, gqkv_ref, ga_ref, go_ref, vec_ref, gx_acc,
        )
        attention_weight_grads(
            core, [(x0_ref, gqkv_ref, o_ref, ga_ref)], held[:2] if second else None,
            made, xt_ref, ot_ref,
        )
        g = gx_acc[...].astype(BF16)
        look = tok_ref.shape[0]
        at_row = 0
        for i, t_ref in enumerate((t0_ref, t1_ref, t2_ref)):
            skip = look - t_ref.shape[0]
            chosen = gr == i
            part = jnp.where(chosen, nt(t_ref[...], g), 0.0)
            if i == 0:
                gx_s = [part]
            else:
                gx_s.append(part)
            masked = jnp.where(chosen, tok_ref[skip:, :], jnp.zeros((1, 1), BF16))
            acc_ref[at_row : at_row + look - skip, :] = nn(masked, g)
            at_row += look - skip
        short, mid, long = gx_s
        a, b = long.shape[0] - short.shape[0], long.shape[0] - mid.shape[0]
        series_ref[:b, :] = long[:b, :].astype(series_ref.dtype)
        series_ref[b:a, :] = (long[b:a, :] + mid[: a - b, :]).astype(series_ref.dtype)
        series_ref[a:, :] = (long[a:, :] + mid[a - b :, :] + short).astype(series_ref.dtype)
        groups = lax.broadcasted_iota(jnp.int32, (8, gr.shape[1]), 0)
        vec_ref[1:4, :] = nn((groups == gr).astype(BF16), g)[0:3, :]
        acc_ref[VECTOR_ROW : VECTOR_ROW + VECTORS, :] = vec_ref[...]
        rest = VECTOR_ROW + VECTORS
        acc_ref[rest:, :] = jnp.zeros((acc_ref.shape[0] - rest, acc_ref.shape[1]), F32)
        if second:
            split(acc_ref[...] + held[2][...])
        else:
            out = Moves(in_sem)
            for source, target in zip((series_ref, *made, acc_ref), outs):
                out.start(source, target)
            for copy in out.started:
                copy.wait()

    if second:
        @pl.when(at[1] == 1)
        def _():
            loads = Moves(in_sem)
            for source, target in zip(far_in, (keep_ref, send_ref, acc_ref)):
                loads.start(source, target)
            for copy in loads.started:
                copy.wait()
            split(acc_ref[...])


def shared_out_kernel(
    at, mine_ref, other_ref,
    t0_ref, t1_ref, t2_ref, embb_ref, gain_ref, offset_ref, att_ref, up_ref, down_ref, pw_ref, pb_ref,
    all_ref,
):
    core, far = at[0], at[1]
    half = mine_ref.shape[0] // 2
    size = at.shape[0] - 2
    piece = half // size
    for who, source in ((core, mine_ref), (1 - core, other_ref)):
        for b in range(size):
            to = pl.ds(pl.multiple_of(who * half + b * piece, 16), piece)
            all_ref[far, to, :] = source[2 * b * piece : (2 * b + 1) * piece, :].astype(F32)
            all_ref[1 - far, to, :] = source[(2 * b + 1) * piece : (2 * b + 2) * piece, :].astype(F32)
    row = 0
    for out in (t0_ref, t1_ref, t2_ref):
        out[...] = all_ref[0, row : row + out.shape[0], :]
        row += out.shape[0]
    pw_ref[...] = all_ref[1, : pw_ref.shape[0], :]
    v = VECTOR_ROW
    width = all_ref.shape[2]
    pb_ref[...] = all_ref[1, v : v + 1, : pb_ref.shape[1]]
    embb_ref[...] = all_ref[0, v + 1 : v + 4, :]
    for l in range(2):
        for i in range(3):
            att_ref[i, l : l + 1, :] = all_ref[l, v + 4 + i : v + 5 + i, :]
        for b in range(4):
            up_ref[l : l + 1, b * width : (b + 1) * width] = all_ref[l, v + 7 + b : v + 8 + b, :]
        down_ref[l : l + 1, :] = all_ref[l, v + 11 : v + 12, :]
    gain_ref[...] = all_ref[far, pl.ds(v + 12 + 2 * core, 1), :]
    offset_ref[...] = all_ref[far, pl.ds(v + 13 + 2 * core, 1), :]


def entry_out_kernel(at, att_ref, att_other_ref, up_ref, up_other_ref, out_ref):
    rows = out_ref.shape[0] // 2
    width = att_ref.shape[1]

    def write(low, high):
        for b in range(out_ref.shape[1] // width):
            cols = slice(b * width, (b + 1) * width)
            out_ref[:rows, cols] = low[b * rows : (b + 1) * rows, :].astype(F32)
            out_ref[rows:, cols] = high[b * rows : (b + 1) * rows, :].astype(F32)

    pl.when(at[0] == 0)(lambda: write(att_ref, att_other_ref))
    pl.when(at[0] == 1)(lambda: write(up_other_ref, up_ref))


def series_out_kernel(at, near_ref, far_ref, out_ref):
    @pl.when(at[1] == 0)
    def _():
        out_ref[...] = near_ref[...]

    @pl.when(at[1] == 1)
    def _():
        out_ref[...] = far_ref[...].astype(F32)


def call(kernel, kinds, outs, scratch=(), out_kinds=None, vmem=60 << 20, flops=0, nbytes=0):
    spaces = {
        "s": pl.BlockSpec(memory_space=pltpu.SMEM),
        "a": pl.BlockSpec(memory_space=pltpu.HBM),
        "l": pl.BlockSpec(memory_space=pltpu.HBM),
        "v": pl.BlockSpec(memory_space=pltpu.VMEM),
    }

    def run(*args):
        assert len(args) == len(kinds)
        loaded = [i for i, k in enumerate(kinds) if k == "l"]

        def body(*refs):
            ins = list(refs[: len(kinds)])
            middle, held, sem = refs[len(kinds) : -1 - len(loaded)], refs[-1 - len(loaded) : -1], refs[-1]
            small = Small([(ins[i], place) for i, place in zip(loaded, held)], sem)
            for i, place in zip(loaded, held):
                ins[i] = place
            kernel(small, *ins, *middle)

        own = [pltpu.VMEM(args[i].shape, args[i].dtype) for i in loaded] + [sems(len(loaded))]
        return pl.pallas_call(
            body if loaded else kernel,
            out_shape=[jax.ShapeDtypeStruct(s, d) for s, d in outs],
            in_specs=[spaces[k] for k in kinds],
            out_specs=[spaces[k] for k in out_kinds or "v" * len(outs)],
            scratch_shapes=[s if not isinstance(s, tuple) else pltpu.VMEM(*s) for s in scratch]
            + (own if loaded else []),
            compiler_params=pltpu.CompilerParams(vmem_limit_bytes=vmem),
            cost_estimate=pl.CostEstimate(flops=flops, bytes_accessed=nbytes, transcendentals=0),
        )(*args)

    return run


def scalars(*values):
    return jnp.stack([jnp.asarray(v, jnp.int32) for v in values])


def sems(count):
    return pltpu.SemaphoreType.DMA((count,))


def first_layer(row, at, tallies, classes, weights, tok, tables, off, bias, upb, downb, norms):
    n, d, ff = tok.shape[1], off.shape[1], upb.shape[1]
    saves = [
        ((n, d), BF16), ((n, d), F32), ((n, 3 * d), BF16), ((n, d), BF16), ((HEADS, n), F32),
        ((n, d), BF16), ((n, d), F32), ((n, ff), BF16), ((n, ff), BF16),
    ]
    return call(
        functools.partial(first_layer_kernel, row),
        "sssaaaa" + "l" * 10,
        [((n, d), BF16)] + saves,
        saves
        + [((n, n), F32), ((d, ff), BF16), ((d, ff), BF16), ((ff, d), BF16), sems(4), sems(7 + 2 * ff // d)],
        "v" + "a" * 9,
        flops=10_000_000_000,
    )(at, tallies, classes, *weights, tok, *tables, off, bias, upb, downb, *norms)


def second_layer(row, at, tallies, classes, weights, x2, adj, pm, pb, bias, upb, downb, norms):
    n, d = x2.shape
    ff, out = upb.shape[1], pm.shape[0]
    saves = [
        ((n, 3 * d), BF16), ((n, d), BF16), ((n, d), BF16), ((n, d), BF16), ((n, ff), BF16),
        ((n, ff), BF16), ((n, d), BF16), ((VECTORS, d), F32), ((out, d), F32),
    ]
    g, pred, x2, gqkv, o, ga, x3, gu, h, gf, vec, gpm = call(
        functools.partial(second_layer_kernel, row),
        "sssaaaav" + "l" * 8,
        [((n, d), BF16), ((out, n), BF16), ((n, d), BF16)] + saves,
        saves
        + [
            ((n, n), F32), ((d, ff), BF16), ((d, ff), BF16), ((ff, d), BF16), ((n, 3 * d), BF16),
            ((HEADS, n), F32), ((n, d), F32), ((n, d), F32), ((n, ff), BF16), ((n, d), F32),
            ((n, d), BF16), sems(4), sems(8 + 2 * ff // d),
        ],
        "vv" + "a" * 10,
        flops=16_000_000_000,
    )(at, tallies, classes, *weights, x2, adj, pm, pb, bias, upb, downb, *norms)
    return g, pred, (x3, h, gu, gf, x2, gqkv, o, ga, vec, gpm)


def share_shapes(d, ff):
    return [((ff // d * (d // 2), d), BF16)] * 2 + [((ff // 2, d), BF16)] * 2, [((2 * d, d), BF16)] * 2


def second_weights(at, rows, shared_rows):
    n, d = rows[0][0].shape
    ff = rows[0][1].shape[1]
    feed, att = share_shapes(d, ff)
    outs = feed + att + [((shared_rows, d), F32)]
    return call(
        second_weights_kernel,
        "s" + "a" * 20,
        outs,
        [(a.shape, a.dtype) for a in (*rows[0], *rows[1])]
        + outs
        + [((2, d, n), BF16)] * 3
        + [sems(20), sems(7)],
        "a" * 7,
        flops=6_000_000_000,
    )(at, *rows[0], *rows[1])


def first_feed_back(at, weights, g, x1, z1, h, dd, norms, prior=()):
    n, d = x1.shape
    ff = h.shape[1]
    feed, _ = share_shapes(d, ff)
    second = bool(prior)
    return call(
        functools.partial(first_feed_back_kernel, second),
        "saaaa" + "a" * (4 + len(prior)) + "vll",
        [((n, d), BF16), ((VECTORS, d), F32)] + feed,
        feed
        + [
            ((n, d), F32), ((n, ff), BF16), ((n, d), BF16), ((n, ff), BF16),
            ((d, ff), BF16), ((ff, d), BF16), ((n, ff), BF16), ((n, d), BF16), ((n, d), F32),
            ((1, d, n), BF16), sems(4), sems(8),
        ],
        "vv" + ("v" if second else "a") * 4,
        flops=7_000_000_000,
    )(at, *weights, z1, dd, x1, h, *prior, g, *norms)


def first_attention_back(
    row, at, tallies, classes, weights, g, x0, z0, qkv, o, lse, norms, tok, tables, vec, after, shared_rows, prior=()
):
    n, d = x0.shape
    _, att = share_shapes(d, 4 * d)
    second = bool(prior)
    shared = [((shared_rows, d), F32)]
    if second:
        outs = [(tok.shape, BF16)] + att + [((shared_rows // 2, d), BF16)] * 2
        extra = att + shared
    else:
        outs = [(tok.shape, F32)] + att + shared
        extra = outs[:3]
    return call(
        functools.partial(first_attention_back_kernel, second, row),
        "sssaa" + "a" * (6 + len(prior)) + "vlllllva",
        outs,
        extra
        + [
            ((n, d), F32), ((n, d), BF16), ((n, 3 * d), BF16), ((HEADS, n), F32), ((n, d), BF16),
            (tok.shape, BF16),
            ((n, n), F32), ((d, 4 * d), BF16), ((n, 3 * d), BF16), ((n, d), BF16), ((n, d), BF16),
            ((n, d), F32), ((1, d, n), BF16), ((1, d, n), BF16), ((VECTORS, d), F32),
            ((shared_rows, d), F32), sems(4), sems(9),
        ],
        ("v" if second else "a") * len(outs),
        flops=9_000_000_000,
    )(at, tallies, classes, *weights[:2], z0, o, qkv, lse, x0, tok, *prior, g, *norms, *tables, vec, after)


def shared_out(core, far, size, mine, other, tables, horizon, ff):
    d = mine.shape[1]
    return call(
        shared_out_kernel,
        "svv",
        [(t.shape, F32) for t in tables]
        + [((3, d), F32), ((1, d), F32), ((1, d), F32), ((3, 2, d), F32), ((2, ff), F32), ((2, d), F32)]
        + [((horizon, d), F32), ((1, horizon), F32)],
        [((2, mine.shape[0], d), F32)],
        nbytes=4_000_000,
    )(scalars(core, far, *([0] * size)), mine, other)


def entry_out(at, att, att_other, up, up_other, shape):
    return call(entry_out_kernel, "svvvv", [(shape, F32)], nbytes=8_000_000)(
        at, att, att_other, up, up_other
    )[0]


def series_out(at, near, far):
    return call(series_out_kernel, "svv", [(near.shape, F32)], nbytes=2_000_000)(at, near, far)[0]


CORES = [(0, 1), (1, 0), (2, 3), (3, 2)]
TO_NEAR = [(2, 0), (3, 1)]
TO_FAR = [(0, 2), (1, 3)]
ORDER = "a AS b a A b S a A b S a A b S A S a b A S"


def move(array, pairs):
    return lax.ppermute(array, "pipe", pairs)


def bits_of(axis, mask):
    place = lax.axis_index(axis)
    index = 0
    for position, m in enumerate(mask):
        index = index + ((place & m) // m) * (1 << position)
    return index


def xor_swap(array, dim, k):
    axis, mask = dim
    flip = sum(m for position, m in enumerate(mask) if k >> position & 1)
    return lax.ppermute(array, axis, [(i, i ^ flip) for i in range(lax.axis_size(axis))])


def combine_kernel(count, ways, g_ref, _, *refs):
    ins, outs = refs[:count], refs[count:]
    rows = outs[0].shape[0]
    step = 128 if rows % 128 == 0 else rows
    for k in range(ways):
        base = (g_ref[0] ^ k) * rows
        for r in range(0, rows, step):
            at = pl.ds(pl.multiple_of(base + r, 16), step)
            total = ins[0][at, :].astype(F32)
            for one in ins[1:]:
                total = total + one[at, :].astype(F32)
            outs[k][r : r + step, :] = total.astype(outs[k].dtype)


def assemble_kernel(ways, g_ref, _, *refs):
    out = refs[ways]
    rows = refs[0].shape[0]
    for k in range(ways):
        base = pl.multiple_of((g_ref[0] ^ k) * rows, 16)
        out[pl.ds(base, rows), :] = refs[k][...].astype(out.dtype)


class Steps:
    def __init__(self):
        self.last = None

    def run(self, kernel, group, arrays, outs):
        after = arrays[0] if self.last is None else self.last
        made = call(
            kernel, "sa" + "v" * len(arrays), outs, vmem=16 << 20, nbytes=arrays[0].size
        )(scalars(group), after, *arrays)
        self.last = made[0]
        return made

    def combine(self, arrays, group, ways):
        rows, cols = arrays[0].shape
        kernel = functools.partial(combine_kernel, len(arrays), ways)
        return self.run(kernel, group, arrays, [((rows // ways, cols), BF16)] * ways)

    def assemble(self, arrays, group):
        ways = len(arrays)
        rows, cols = arrays[0].shape
        kernel = functools.partial(assemble_kernel, ways)
        return self.run(kernel, group, arrays, [((rows * ways, cols), BF16)])[0]


def dims_of(name):
    size = lax.axis_size("dp")
    if name == "y":
        return [("dp", (1,))]
    rest = []
    m = 2
    while m < size:
        rest.append(m)
        m *= 2
    return [("dp", tuple(rest[i : i + 2])) for i in range(0, len(rest), 2)]


def plane_sum(steps, arrays, order, shared=False):
    dims = [dim for name in order for dim in dims_of(name)]
    for dim in dims:
        ways = 1 << len(dim[1])
        pieces = steps.combine(arrays, bits_of(*dim), ways)
        arrays = [pieces[0]] + [xor_swap(pieces[k], dim, k) for k in range(1, ways)]
        yield
    piece = steps.combine(arrays, 0, 1)[0]
    if shared:
        other = move(piece, TO_FAR + TO_NEAR)
        yield
        piece = steps.assemble([piece, other], 0)
    for i, dim in enumerate(reversed(dims)):
        ways = 1 << len(dim[1])
        pieces = [piece] + [xor_swap(piece, dim, k) for k in range(1, ways)]
        yield
        piece = steps.assemble(pieces, bits_of(*dim))
    return piece


def interleave(chunks, order):
    results = {}

    def advance(name):
        try:
            next(chunks[name])
        except StopIteration as end:
            results[name] = end.value

    for name in order:
        if name in chunks and name not in results:
            advance(name)
    while len(results) < len(chunks):
        for name in chunks:
            if name not in results:
                advance(name)
    return results


def per_device(
    lookback_readings,
    prediction_adjoint,
    variate_tallies,
    lookback_classes,
    brief_lift_table,
    moderate_lift_table,
    distant_lift_table,
    lift_offsets,
    part_entry_arrays,
    part_shrink_lines,
    part_layernorm_scale,
    part_layernorm_offset,
    mixing_offsets,
    expand_offsets,
    shrink_offsets,
    prediction_matrix,
    prediction_offset,
):
    place = lax.axis_index("pipe")
    core, far = place & 1, place // 2
    at = scalars(core, far)
    entry, shrink = part_entry_arrays[0], part_shrink_lines[0]
    entry_other, shrink_other = move(entry, CORES), move(shrink, CORES)
    tok, adjoint = lookback_readings[0].T, prediction_adjoint[0].T
    tables = (brief_lift_table, moderate_lift_table, distant_lift_table)
    norm = jnp.concatenate([part_layernorm_scale, part_layernorm_offset], 0)

    weights = (entry, entry_other, shrink, shrink_other)
    norms = (norm, move(norm, CORES))
    toks = (tok, move(tok, TO_NEAR))
    adjoints = (move(adjoint, TO_FAR), adjoint)
    layout = (variate_tallies, lookback_classes)
    mixing = mixing_offsets.transpose(1, 0, 2)

    first = []
    arrived = []
    for r in range(2):
        out = first_layer(
            r, at, *layout, weights, toks[r], tables, lift_offsets, mixing, expand_offsets,
            shrink_offsets, norms,
        )
        first.append(out[1:])
        arrived.append(move(out[0], TO_FAR))
    second = []
    returned = []
    predictions = []
    for r in range(2):
        g, prediction, saved = second_layer(
            r, at, *layout, weights, arrived[r], adjoints[r], prediction_matrix.T,
            prediction_offset[None], mixing, expand_offsets, shrink_offsets, norms,
        )
        returned.append(move(g, TO_NEAR))
        predictions.append(prediction)
        second.append(saved)
    shared_rows = max(768, 32 * lax.axis_size("dp"))
    away = second_weights(at, second, shared_rows)

    steps = Steps()
    feed, att, series, shared = (), (), [], ()
    chunks = {}
    for r in range(2):
        x0, z0, qkv, o, lse, x1, z1, h, d = first[r]
        prior = (*feed, *away[:4]) if r else ()
        g, vec, *feed = first_feed_back(at, weights, returned[r], x1, z1, h, d, norms, prior)
        after = g
        if r:
            for name, i in (("a", 0), ("b", 2)):
                chunks[name] = plane_sum(steps, [feed[i], move(feed[i + 1], CORES)], "yz")
                next(chunks[name])
            after = steps.last
        prior = (*att, *shared, *away[4:]) if r else ()
        series_row, *rest = first_attention_back(
            r, at, *layout, weights, g, x0, z0, qkv, o, lse, norms, toks[r], tables, vec,
            after, shared_rows, prior,
        )
        series.append(series_row)
        att, shared = rest[:2], rest[2:]
    series_other = move(series[1], TO_FAR)
    chunks["A"] = plane_sum(steps, [att[0], move(att[1], CORES)], "yz")
    chunks["S"] = plane_sum(steps, [shared[0], move(shared[1], CORES)], "yz", True)
    prediction = jnp.where(far == 0, move(predictions[0], TO_NEAR), predictions[1])
    series_grad = series_out(at, series[0], series_other)

    sums = interleave(chunks, ORDER)
    up_other = move(sums["a"], [(0, 1), (2, 3)])
    shared_other = move(sums["S"], CORES)
    att_other = move(sums["A"], [(1, 0), (3, 2)])
    down_grad = sums["b"].astype(F32)
    t0, t1, t2, embb, gain, offset, attb, upb, downb, pw, pb = shared_out(
        core, far, lax.axis_size("dp"), sums["S"], shared_other, tables,
        prediction_matrix.shape[1], entry.shape[1],
    )
    entry_grad = entry_out(at, sums["A"], att_other, sums["a"], up_other, entry.shape)
    return (
        prediction.T[None],
        series_grad.T[None],
        t0,
        t1,
        t2,
        embb,
        entry_grad[None],
        down_grad[None],
        gain,
        offset,
        attb.transpose(1, 0, 2),
        upb,
        downb,
        pw.T,
        pb[0],
    )


def solution(mesh):
    placed = (
        P("pipe", "dp", None),
        P("pipe", "dp", None),
        P(None, "dp", None),
        P(None, "dp", None),
        P(),
        P(),
        P(),
        P(),
        P("pipe", None, None),
        P("pipe", None, None),
        P("pipe", None),
        P("pipe", None),
        P(),
        P(),
        P(),
        P(),
        P(),
    )
    return jax.shard_map(
        per_device,
        mesh=mesh,
        in_specs=placed,
        out_specs=(
            P("pipe", "dp", None),
            P("pipe", "dp", None),
            P(),
            P(),
            P(),
            P(),
            P("pipe", None, None),
            P("pipe", None, None),
            P("pipe", None),
            P("pipe", None),
            P(),
            P(),
            P(),
            P(),
            P(),
        ),
        check_vma=False,
    )
```

```python
import functools

import jax
import jax.numpy as jnp
from jax import lax
from jax.experimental import pallas as pl
from jax.experimental.pallas import tpu as pltpu
from jax.sharding import PartitionSpec as P

HEADS = 8
HEAD_DIM = 64
F32 = jnp.float32
BF16 = jnp.bfloat16
VECTOR_ROW = 624
VECTORS = 16


def nn(a, b):
    return lax.dot_general(a, b, (((1,), (0,)), ((), ())), preferred_element_type=F32)


def nt(a, b):
    return lax.dot_general(a, b, (((1,), (1,)), ((), ())), preferred_element_type=F32)


def tn(a, b):
    return lax.dot_general(a, b, (((0,), (0,)), ((), ())), preferred_element_type=F32)


def column_sum(a):
    return jnp.sum(a.astype(F32), 0, keepdims=True)


def normalise(z):
    centre = z - jnp.mean(z, -1, keepdims=True)
    inverse = lax.rsqrt(jnp.mean(centre * centre, -1, keepdims=True) + 1e-05)
    return centre * inverse, inverse


def norm_back(upstream, z, gain):
    normed, inverse = normalise(z)
    gain_grad = jnp.sum(upstream * normed, 0, keepdims=True)
    offset_grad = jnp.sum(upstream, 0, keepdims=True)
    scaled = upstream * gain
    back = inverse * (
        scaled
        - jnp.mean(scaled, -1, keepdims=True)
        - normed * jnp.mean(scaled * normed, -1, keepdims=True)
    )
    return back, gain_grad, offset_grad


def gelu_both(u):
    bell = jnp.exp(u * u * -0.5)
    t = 1.0 / (1.0 + (0.3275911 * 0.5**0.5) * jnp.abs(u))
    poly = t * (
        0.127414796
        + t * (-0.142248368 + t * (0.7107068705 + t * (-0.7265760135 + t * 0.5307027145)))
    )
    half = poly * bell
    phi = jnp.where(u >= 0, 1.0 - half, half)
    return u * phi, phi + u * bell * 0.3989422804014327


def same_window_bias(seg_col, seg_row):
    return jnp.where(seg_col == seg_row, 0.0, -1e30).astype(F32)


class Choice:
    def __init__(self, index, sources, place, sem):
        self.index = index
        self.copies = [pltpu.make_async_copy(s, place, sem) for s in sources]

    def start(self):
        for k, copy in enumerate(self.copies):
            pl.when(self.index == k)(copy.start)

    def wait(self):
        for k, copy in enumerate(self.copies):
            pl.when(self.index == k)(copy.wait)


def weight_loads(core, entry, other, shrink, shrink_other, att_ref, up_ref, down_ref, sem):
    loads = []
    if att_ref is not None:
        loads.append(Choice(core, (entry, other), att_ref, sem.at[0]))
    if up_ref is not None:
        loads.append(Choice(1 - core, (entry, other), up_ref, sem.at[1]))
        half = down_ref.shape[0] // 2
        low, high = down_ref.at[pl.ds(0, half)], down_ref.at[pl.ds(half, half)]
        loads.append(Choice(core, (shrink, shrink_other), low, sem.at[2]))
        loads.append(Choice(1 - core, (shrink, shrink_other), high, sem.at[3]))
    for one in loads:
        one.start()
    return loads


def chosen_norms(core, own_ref, other_ref):
    own, other = own_ref[...], other_ref[...]
    first = core == 0
    return jnp.where(first, own, other), jnp.where(first, other, own)


class Moves:
    def __init__(self, sem):
        self.sem = sem
        self.started = []

    def start(self, source, target):
        copy = pltpu.make_async_copy(source, target, self.sem.at[len(self.started)])
        copy.start()
        self.started.append(copy)
        return copy


class Small:
    def __init__(self, pairs, sem):
        self.copies = [pltpu.make_async_copy(s, t, sem.at[i]) for i, (s, t) in enumerate(pairs)]

    def start(self):
        for copy in self.copies:
            copy.start()

    def wait(self):
        for copy in self.copies:
            copy.wait()


def row_windows(tallies, classes, micro, count):
    windows = 4
    ends, total = [], 0
    for w in range(windows - 1):
        total = total + tallies[micro, 0, w]
        ends.append(total)
    out = []
    for shape, axis in (((count, 1), 0), ((1, count), 1)):
        position = lax.broadcasted_iota(jnp.int32, shape, axis)
        window = sum((position >= end).astype(jnp.int32) for end in ends)
        group = jnp.full(shape, classes[micro, 0, 0], jnp.int32)
        for w in range(1, windows):
            group = jnp.where(window == w, classes[micro, 0, w], group)
        out.append((window, group))
    return out


def attention_core(x, w_ref, biases, norm, mask_ref, qkv_ref, o_ref, lse_ref, z_ref):
    width = x.shape[1]
    qkv_ref[:, :width] = ((nn(x, w_ref[:, :width]) + biases[0]) * HEAD_DIM**-0.5).astype(BF16)
    qkv_ref[:, width : 2 * width] = nn(x, w_ref[:, width : 2 * width]).astype(BF16)
    qkv_ref[:, 2 * width : 3 * width] = (
        nn(x, w_ref[:, 2 * width : 3 * width]) + biases[1]
    ).astype(BF16)
    pair = 2 * HEAD_DIM
    low = lax.broadcasted_iota(jnp.int32, (1, pair), 1) < HEAD_DIM
    for p in range(HEADS // 2):
        q2 = qkv_ref[:, p * pair : (p + 1) * pair]
        k2 = qkv_ref[:, width + p * pair : width + (p + 1) * pair]
        v2 = qkv_ref[:, 2 * width + p * pair : 2 * width + (p + 1) * pair]
        v2t = v2.T
        parts = []
        for h in range(2):
            kh = jnp.where(low if h == 0 else ~low, k2, jnp.zeros_like(k2))
            s = nt(kh, q2) + mask_ref[...]
            top = jnp.max(s, 0, keepdims=True)
            e = jnp.exp(s - top)
            total = jnp.sum(e, 0, keepdims=True)
            lse_ref[2 * p + h : 2 * p + h + 1, :] = top + jnp.log(total)
            ot = nn(v2t[h * HEAD_DIM : (h + 1) * HEAD_DIM, :], e.astype(BF16))
            parts.append(ot * (1.0 / total))
        o_ref[:, p * pair : (p + 1) * pair] = jnp.concatenate(parts, 0).T.astype(BF16)
    z = x.astype(F32) + (nn(o_ref[...], w_ref[:, 3 * width :]) + biases[2])
    z_ref[...] = z
    return (normalise(z)[0] * norm[0:1, :] + norm[1:2, :]).astype(BF16)


def feed_core(x, up_ref, down_ref, upb, downb, norm, h_ref, d_ref, z_ref, done=None, block=512):
    total = None
    for c in range(0, up_ref.shape[1], block):
        u = nn(x, up_ref[:, c : c + block]) + upb[:, c : c + block]
        h, d = gelu_both(u)
        hb = h.astype(BF16)
        h_ref[:, c : c + block] = hb
        d_ref[:, c : c + block] = d.astype(BF16)
        if done is not None:
            done(slice(c, c + block))
        part = nn(hb, down_ref[c : c + block, :])
        total = part if total is None else total + part
    z = x.astype(F32) + (total + downb)
    z_ref[...] = z
    return (normalise(z)[0] * norm[0:1, :] + norm[1:2, :]).astype(BF16)


def feed_back_chain(upstream, z_ref, d_ref, up_ref, down_ref, norm, gu_ref, gf_ref, vec_ref, gx_acc, done=None):
    back, gain_grad, offset_grad = norm_back(upstream, z_ref[...], norm[0:1, :])
    gf_ref[...] = back.astype(BF16)
    gx_acc[...] = back
    width = back.shape[1]
    for b in range(up_ref.shape[1] // width):
        cols = slice(b * width, (b + 1) * width)
        gu = (nt(gf_ref[...], down_ref[cols, :]) * d_ref[:, cols].astype(F32)).astype(BF16)
        gu_ref[:, cols] = gu
        if done is not None:
            done(cols)
        vec_ref[7 + b : 8 + b, :] = column_sum(gu)
        gx_acc[...] += nt(gu, up_ref[:, cols])
    vec_ref[11:12, :] = column_sum(gf_ref[...])
    vec_ref[14:15, :] = gain_grad
    vec_ref[15:16, :] = offset_grad


def attention_back_chain(
    upstream, z_ref, qkv_ref, o_ref, lse_ref, w_ref, norm, mask_ref,
    gqkv_ref, ga_ref, go_ref, vec_ref, gx_acc,
):
    back, gain_grad, offset_grad = norm_back(upstream, z_ref[...], norm[0:1, :])
    width = back.shape[1]
    ga_ref[...] = back.astype(BF16)
    gx_acc[...] = back
    vec_ref[6:7, :] = column_sum(ga_ref[...])
    vec_ref[12:13, :] = gain_grad
    vec_ref[13:14, :] = offset_grad
    go_ref[...] = nt(ga_ref[...], w_ref[:, 3 * width :]).astype(BF16)
    pair = 2 * HEAD_DIM
    low = lax.broadcasted_iota(jnp.int32, (1, pair), 1) < HEAD_DIM
    for p in range(HEADS // 2):
        q2 = qkv_ref[:, p * pair : (p + 1) * pair]
        k2 = qkv_ref[:, width + p * pair : width + (p + 1) * pair]
        v2 = qkv_ref[:, 2 * width + p * pair : 2 * width + (p + 1) * pair]
        go2 = go_ref[:, p * pair : (p + 1) * pair]
        o2 = o_ref[:, p * pair : (p + 1) * pair]
        k2t = k2.T
        prod = (go2.astype(F32) * o2.astype(F32)).T
        gq, gk, gv = [], None, None
        for h in range(2):
            own = low if h == 0 else ~low
            zero = jnp.zeros_like(k2)
            lanes = slice(h * HEAD_DIM, (h + 1) * HEAD_DIM)
            centred = jnp.sum(prod[lanes, :], 0, keepdims=True)
            s = nt(jnp.where(own, k2, zero), q2) + mask_ref[...]
            weights = jnp.exp(s - lse_ref[2 * p + h : 2 * p + h + 1, :])
            gp = nt(jnp.where(own, v2, zero), go2)
            gs = (weights * (gp - centred)).astype(BF16)
            gv_part = nn(weights.astype(BF16), jnp.where(own, go2, zero))
            gk_part = nn(gs, jnp.where(own, q2, zero))
            gv = gv_part if gv is None else gv + gv_part
            gk = gk_part if gk is None else gk + gk_part
            gq.append(nn(k2t[lanes, :], gs) * HEAD_DIM**-0.5)
        cols = slice(p * pair, (p + 1) * pair)
        gqkv_ref[:, cols] = jnp.concatenate(gq, 0).T.astype(BF16)
        gqkv_ref[:, width + p * pair : width + (p + 1) * pair] = gk.astype(BF16)
        gqkv_ref[:, 2 * width + p * pair : 2 * width + (p + 1) * pair] = gv.astype(BF16)
    gx_acc[...] += nt(gqkv_ref[...], w_ref[:, : 3 * width])
    vec_ref[4:5, :] = column_sum(gqkv_ref[:, :width])
    vec_ref[5:6, :] = column_sum(gqkv_ref[:, 2 * width :])


def shares(core, rows):
    mine = pl.ds(pl.multiple_of(core * rows, rows), rows)
    other = pl.ds(pl.multiple_of((1 - core) * rows, rows), rows)
    return mine, other


def feed_weight_grads(core, rows_of, prior, outs, xt_ref):
    width = rows_of[0][0].shape[1]
    half = width // 2
    blocks = rows_of[0][1].shape[1] // width
    for i, (x, _, _, _) in enumerate(rows_of):
        xt_ref[i] = x[...].T
    parts = shares(core, half)

    def put(index, at, value):
        if prior is not None:
            value = value + prior[index][at, :].astype(F32)
        outs[index][at, :] = value.astype(BF16)

    for j in range(blocks):
        b = lax.rem(j + core * (blocks // 2), blocks)
        cols = pl.ds(pl.multiple_of(b * width, width), width)
        at = blocks * half + (j % (blocks // 2)) * width
        value = sum(tn(h[:, cols], gf[...]) for _, h, _, gf in rows_of)
        put(j // (blocks // 2), slice(at, at + width), value)
        at = pl.ds(pl.multiple_of(b * half, half), half)
        for index, part in enumerate(parts):
            put(index, at, sum(nn(xt_ref[i, part, :], gu[:, cols]) for i, (_, _, gu, _) in enumerate(rows_of)))


def store_mixed(out, row, value, block, gap):
    for k in range(0, value.shape[0], block):
        at = (row + k) // block * (block + gap)
        out[at : at + block, :] = value[k : k + block, :]


def attention_weight_grads(core, rows_of, prior, outs, xt_ref, ot_ref, block=None, gap=0):
    width = rows_of[0][0].shape[1]
    half = width // 2
    parts = shares(core, half)

    def put(index, b, value):
        at = slice(b * half, (b + 1) * half)
        if prior is not None:
            value = value + prior[index][at, :].astype(F32)
        store_mixed(outs[index], b * half, value.astype(BF16), block or half, gap)

    for i, (_, _, o, _) in enumerate(rows_of):
        ot_ref[i] = o[...].T
    for index, part in enumerate(parts):
        put(index, 3, sum(nn(ot_ref[i, part, :], ga[...]) for i, (_, _, _, ga) in enumerate(rows_of)))
    for i, (x, _, _, _) in enumerate(rows_of):
        xt_ref[i] = x[...].T
    for b in range(3):
        for index, part in enumerate(parts):
            put(index, b, sum(
                nn(xt_ref[i, part, :], gqkv[:, b * width : (b + 1) * width])
                for i, (_, gqkv, _, _) in enumerate(rows_of)
            ))


def embed(tok, group_col, group_row, tables, off_ref):
    look = tok.shape[0]
    total = None
    for g, t_ref in enumerate(tables):
        skip = look - t_ref.shape[0]
        masked = jnp.where(group_row == g, tok[skip:, :], jnp.zeros((1, 1), BF16))
        part = tn(masked, t_ref[...]) + jnp.where(group_col == g, off_ref[g : g + 1, :], 0.0)
        total = part if total is None else total + part
    return total.astype(BF16)


def first_layer_kernel(
    small, at, tallies, classes, entry, other, shrink, shrink_other,
    tok_ref, t0_ref, t1_ref, t2_ref, off_ref, bias_ref, upb_ref, downb_ref, norm_ref, norm_other_ref,
    x2_ref, x0_out, z0_out, qkv_out, o_out, lse_out, x1_out, z1_out, h_out, d_out,
    x0_ref, z0_ref, qkv_ref, o_ref, lse_ref, x1_ref, z1_ref, h_ref, d_ref,
    mask_ref, att_ref, up_ref, down_ref, sem, out_sem,
):
    @pl.when(at[1] == 0)
    def _():
        core = at[0]
        small.start()
        loads = weight_loads(
            core, entry, other, shrink, shrink_other, att_ref, up_ref, down_ref, sem
        )
        out = Moves(out_sem)
        (wc, gc), (wr, gr) = row_windows(tallies, classes, core + 2 * at[2], x0_ref.shape[0])
        mask_ref[...] = same_window_bias(wc, wr)
        small.wait()
        x0_ref[...] = embed(tok_ref[...], gc, gr, (t0_ref, t1_ref, t2_ref), off_ref)
        out.start(x0_ref, x0_out)
        norm_att, norm_feed = chosen_norms(core, norm_ref, norm_other_ref)
        loads[0].wait()
        x1_ref[...] = attention_core(
            x0_ref[...], att_ref, [bias_ref[i, 0:1, :] for i in range(3)], norm_att, mask_ref,
            qkv_ref, o_ref, lse_ref, z0_ref,
        )
        for source, target in (
            (qkv_ref, qkv_out), (o_ref, o_out), (lse_ref, lse_out), (z0_ref, z0_out), (x1_ref, x1_out)
        ):
            out.start(source, target)
        for one in loads[1:]:
            one.wait()

        def done(cols):
            out.start(h_ref.at[:, cols], h_out.at[:, cols])
            out.start(d_ref.at[:, cols], d_out.at[:, cols])

        x2_ref[...] = feed_core(
            x1_ref[...], up_ref, down_ref, upb_ref[0:1, :], downb_ref[0:1, :], norm_feed,
            h_ref, d_ref, z1_ref, done,
        )
        out.start(z1_ref, z1_out)
        for copy in out.started:
            copy.wait()


def second_layer_kernel(
    small, at, tallies, classes, entry, other, shrink, shrink_other,
    x2_ref, adj_ref, pm_ref, pb_ref, bias_ref, upb_ref, downb_ref, norm_ref, norm_other_ref,
    g_ref, pred_ref, x2_out, gqkv_out, o_out, ga_out, x3_out, gu_out, h_out, gf_out, vec_out, gpm_out,
    gqkv_ref, o_ref, ga_ref, x3_ref, gu_ref, h_ref, gf_ref, vec_ref, gpm_ref,
    mask_ref, att_ref, up_ref, down_ref, qkv_ref, lse_ref, z2_ref, z3_ref, d_ref, gx_acc, go_ref,
    sem, out_sem,
):
    @pl.when(at[1] == 1)
    def _():
        core = at[0]
        small.start()
        loads = weight_loads(
            core, entry, other, shrink, shrink_other, att_ref, up_ref, down_ref, sem
        )
        out = Moves(out_sem)
        out.start(x2_ref, x2_out)
        (wc, _), (wr, _) = row_windows(tallies, classes, core + 2 * at[2], x2_ref.shape[0])
        mask_ref[...] = same_window_bias(wc, wr)
        small.wait()
        norm_att, norm_feed = chosen_norms(core, norm_ref, norm_other_ref)
        loads[0].wait()
        x3_ref[...] = attention_core(
            x2_ref[...], att_ref, [bias_ref[i, 1:2, :] for i in range(3)], norm_att, mask_ref,
            qkv_ref, o_ref, lse_ref, z2_ref,
        )
        out.start(o_ref, o_out)
        out.start(x3_ref, x3_out)
        for one in loads[1:]:
            one.wait()
        y = feed_core(
            x3_ref[...], up_ref, down_ref, upb_ref[1:2, :], downb_ref[1:2, :], norm_feed,
            h_ref, d_ref, z3_ref, lambda cols: out.start(h_ref.at[:, cols], h_out.at[:, cols]),
        )
        pm, adj = pm_ref[...], adj_ref[...]
        pred_ref[...] = (nt(pm, y) + pb_ref[...].T).astype(BF16)
        gpm_ref[...] = nn(adj, y)
        out.start(gpm_ref, gpm_out)
        width = y.shape[1]
        horizon = adj.shape[0]
        gpb = jnp.sum(adj.astype(F32), 1, keepdims=True).T
        vec_ref[0:1, :] = jnp.concatenate([gpb, jnp.zeros((1, width - horizon), F32)], 1)
        vec_ref[1:4, :] = jnp.zeros((3, width), F32)
        feed_back_chain(
            tn(adj, pm), z3_ref, d_ref, up_ref, down_ref, norm_feed, gu_ref, gf_ref, vec_ref, gx_acc,
            lambda cols: out.start(gu_ref.at[:, cols], gu_out.at[:, cols]),
        )
        out.start(gf_ref, gf_out)
        attention_back_chain(
            gx_acc[...].astype(BF16).astype(F32), z2_ref, qkv_ref, o_ref, lse_ref, att_ref, norm_att,
            mask_ref, gqkv_ref, ga_ref, go_ref, vec_ref, gx_acc,
        )
        g_ref[...] = gx_acc[...].astype(BF16)
        out.start(ga_ref, ga_out)
        out.start(gqkv_ref, gqkv_out)
        out.start(vec_ref, vec_out)
        for copy in out.started:
            copy.wait()


def second_weights_kernel(at, *refs):
    sources, refs = refs[:20], refs[20:]
    outs, refs = refs[:5], refs[5:]
    held, refs = refs[:20], refs[20:]
    made, (xt_ref, xt2_ref, ot_ref, sem, out_sem) = refs[:5], refs[5:]

    @pl.when(at[1] == 1)
    def _():
        core = at[0]
        loads = Moves(sem)
        for i in range(10):
            for r in range(2):
                loads.start(sources[10 * r + i], held[10 * r + i])
        out = Moves(out_sem)
        rows = held[:10], held[10:]
        for copy in loads.started[:8]:
            copy.wait()
        feed_weight_grads(core, [r[:4] for r in rows], None, made[:2], xt_ref)
        for i in range(2):
            out.start(made[i], outs[i])
        for copy in loads.started[8:]:
            copy.wait()
        attention_weight_grads(core, [r[4:8] for r in rows], None, made[2:4], xt2_ref, ot_ref)
        horizon = rows[0][9].shape[0]
        shared_ref = made[4]
        shared_ref[...] = jnp.zeros(shared_ref.shape, F32)
        shared_ref[:horizon, :] = rows[0][9][...] + rows[1][9][...]
        shared_ref[VECTOR_ROW : VECTOR_ROW + VECTORS, :] = rows[0][8][...] + rows[1][8][...]
        for i in range(2, 5):
            out.start(made[i], outs[i])
        for copy in out.started:
            copy.wait()


def first_feed_back_kernel(second, small, at, entry, other, shrink, shrink_other, *refs):
    z1_in, d_in, x1_in, h_in = refs[:4]
    refs = refs[4:]
    prior, far_in = (refs[:2], refs[2:4]) if second else (None, None)
    refs = refs[4:] if second else refs
    g_ref, norm_ref, norm_other_ref, _, gx_ref, vec_ref = refs[:6]
    outs, refs = refs[6:8], refs[8:]
    if second:
        held, refs = refs[:2], refs[2:]
    else:
        made, refs = refs[:2], refs[2:]
    z1_ref, d_ref, x1_ref, h_ref, up_ref, down_ref, gu_ref, gf_ref, gx_acc, xt_ref, sem, in_sem = refs

    @pl.when(at[1] == 0)
    def _():
        core = at[0]
        loads = Moves(in_sem)
        small.start()
        loads.start(z1_in, z1_ref)
        loads.start(d_in, d_ref)
        weights = weight_loads(core, entry, other, shrink, shrink_other, None, up_ref, down_ref, sem)
        loads.start(x1_in, x1_ref)
        loads.start(h_in, h_ref)
        if second:
            for source, target in zip(prior, held):
                loads.start(source, target)
        small.wait()
        _, norm_feed = chosen_norms(core, norm_ref, norm_other_ref)
        vec_ref[...] = jnp.zeros(vec_ref.shape, F32)
        for copy in loads.started[:2]:
            copy.wait()
        for one in weights:
            one.wait()
        feed_back_chain(
            g_ref[...].astype(F32), z1_ref, d_ref, up_ref, down_ref, norm_feed,
            gu_ref, gf_ref, vec_ref, gx_acc,
        )
        gx_ref[...] = gx_acc[...].astype(BF16)
        for copy in loads.started[2:]:
            copy.wait()
        feed_weight_grads(
            core, [(x1_ref, h_ref, gu_ref, gf_ref)], held if second else None,
            outs if second else made, xt_ref,
        )
        if not second:
            out = Moves(in_sem)
            for source, target in zip(made, outs):
                out.start(source, target)
            for copy in out.started:
                copy.wait()

    if second:
        @pl.when(at[1] == 1)
        def _():
            loads = Moves(in_sem)
            for source, target in zip(far_in, outs):
                loads.start(source, target)
            for copy in loads.started:
                copy.wait()


def first_attention_back_kernel(second, size, small, at, tallies, classes, entry, other, *refs):
    z0_in, o_in, qkv_in, lse_in, x0_in, tok_in = refs[:6]
    refs = refs[6:]
    prior, far_in = (refs[:3], refs[3:6]) if second else (None, None)
    refs = refs[6:] if second else refs
    g_ref, norm_ref, norm_other_ref, t0_ref, t1_ref, t2_ref, vec_in = refs[:7]
    refs = refs[8:]
    if second:
        (series_ref, keep_ref, send_ref), refs = refs[:3], refs[3:]
        held, refs = refs[:3], refs[3:]
        made = (keep_ref, send_ref)
    else:
        outs, refs = refs[:4], refs[4:]
        (series_ref, *made), refs = refs[:3], refs[3:]
    (z0_ref, o_ref, qkv_ref, lse_ref, x0_ref, tok_ref, mask_ref, att_ref, gqkv_ref, ga_ref, go_ref,
     gx_acc, xt_ref, ot_ref, vec_ref, acc_ref, sem, in_sem) = refs

    if second:
        half = acc_ref.shape[0] // 2
        gap = half // size
        block = keep_ref.shape[0] // size - gap
    else:
        block, gap = None, 0

    def split(total):
        total_ref = held[2]
        total_ref[...] = total
        for index, out in enumerate((keep_ref, send_ref)):
            first = (at[0] if index == 0 else 1 - at[0]) * half
            for p in range(size):
                rows = pl.ds(pl.multiple_of(first + p * gap, 16), gap)
                to = p * (block + gap) + block
                out[to : to + gap, :] = total_ref[rows, :].astype(BF16)

    @pl.when(at[1] == 0)
    def _():
        core = at[0]
        loads = Moves(in_sem)
        small.start()
        loads.start(z0_in, z0_ref)
        weights = weight_loads(core, entry, other, None, None, att_ref, None, None, sem)
        loads.start(o_in, o_ref)
        loads.start(qkv_in, qkv_ref)
        loads.start(lse_in, lse_ref)
        loads.start(x0_in, x0_ref)
        loads.start(tok_in, tok_ref)
        if second:
            for source, target in zip(prior, held):
                loads.start(source, target)
        small.wait()
        norm_att, _ = chosen_norms(core, norm_ref, norm_other_ref)
        (wc, _), (wr, gr) = row_windows(tallies, classes, core + 2 * at[2], x0_ref.shape[0])
        mask_ref[...] = same_window_bias(wc, wr)
        vec_ref[...] = vec_in[...]
        weights[0].wait()
        for copy in loads.started:
            copy.wait()
        attention_back_chain(
            g_ref[...].astype(F32), z0_ref, qkv_ref, o_ref, lse_ref, att_ref, norm_att,
            mask_ref, gqkv_ref, ga_ref, go_ref, vec_ref, gx_acc,
        )
        attention_weight_grads(
            core, [(x0_ref, gqkv_ref, o_ref, ga_ref)], held[:2] if second else None,
            made, xt_ref, ot_ref, block, gap,
        )
        g = gx_acc[...].astype(BF16)
        look = tok_ref.shape[0]
        at_row = 0
        for i, t_ref in enumerate((t0_ref, t1_ref, t2_ref)):
            skip = look - t_ref.shape[0]
            chosen = gr == i
            part = jnp.where(chosen, nt(t_ref[...], g), 0.0)
            if i == 0:
                gx_s = [part]
            else:
                gx_s.append(part)
            masked = jnp.where(chosen, tok_ref[skip:, :], jnp.zeros((1, 1), BF16))
            acc_ref[at_row : at_row + look - skip, :] = nn(masked, g)
            at_row += look - skip
        short, mid, long = gx_s
        a, b = long.shape[0] - short.shape[0], long.shape[0] - mid.shape[0]
        series_ref[:b, :] = long[:b, :].astype(series_ref.dtype)
        series_ref[b:a, :] = (long[b:a, :] + mid[: a - b, :]).astype(series_ref.dtype)
        series_ref[a:, :] = (long[a:, :] + mid[a - b :, :] + short).astype(series_ref.dtype)
        groups = lax.broadcasted_iota(jnp.int32, (8, gr.shape[1]), 0)
        vec_ref[1:4, :] = nn((groups == gr).astype(BF16), g)[0:3, :]
        acc_ref[VECTOR_ROW : VECTOR_ROW + VECTORS, :] = vec_ref[...]
        rest = VECTOR_ROW + VECTORS
        acc_ref[rest:, :] = jnp.zeros((acc_ref.shape[0] - rest, acc_ref.shape[1]), F32)
        if second:
            split(acc_ref[...] + held[2][...])
        else:
            out = Moves(in_sem)
            for source, target in zip((series_ref, *made, acc_ref), outs):
                out.start(source, target)
            for copy in out.started:
                copy.wait()

    if second:
        @pl.when(at[1] == 1)
        def _():
            loads = Moves(in_sem)
            for source, target in zip(far_in, (held[0], held[1], acc_ref)):
                loads.start(source, target)
            for copy in loads.started:
                copy.wait()
            for source, target in zip(held, (keep_ref, send_ref)):
                store_mixed(target, 0, source[...], block, gap)
            split(acc_ref[...])


def shared_out_kernel(
    at, _, mine_ref, other_ref, mine_away_ref, other_away_ref,
    t0_ref, t1_ref, t2_ref, embb_ref, gain_ref, offset_ref, att_ref, up_ref, down_ref, pw_ref, pb_ref,
    all_ref,
):
    core, far = at[0], at[1]
    half = mine_ref.shape[0]
    for plane, pair in ((far, (mine_ref, other_ref)), (1 - far, (mine_away_ref, other_away_ref))):
        for who, source in ((core, pair[0]), (1 - core, pair[1])):
            all_ref[plane, pl.ds(pl.multiple_of(who * half, 16), half), :] = source[...].astype(F32)
    row = 0
    for out in (t0_ref, t1_ref, t2_ref):
        out[...] = all_ref[0, row : row + out.shape[0], :]
        row += out.shape[0]
    pw_ref[...] = all_ref[1, : pw_ref.shape[0], :]
    v = VECTOR_ROW
    width = all_ref.shape[2]
    pb_ref[...] = all_ref[1, v : v + 1, : pb_ref.shape[1]]
    embb_ref[...] = all_ref[0, v + 1 : v + 4, :]
    for l in range(2):
        for i in range(3):
            att_ref[i, l : l + 1, :] = all_ref[l, v + 4 + i : v + 5 + i, :]
        for b in range(4):
            up_ref[l : l + 1, b * width : (b + 1) * width] = all_ref[l, v + 7 + b : v + 8 + b, :]
        down_ref[l : l + 1, :] = all_ref[l, v + 11 : v + 12, :]
    gain_ref[...] = all_ref[far, pl.ds(v + 12 + 2 * core, 1), :]
    offset_ref[...] = all_ref[far, pl.ds(v + 13 + 2 * core, 1), :]


def entry_out_kernel(at, _, att_ref, att_other_ref, up_ref, up_other_ref, out_ref):
    rows = out_ref.shape[0] // 2
    width = att_ref.shape[1]

    def write(low, high):
        for b in range(out_ref.shape[1] // width):
            cols = slice(b * width, (b + 1) * width)
            out_ref[:rows, cols] = low[b * rows : (b + 1) * rows, :].astype(F32)
            out_ref[rows:, cols] = high[b * rows : (b + 1) * rows, :].astype(F32)

    pl.when(at[0] == 0)(lambda: write(att_ref, att_other_ref))
    pl.when(at[0] == 1)(lambda: write(up_other_ref, up_ref))


def series_out_kernel(at, _, near_ref, far_ref, down_ref, pred_near_ref, pred_far_ref, out_ref, down_out, pred_out):
    down_out[...] = down_ref[...].astype(F32)

    @pl.when(at[1] == 0)
    def _():
        out_ref[...] = near_ref[...]
        pred_out[...] = pred_near_ref[...]

    @pl.when(at[1] == 1)
    def _():
        out_ref[...] = far_ref[...].astype(F32)
        pred_out[...] = pred_far_ref[...]


def call(kernel, kinds, outs, scratch=(), out_kinds=None, vmem=60 << 20, flops=0, nbytes=0):
    spaces = {
        "s": pl.BlockSpec(memory_space=pltpu.SMEM),
        "a": pl.BlockSpec(memory_space=pltpu.HBM),
        "l": pl.BlockSpec(memory_space=pltpu.HBM),
        "v": pl.BlockSpec(memory_space=pltpu.VMEM),
    }

    def run(*args):
        assert len(args) == len(kinds)
        loaded = [i for i, k in enumerate(kinds) if k == "l"]

        def body(*refs):
            ins = list(refs[: len(kinds)])
            middle, held, sem = refs[len(kinds) : -1 - len(loaded)], refs[-1 - len(loaded) : -1], refs[-1]
            small = Small([(ins[i], place) for i, place in zip(loaded, held)], sem)
            for i, place in zip(loaded, held):
                ins[i] = place
            kernel(small, *ins, *middle)

        own = [pltpu.VMEM(args[i].shape, args[i].dtype) for i in loaded] + [sems(len(loaded))]
        return pl.pallas_call(
            body if loaded else kernel,
            out_shape=[jax.ShapeDtypeStruct(s, d) for s, d in outs],
            in_specs=[spaces[k] for k in kinds],
            out_specs=[spaces[k] for k in out_kinds or "v" * len(outs)],
            scratch_shapes=[s if not isinstance(s, tuple) else pltpu.VMEM(*s) for s in scratch]
            + (own if loaded else []),
            compiler_params=pltpu.CompilerParams(vmem_limit_bytes=vmem),
            cost_estimate=pl.CostEstimate(flops=flops, bytes_accessed=nbytes, transcendentals=0),
        )(*args)

    return run


def scalars(*values):
    return jnp.stack([jnp.asarray(v, jnp.int32) for v in values])


def sems(count):
    return pltpu.SemaphoreType.DMA((count,))


def first_layer(at, tallies, classes, weights, tok, tables, off, bias, upb, downb, norms):
    n, d, ff = tok.shape[1], off.shape[1], upb.shape[1]
    saves = [
        ((n, d), BF16), ((n, d), F32), ((n, 3 * d), BF16), ((n, d), BF16), ((HEADS, n), F32),
        ((n, d), BF16), ((n, d), F32), ((n, ff), BF16), ((n, ff), BF16),
    ]
    return call(
        first_layer_kernel,
        "sssaaaa" + "l" * 10,
        [((n, d), BF16)] + saves,
        saves
        + [((n, n), F32), ((d, ff), BF16), ((d, ff), BF16), ((ff, d), BF16), sems(4), sems(7 + 2 * ff // d)],
        "v" + "a" * 9,
        flops=10_000_000_000,
    )(at, tallies, classes, *weights, tok, *tables, off, bias, upb, downb, *norms)


def second_layer(at, tallies, classes, weights, x2, adj, pm, pb, bias, upb, downb, norms):
    n, d = x2.shape
    ff, out = upb.shape[1], pm.shape[0]
    saves = [
        ((n, 3 * d), BF16), ((n, d), BF16), ((n, d), BF16), ((n, d), BF16), ((n, ff), BF16),
        ((n, ff), BF16), ((n, d), BF16), ((VECTORS, d), F32), ((out, d), F32),
    ]
    g, pred, x2, gqkv, o, ga, x3, gu, h, gf, vec, gpm = call(
        second_layer_kernel,
        "sssaaaav" + "l" * 8,
        [((n, d), BF16), ((out, n), BF16), ((n, d), BF16)] + saves,
        saves
        + [
            ((n, n), F32), ((d, ff), BF16), ((d, ff), BF16), ((ff, d), BF16), ((n, 3 * d), BF16),
            ((HEADS, n), F32), ((n, d), F32), ((n, d), F32), ((n, ff), BF16), ((n, d), F32),
            ((n, d), BF16), sems(4), sems(8 + 2 * ff // d),
        ],
        "vv" + "a" * 10,
        flops=16_000_000_000,
    )(at, tallies, classes, *weights, x2, adj, pm, pb, bias, upb, downb, *norms)
    return g, pred, (x3, h, gu, gf, x2, gqkv, o, ga, vec, gpm)


def share_shapes(d, ff):
    return [((ff // d * (d // 2) + ff // 2, d), BF16)] * 2, [((2 * d, d), BF16)] * 2


def second_weights(at, rows, shared_rows):
    n, d = rows[0][0].shape
    ff = rows[0][1].shape[1]
    feed, att = share_shapes(d, ff)
    outs = feed + att + [((shared_rows, d), F32)]
    return call(
        second_weights_kernel,
        "s" + "a" * 20,
        outs,
        [(a.shape, a.dtype) for a in (*rows[0], *rows[1])]
        + outs
        + [((2, d, n), BF16)] * 3
        + [sems(20), sems(5)],
        "a" * 5,
        flops=6_000_000_000,
    )(at, *rows[0], *rows[1])


def first_feed_back(at, weights, g, x1, z1, h, dd, norms, after, prior=()):
    n, d = x1.shape
    ff = h.shape[1]
    feed, _ = share_shapes(d, ff)
    second = bool(prior)
    return call(
        functools.partial(first_feed_back_kernel, second),
        "saaaa" + "a" * (4 + len(prior)) + "vlla",
        [((n, d), BF16), ((VECTORS, d), F32)] + feed,
        feed
        + [
            ((n, d), F32), ((n, ff), BF16), ((n, d), BF16), ((n, ff), BF16),
            ((d, ff), BF16), ((ff, d), BF16), ((n, ff), BF16), ((n, d), BF16), ((n, d), F32),
            ((1, d, n), BF16), sems(4), sems(8),
        ],
        "vv" + ("v" if second else "a") * 2,
        flops=7_000_000_000,
    )(at, *weights, z1, dd, x1, h, *prior, g, *norms, after)


def first_attention_back(
    at, tallies, classes, weights, g, x0, z0, qkv, o, lse, norms, tok, tables, vec, after, shared_rows, size, prior=()
):
    n, d = x0.shape
    _, att = share_shapes(d, 4 * d)
    second = bool(prior)
    shared = [((shared_rows, d), F32)]
    if second:
        outs = [(tok.shape, BF16)] + [((att[0][0][0] + shared_rows // 2, d), BF16)] * 2
        extra = att + shared
    else:
        outs = [(tok.shape, F32)] + att + shared
        extra = outs[:3]
    return call(
        functools.partial(first_attention_back_kernel, second, size),
        "sssaa" + "a" * (6 + len(prior)) + "vlllllva",
        outs,
        extra
        + [
            ((n, d), F32), ((n, d), BF16), ((n, 3 * d), BF16), ((HEADS, n), F32), ((n, d), BF16),
            (tok.shape, BF16),
            ((n, n), F32), ((d, 4 * d), BF16), ((n, 3 * d), BF16), ((n, d), BF16), ((n, d), BF16),
            ((n, d), F32), ((1, d, n), BF16), ((1, d, n), BF16), ((VECTORS, d), F32),
            ((shared_rows, d), F32), sems(4), sems(9),
        ],
        ("v" if second else "a") * len(outs),
        flops=9_000_000_000,
    )(at, tallies, classes, *weights[:2], z0, o, qkv, lse, x0, tok, *prior, g, *norms, *tables, vec, after)


def shared_out(at, halves, tables, horizon, ff):
    d = halves[0].shape[1]
    outs = [(t.shape, F32) for t in tables]
    outs += [((3, d), F32), ((1, d), F32), ((1, d), F32), ((3, 2, d), F32), ((2, ff), F32), ((2, d), F32)]
    outs += [((horizon, d), F32), ((1, horizon), F32)]
    scratch = [((2, 2 * halves[0].shape[0], d), F32)]
    return call(shared_out_kernel, "savvvv", outs, scratch, vmem=24 << 20)(at, halves[0], *halves)


def entry_out(at, after, att, att_other, up, up_other, shape):
    return call(entry_out_kernel, "savvvv", [(shape, F32)], vmem=24 << 20)(
        at, after, att, att_other, up, up_other
    )[0]


def local_out(at, after, near, far, down, pred_near, pred_far):
    outs = [(near.shape, F32), (down.shape, F32), (pred_far.shape, BF16)]
    return call(series_out_kernel, "savvvvv", outs, vmem=24 << 20)(
        at, after, near, far, down, pred_near, pred_far
    )


CORES = [(0, 1), (1, 0), (2, 3), (3, 2)]
TO_NEAR = [(2, 0), (3, 1)]
TO_FAR = [(0, 2), (1, 3)]


def move(array, pairs):
    return lax.ppermute(array, "pipe", pairs)


def bits_of(axis, mask):
    place = lax.axis_index(axis)
    index = 0
    for position, m in enumerate(mask):
        index = index + ((place & m) // m) * (1 << position)
    return index


def xor_swap(array, dim, k):
    axis, mask = dim
    flip = sum(m for position, m in enumerate(mask) if k >> position & 1)
    return lax.ppermute(array, axis, [(i, i ^ flip) for i in range(lax.axis_size(axis))])


class Phase:
    def __init__(self, after=()):
        self.after = list(after)
        self.numbers = []
        self.args = []
        self.outs = []
        self.work = []

    def take(self, arrays):
        at = len(self.args)
        self.args += arrays
        return slice(at, at + len(arrays))

    def make(self, shapes):
        at = len(self.outs)
        self.outs += [(s, BF16) for s in shapes]
        return slice(at, at + len(shapes))

    def sum(self, arrays, group=0, ways=1):
        rows, cols = arrays[0].shape
        ins, outs = self.take(arrays), self.make([(rows // ways, cols)] * ways)
        number = len(self.numbers)
        self.numbers.append(group)

        def work(numbers, args, made):
            for k, out in enumerate(made[outs]):
                base = (numbers[number] ^ k) * out.shape[0]
                step = 128 if out.shape[0] % 128 == 0 else out.shape[0]
                for r in range(0, out.shape[0], step):
                    at = pl.ds(pl.multiple_of(base + r, 16), step)
                    total = sum(one[at, :].astype(F32) for one in args[ins])
                    out[r : r + step, :] = total.astype(BF16)

        self.work.append(work)
        return outs

    def join(self, arrays, group, blocks=None):
        ways = len(arrays)
        rows, cols = arrays[0].shape
        if blocks is None:
            shapes = [(rows * ways, cols)]
        else:
            shapes = [(blocks[0] * blocks[1], cols), (blocks[0] * blocks[2], cols)]
        ins, outs = self.take(arrays), self.make(shapes)
        number = len(self.numbers)
        self.numbers.append(group)

        def work(numbers, args, made):
            for k, one in enumerate(args[ins]):
                which = numbers[number] ^ k
                if blocks is None:
                    made[outs][0][pl.ds(pl.multiple_of(which * rows, 16), rows), :] = one[...]
                    continue
                count, block, gap = blocks
                for p in range(count // ways):
                    at = p * (block + gap)
                    for out, skip, size in zip(made[outs], (0, block), (block, gap)):
                        to = pl.ds(pl.multiple_of((which * (count // ways) + p) * size, 16), size)
                        out[to, :] = one[at + skip : at + skip + size, :]

        self.work.append(work)
        return outs

    def run(self):
        count, extra = len(self.args), len(self.after)

        def kernel(numbers, *refs):
            refs = refs[extra:]
            for work in self.work:
                work(numbers, refs[:count], refs[count:])

        made = call(
            kernel, "s" + "a" * extra + "v" * count, self.outs, vmem=24 << 20
        )(scalars(*self.numbers), *self.after, *self.args)
        return made


def plane_dims():
    bits = [1 << i for i in range((lax.axis_size("dp") - 1).bit_length())]
    groups = [tuple(bits[:1])] + [tuple(bits[i : i + 2]) for i in range(1, len(bits), 2)]
    return [("dp", group) for group in groups]


def swaps(pieces, dim):
    return [pieces[0]] + [xor_swap(pieces[k], dim, k) for k in range(1, len(pieces))]


def plane_sums(feed, att, between, blocks, finish_feed):
    dims = plane_dims()
    count = len(dims)
    ways = [1 << len(dim[1]) for dim in dims]
    place = [bits_of(*dim) for dim in dims]
    rounds = 2 * count
    arrays = [feed[0], move(feed[1], CORES)]
    other = None
    done = {}

    def step(phase, arrays, number):
        if number < count:
            return phase.sum(arrays, place[number], ways[number]), dims[number], False
        if number == count:
            return phase.sum(arrays), dims[-1], True
        last = 2 * count - number
        if number < rounds:
            return phase.join(arrays, place[last]), dims[last - 1], True
        return None

    def send(made, queued):
        outs, dim, gather = queued
        pieces = made[outs]
        if gather:
            pieces = pieces * (1 << len(dim[1]))
        return swaps(pieces, dim)

    phase = Phase()
    queued = step(phase, arrays, 0)
    made = phase.run()
    arrays = send(made, queued)
    att, after = between(made[0])
    for number in range(1, rounds + 3):
        if number == rounds + 2:
            after = done["local"]()
        phase = Phase([after] if number in (1, rounds + 2) else [])
        queued_feed = step(phase, arrays, number) if number < rounds else None
        if number == rounds:
            queued_feed = phase.join(arrays, place[0])
        queued_att = None
        if number >= 2:
            if number - 2 < rounds:
                queued_att = step(phase, other, number - 2)
            else:
                queued_att = phase.join(other, place[0], blocks)
        if number == 1:
            queued_send = phase.sum([att[1]])
        made = phase.run()
        if number == 1:
            other = [att[0], move(made[queued_send][0], CORES)]
        if number < rounds:
            arrays = send(made, queued_feed)
        elif number == rounds:
            done["feed"] = made[queued_feed][0]
        if number >= 2:
            if number - 2 < rounds:
                other = send(made, queued_att)
                if number == rounds + 1:
                    done["local"] = finish_feed(done["feed"])
            else:
                done["att"], done["shared"] = made[queued_att]
    return done


def per_device(
    lookback_readings,
    prediction_adjoint,
    variate_tallies,
    lookback_classes,
    brief_lift_table,
    moderate_lift_table,
    distant_lift_table,
    lift_offsets,
    part_entry_arrays,
    part_shrink_lines,
    part_layernorm_scale,
    part_layernorm_offset,
    mixing_offsets,
    expand_offsets,
    shrink_offsets,
    prediction_matrix,
    prediction_offset,
):
    place = lax.axis_index("pipe")
    core, far = place & 1, place // 2
    places = [scalars(core, far, r) for r in range(2)]
    at = places[0]
    entry, shrink = part_entry_arrays[0], part_shrink_lines[0]
    entry_other, shrink_other = move(entry, CORES), move(shrink, CORES)
    tok, adjoint = lookback_readings[0].T, prediction_adjoint[0].T
    tables = (brief_lift_table, moderate_lift_table, distant_lift_table)
    norm = jnp.concatenate([part_layernorm_scale, part_layernorm_offset], 0)

    weights = (entry, entry_other, shrink, shrink_other)
    norms = (norm, move(norm, CORES))
    toks = (tok, move(tok, TO_NEAR))
    adjoints = (move(adjoint, TO_FAR), adjoint)
    layout = (variate_tallies, lookback_classes)
    mixing = mixing_offsets.transpose(1, 0, 2)

    first = []
    arrived = []
    for r in range(2):
        out = first_layer(
            places[r], *layout, weights, toks[r], tables, lift_offsets, mixing, expand_offsets,
            shrink_offsets, norms,
        )
        first.append(out[1:])
        arrived.append(move(out[0], TO_FAR))
    second = []
    returned = []
    predictions = []
    for r in range(2):
        g, prediction, saved = second_layer(
            places[r], *layout, weights, arrived[r], adjoints[r], prediction_matrix.T,
            prediction_offset[None], mixing, expand_offsets, shrink_offsets, norms,
        )
        returned.append(move(g, TO_NEAR))
        predictions.append(prediction)
        second.append(saved)
    shared_rows = max(768, 32 * lax.axis_size("dp"))
    away = second_weights(at, second, shared_rows)

    size = lax.axis_size("dp")
    x0, z0, qkv, o, lse, x1, z1, h, d = first[0]
    g, vec, *feed = first_feed_back(at, weights, returned[0], x1, z1, h, d, norms, arrived[1])
    near_series, *att, shared = first_attention_back(
        places[0], *layout, weights, g, x0, z0, qkv, o, lse, norms, toks[0], tables, vec, g,
        shared_rows, size,
    )
    x0, z0, qkv, o, lse, x1, z1, h, d = first[1]
    g, vec, *feed = first_feed_back(
        at, weights, returned[1], x1, z1, h, d, norms, att[0], (*feed, *away[:2])
    )
    far_series = []

    def between(after):
        series, keep, send = first_attention_back(
            places[1], *layout, weights, g, x0, z0, qkv, o, lse, norms, toks[1], tables, vec, after,
            shared_rows, size, (*att, shared, *away[2:]),
        )
        far_series.append(series)
        return (keep, send), keep

    held = {}
    rows = entry.shape[0] * entry.shape[1] // shrink.shape[1] // 2

    def finish_feed(feed):
        held["up"] = move(feed[:rows], [(0, 1), (2, 3)])
        held["series"] = move(far_series[0], TO_FAR)
        held["prediction"] = move(predictions[0], TO_NEAR)

        def local():
            held["local"] = local_out(
                at, feed, near_series, held["series"], feed[rows:], held["prediction"], predictions[1]
            )
            return held["local"][1]

        return local

    blocks = (size, att[0].shape[0] // size, shared_rows // 2 // size)
    sums = plane_sums(feed, None, between, blocks, finish_feed)
    att_other = move(sums["att"], [(1, 0), (3, 2)])
    shared_other = move(sums["shared"], CORES)
    shared_away = move(sums["shared"], TO_FAR + TO_NEAR)
    series_grad, down_grad, prediction = held["local"]
    entry_grad = entry_out(
        at, series_grad, sums["att"], att_other, sums["feed"][:rows], held["up"], entry.shape
    )
    t0, t1, t2, embb, gain, offset, attb, upb, downb, pw, pb = shared_out(
        at, (sums["shared"], shared_other, shared_away, move(shared_away, CORES)), tables,
        prediction_matrix.shape[1], entry.shape[1],
    )
    return (
        prediction.T[None],
        series_grad.T[None],
        t0,
        t1,
        t2,
        embb,
        entry_grad[None],
        down_grad[None],
        gain,
        offset,
        attb.transpose(1, 0, 2),
        upb,
        downb,
        pw.T,
        pb[0],
    )


def solution(mesh):
    placed = (
        P("pipe", "dp", None),
        P("pipe", "dp", None),
        P(None, "dp", None),
        P(None, "dp", None),
        P(),
        P(),
        P(),
        P(),
        P("pipe", None, None),
        P("pipe", None, None),
        P("pipe", None),
        P("pipe", None),
        P(),
        P(),
        P(),
        P(),
        P(),
    )
    return jax.shard_map(
        per_device,
        mesh=mesh,
        in_specs=placed,
        out_specs=(
            P("pipe", "dp", None),
            P("pipe", "dp", None),
            P(),
            P(),
            P(),
            P(),
            P("pipe", None, None),
            P("pipe", None, None),
            P("pipe", None),
            P("pipe", None),
            P(),
            P(),
            P(),
            P(),
            P(),
        ),
        check_vma=False,
    )
```

```python
import functools

import jax
import jax.numpy as jnp
from jax import lax
from jax.experimental import pallas as pl
from jax.experimental.pallas import tpu as pltpu
from jax.sharding import PartitionSpec as P

HEADS = 8
HEAD_DIM = 64
F32 = jnp.float32
BF16 = jnp.bfloat16
VECTOR_ROW = 624
VECTORS = 16


def nn(a, b):
    return lax.dot_general(a, b, (((1,), (0,)), ((), ())), preferred_element_type=F32)


def nt(a, b):
    return lax.dot_general(a, b, (((1,), (1,)), ((), ())), preferred_element_type=F32)


def tn(a, b):
    return lax.dot_general(a, b, (((0,), (0,)), ((), ())), preferred_element_type=F32)


def column_sum(a):
    return jnp.sum(a.astype(F32), 0, keepdims=True)


def normalise(z):
    centre = z - jnp.mean(z, -1, keepdims=True)
    inverse = lax.rsqrt(jnp.mean(centre * centre, -1, keepdims=True) + 1e-05)
    return centre * inverse, inverse


def norm_back(upstream, z, gain):
    normed, inverse = normalise(z)
    gain_grad = jnp.sum(upstream * normed, 0, keepdims=True)
    offset_grad = jnp.sum(upstream, 0, keepdims=True)
    scaled = upstream * gain
    back = inverse * (
        scaled
        - jnp.mean(scaled, -1, keepdims=True)
        - normed * jnp.mean(scaled * normed, -1, keepdims=True)
    )
    return back, gain_grad, offset_grad


def gelu_both(u):
    bell = jnp.exp(u * u * -0.5)
    t = 1.0 / (1.0 + (0.3275911 * 0.5**0.5) * jnp.abs(u))
    poly = t * (
        0.127414796
        + t * (-0.142248368 + t * (0.7107068705 + t * (-0.7265760135 + t * 0.5307027145)))
    )
    half = poly * bell
    phi = jnp.where(u >= 0, 1.0 - half, half)
    return u * phi, phi + u * bell * 0.3989422804014327


def same_window_bias(seg_col, seg_row):
    return jnp.where(seg_col == seg_row, 0.0, -1e30).astype(F32)


class Choice:
    def __init__(self, index, sources, place, sem):
        self.index = index
        self.copies = [pltpu.make_async_copy(s, place, sem) for s in sources]

    def start(self):
        for k, copy in enumerate(self.copies):
            pl.when(self.index == k)(copy.start)

    def wait(self):
        for k, copy in enumerate(self.copies):
            pl.when(self.index == k)(copy.wait)


def weight_loads(core, entry, other, shrink, shrink_other, att_ref, up_ref, down_ref, sem):
    loads = []
    if att_ref is not None:
        loads.append(Choice(core, (entry, other), att_ref, sem.at[0]))
    if up_ref is not None:
        loads.append(Choice(1 - core, (entry, other), up_ref, sem.at[1]))
        half = down_ref.shape[0] // 2
        low, high = down_ref.at[pl.ds(0, half)], down_ref.at[pl.ds(half, half)]
        loads.append(Choice(core, (shrink, shrink_other), low, sem.at[2]))
        loads.append(Choice(1 - core, (shrink, shrink_other), high, sem.at[3]))
    for one in loads:
        one.start()
    return loads


def chosen_norms(core, own_ref, other_ref):
    own, other = own_ref[...], other_ref[...]
    first = core == 0
    return jnp.where(first, own, other), jnp.where(first, other, own)


class Moves:
    def __init__(self, sem):
        self.sem = sem
        self.started = []

    def start(self, source, target):
        copy = pltpu.make_async_copy(source, target, self.sem.at[len(self.started)])
        copy.start()
        self.started.append(copy)
        return copy


class Small:
    def __init__(self, pairs, sem):
        self.copies = [pltpu.make_async_copy(s, t, sem.at[i]) for i, (s, t) in enumerate(pairs)]

    def start(self):
        for copy in self.copies:
            copy.start()

    def wait(self):
        for copy in self.copies:
            copy.wait()


def row_windows(tallies, classes, micro, count):
    windows = 4
    ends, total = [], 0
    for w in range(windows - 1):
        total = total + tallies[micro, 0, w]
        ends.append(total)
    out = []
    for shape, axis in (((count, 1), 0), ((1, count), 1)):
        position = lax.broadcasted_iota(jnp.int32, shape, axis)
        window = sum((position >= end).astype(jnp.int32) for end in ends)
        group = jnp.full(shape, classes[micro, 0, 0], jnp.int32)
        for w in range(1, windows):
            group = jnp.where(window == w, classes[micro, 0, w], group)
        out.append((window, group))
    return out


def attention_core(x, w_ref, biases, norm, mask_ref, qkv_ref, o_ref, lse_ref, z_ref):
    width = x.shape[1]
    qkv_ref[:, :width] = ((nn(x, w_ref[:, :width]) + biases[0]) * HEAD_DIM**-0.5).astype(BF16)
    qkv_ref[:, width : 2 * width] = nn(x, w_ref[:, width : 2 * width]).astype(BF16)
    qkv_ref[:, 2 * width : 3 * width] = (
        nn(x, w_ref[:, 2 * width : 3 * width]) + biases[1]
    ).astype(BF16)
    pair = 2 * HEAD_DIM
    low = lax.broadcasted_iota(jnp.int32, (1, pair), 1) < HEAD_DIM
    for p in range(HEADS // 2):
        q2 = qkv_ref[:, p * pair : (p + 1) * pair]
        k2 = qkv_ref[:, width + p * pair : width + (p + 1) * pair]
        v2 = qkv_ref[:, 2 * width + p * pair : 2 * width + (p + 1) * pair]
        v2t = v2.T
        zero = jnp.zeros_like(k2)
        both = nt(jnp.concatenate([jnp.where(low, k2, zero), jnp.where(low, zero, k2)], 0), q2)
        parts = []
        count = k2.shape[0]
        for h in range(2):
            s = both[h * count : (h + 1) * count, :] + mask_ref[...]
            top = jnp.max(s, 0, keepdims=True)
            e = jnp.exp(s - top)
            total = jnp.sum(e, 0, keepdims=True)
            lse_ref[2 * p + h : 2 * p + h + 1, :] = top + jnp.log(total)
            ot = nn(v2t[h * HEAD_DIM : (h + 1) * HEAD_DIM, :], e.astype(BF16))
            parts.append(ot * (1.0 / total))
        o_ref[:, p * pair : (p + 1) * pair] = jnp.concatenate(parts, 0).T.astype(BF16)
    z = x.astype(F32) + (nn(o_ref[...], w_ref[:, 3 * width :]) + biases[2])
    z_ref[...] = z
    return (normalise(z)[0] * norm[0:1, :] + norm[1:2, :]).astype(BF16)


def feed_core(x, up_ref, down_ref, upb, downb, norm, h_ref, d_ref, z_ref, done=None, block=512):
    total = None
    for c in range(0, up_ref.shape[1], block):
        u = nn(x, up_ref[:, c : c + block]) + upb[:, c : c + block]
        h, d = gelu_both(u)
        hb = h.astype(BF16)
        h_ref[:, c : c + block] = hb
        d_ref[:, c : c + block] = d.astype(BF16)
        if done is not None:
            done(slice(c, c + block))
        part = nn(hb, down_ref[c : c + block, :])
        total = part if total is None else total + part
    z = x.astype(F32) + (total + downb)
    z_ref[...] = z
    return (normalise(z)[0] * norm[0:1, :] + norm[1:2, :]).astype(BF16)


def feed_back_chain(upstream, z_ref, d_ref, up_ref, down_ref, norm, gu_ref, gf_ref, vec_ref, gx_acc,
    ready=None, done=None,
):
    back, gain_grad, offset_grad = norm_back(upstream, z_ref[...], norm[0:1, :])
    gf_ref[...] = back.astype(BF16)
    gx_acc[...] = back
    width = back.shape[1]
    if ready is not None:
        ready()
    for b in range(up_ref.shape[1] // width):
        cols = slice(b * width, (b + 1) * width)
        gu = (nt(gf_ref[...], down_ref[cols, :]) * d_ref[:, cols].astype(F32)).astype(BF16)
        gu_ref[:, cols] = gu
        if done is not None:
            done(cols)
        vec_ref[7 + b : 8 + b, :] = column_sum(gu)
        gx_acc[...] += nt(gu, up_ref[:, cols])
    vec_ref[11:12, :] = column_sum(gf_ref[...])
    vec_ref[14:15, :] = gain_grad
    vec_ref[15:16, :] = offset_grad


def attention_back_chain(
    upstream, z_ref, qkv_ref, o_ref, lse_ref, w_ref, norm, mask_ref,
    gqkv_ref, ga_ref, go_ref, vec_ref, gx_acc, ready=None,
):
    back, gain_grad, offset_grad = norm_back(upstream, z_ref[...], norm[0:1, :])
    width = back.shape[1]
    ga_ref[...] = back.astype(BF16)
    gx_acc[...] = back
    vec_ref[6:7, :] = column_sum(ga_ref[...])
    vec_ref[12:13, :] = gain_grad
    vec_ref[13:14, :] = offset_grad
    if ready is not None:
        ready()
    go_ref[...] = nt(ga_ref[...], w_ref[:, 3 * width :]).astype(BF16)
    pair = 2 * HEAD_DIM
    low = lax.broadcasted_iota(jnp.int32, (1, pair), 1) < HEAD_DIM
    for p in range(HEADS // 2):
        q2 = qkv_ref[:, p * pair : (p + 1) * pair]
        k2 = qkv_ref[:, width + p * pair : width + (p + 1) * pair]
        v2 = qkv_ref[:, 2 * width + p * pair : 2 * width + (p + 1) * pair]
        go2 = go_ref[:, p * pair : (p + 1) * pair]
        o2 = o_ref[:, p * pair : (p + 1) * pair]
        k2t = k2.T
        prod = (go2.astype(F32) * o2.astype(F32)).T
        zero = jnp.zeros_like(k2)

        def split(a):
            return jnp.concatenate([jnp.where(low, a, zero), jnp.where(low, zero, a)], 0)

        both = nt(split(k2), q2)
        both_gp = nt(split(v2), go2)
        count = k2.shape[0]
        gq, all_w, all_g = [], [], []
        for h in range(2):
            lanes = slice(h * HEAD_DIM, (h + 1) * HEAD_DIM)
            rows = slice(h * count, (h + 1) * count)
            centred = jnp.sum(prod[lanes, :], 0, keepdims=True)
            weights = jnp.exp(both[rows, :] + mask_ref[...] - lse_ref[2 * p + h : 2 * p + h + 1, :])
            gs = (weights * (both_gp[rows, :] - centred)).astype(BF16)
            all_w.append(weights.astype(BF16))
            all_g.append(gs)
            gq.append(nn(k2t[lanes, :], gs) * HEAD_DIM**-0.5)
        gv = nn(jnp.concatenate(all_w, 1), split(go2))
        gk = nn(jnp.concatenate(all_g, 1), split(q2))
        cols = slice(p * pair, (p + 1) * pair)
        gqkv_ref[:, cols] = jnp.concatenate(gq, 0).T.astype(BF16)
        gqkv_ref[:, width + p * pair : width + (p + 1) * pair] = gk.astype(BF16)
        gqkv_ref[:, 2 * width + p * pair : 2 * width + (p + 1) * pair] = gv.astype(BF16)
    gx_acc[...] += nt(gqkv_ref[...], w_ref[:, : 3 * width])
    vec_ref[4:5, :] = column_sum(gqkv_ref[:, :width])
    vec_ref[5:6, :] = column_sum(gqkv_ref[:, 2 * width :])


def shares(core, rows):
    mine = pl.ds(pl.multiple_of(core * rows, rows), rows)
    other = pl.ds(pl.multiple_of((1 - core) * rows, rows), rows)
    return mine, other


def feed_weight_grads(core, rows_of, prior, outs, xt_ref):
    width = rows_of[0][0].shape[1]
    half = width // 2
    blocks = rows_of[0][1].shape[1] // width
    for i, (x, _, _, _) in enumerate(rows_of):
        xt_ref[i] = x[...].T
    parts = shares(core, half)

    def put(index, at, value):
        if prior is not None:
            value = value + prior[index][at, :].astype(F32)
        outs[index][at, :] = value.astype(BF16)

    for j in range(blocks):
        b = lax.rem(j + core * (blocks // 2), blocks)
        cols = pl.ds(pl.multiple_of(b * width, width), width)
        at = blocks * half + (j % (blocks // 2)) * width
        value = sum(tn(h[:, cols], gf[...]) for _, h, _, gf in rows_of)
        put(j // (blocks // 2), slice(at, at + width), value)
        at = pl.ds(pl.multiple_of(b * half, half), half)
        for index, part in enumerate(parts):
            put(index, at, sum(nn(xt_ref[i, part, :], gu[:, cols]) for i, (_, _, gu, _) in enumerate(rows_of)))


def store_mixed(out, row, value, block, gap):
    for k in range(0, value.shape[0], block):
        at = (row + k) // block * (block + gap)
        out[at : at + block, :] = value[k : k + block, :]


def attention_weight_grads(core, rows_of, prior, outs, xt_ref, ot_ref, block=None, gap=0):
    width = rows_of[0][0].shape[1]
    half = width // 2
    parts = shares(core, half)

    def put(index, b, value):
        at = slice(b * half, (b + 1) * half)
        if prior is not None:
            value = value + prior[index][at, :].astype(F32)
        store_mixed(outs[index], b * half, value.astype(BF16), block or half, gap)

    for i, (_, _, o, _) in enumerate(rows_of):
        ot_ref[i] = o[...].T
    for index, part in enumerate(parts):
        put(index, 3, sum(nn(ot_ref[i, part, :], ga[...]) for i, (_, _, _, ga) in enumerate(rows_of)))
    for i, (x, _, _, _) in enumerate(rows_of):
        xt_ref[i] = x[...].T
    for b in range(3):
        for index, part in enumerate(parts):
            put(index, b, sum(
                nn(xt_ref[i, part, :], gqkv[:, b * width : (b + 1) * width])
                for i, (_, gqkv, _, _) in enumerate(rows_of)
            ))


def embed(tok, group_col, group_row, tables, off_ref):
    look = tok.shape[0]
    total = None
    for g, t_ref in enumerate(tables):
        skip = look - t_ref.shape[0]
        masked = jnp.where(group_row == g, tok[skip:, :], jnp.zeros((1, 1), BF16))
        part = tn(masked, t_ref[...]) + jnp.where(group_col == g, off_ref[g : g + 1, :], 0.0)
        total = part if total is None else total + part
    return total.astype(BF16)


def first_layer_kernel(
    small, at, tallies, classes, entry, other, shrink, shrink_other,
    adj_in, tok_ref, t0_ref, t1_ref, t2_ref, off_ref, bias_ref, upb_ref, downb_ref, norm_ref, norm_other_ref,
    x2_ref, adj_out, x0_out, z0_out, qkv_out, o_out, lse_out, x1_out, z1_out, h_out, d_out,
    x0_ref, z0_ref, qkv_ref, o_ref, lse_ref, x1_ref, z1_ref, h_ref, d_ref,
    mask_ref, att_ref, up_ref, down_ref, sem, out_sem,
):
    @pl.when(at[1] == 0)
    def _():
        core = at[0]
        small.start()
        loads = weight_loads(
            core, entry, other, shrink, shrink_other, att_ref, up_ref, down_ref, sem
        )
        out = Moves(out_sem)
        (wc, gc), (wr, gr) = row_windows(tallies, classes, core + 2 * at[2], x0_ref.shape[0])
        mask_ref[...] = same_window_bias(wc, wr)
        small.wait()
        x0_ref[...] = embed(tok_ref[...], gc, gr, (t0_ref, t1_ref, t2_ref), off_ref)
        out.start(x0_ref, x0_out)
        out.start(adj_in, adj_out)
        norm_att, norm_feed = chosen_norms(core, norm_ref, norm_other_ref)
        loads[0].wait()
        x1_ref[...] = attention_core(
            x0_ref[...], att_ref, [bias_ref[i, 0:1, :] for i in range(3)], norm_att, mask_ref,
            qkv_ref, o_ref, lse_ref, z0_ref,
        )
        for source, target in (
            (qkv_ref, qkv_out), (o_ref, o_out), (lse_ref, lse_out), (z0_ref, z0_out), (x1_ref, x1_out)
        ):
            out.start(source, target)
        for one in loads[1:]:
            one.wait()

        def done(cols):
            out.start(h_ref.at[:, cols], h_out.at[:, cols])
            out.start(d_ref.at[:, cols], d_out.at[:, cols])

        x2_ref[...] = feed_core(
            x1_ref[...], up_ref, down_ref, upb_ref[0:1, :], downb_ref[0:1, :], norm_feed,
            h_ref, d_ref, z1_ref, done,
        )
        out.start(z1_ref, z1_out)
        for copy in out.started:
            copy.wait()


def second_layer_kernel(
    small, at, tallies, classes, entry, other, shrink, shrink_other,
    x2_ref, adj_ref, pm_ref, pb_ref, bias_ref, upb_ref, downb_ref, norm_ref, norm_other_ref,
    g_ref, pred_ref, x2_out, gqkv_out, o_out, ga_out, x3_out, gu_out, h_out, gf_out, vec_out, gpm_out,
    gqkv_ref, o_ref, ga_ref, x3_ref, gu_ref, h_ref, gf_ref, vec_ref, gpm_ref,
    mask_ref, att_ref, up_ref, down_ref, qkv_ref, lse_ref, z2_ref, z3_ref, d_ref, gx_acc, go_ref,
    sem, out_sem,
):
    @pl.when(at[1] == 1)
    def _():
        core = at[0]
        small.start()
        loads = weight_loads(
            core, entry, other, shrink, shrink_other, att_ref, up_ref, down_ref, sem
        )
        out = Moves(out_sem)
        out.start(x2_ref, x2_out)
        (wc, _), (wr, _) = row_windows(tallies, classes, core + 2 * at[2], x2_ref.shape[0])
        mask_ref[...] = same_window_bias(wc, wr)
        small.wait()
        norm_att, norm_feed = chosen_norms(core, norm_ref, norm_other_ref)
        loads[0].wait()
        x3_ref[...] = attention_core(
            x2_ref[...], att_ref, [bias_ref[i, 1:2, :] for i in range(3)], norm_att, mask_ref,
            qkv_ref, o_ref, lse_ref, z2_ref,
        )
        out.start(o_ref, o_out)
        out.start(x3_ref, x3_out)
        for one in loads[1:]:
            one.wait()
        y = feed_core(
            x3_ref[...], up_ref, down_ref, upb_ref[1:2, :], downb_ref[1:2, :], norm_feed,
            h_ref, d_ref, z3_ref, lambda cols: out.start(h_ref.at[:, cols], h_out.at[:, cols]),
        )
        pm, adj = pm_ref[...], adj_ref[...]
        pred_ref[...] = (nt(pm, y) + pb_ref[...].T).astype(BF16)
        gpm_ref[...] = nn(adj, y)
        out.start(gpm_ref, gpm_out)
        width = y.shape[1]
        horizon = adj.shape[0]
        gpb = jnp.sum(adj.astype(F32), 1, keepdims=True).T
        vec_ref[0:1, :] = jnp.concatenate([gpb, jnp.zeros((1, width - horizon), F32)], 1)
        vec_ref[1:4, :] = jnp.zeros((3, width), F32)
        feed_back_chain(
            tn(adj, pm), z3_ref, d_ref, up_ref, down_ref, norm_feed, gu_ref, gf_ref, vec_ref, gx_acc, None,
            lambda cols: out.start(gu_ref.at[:, cols], gu_out.at[:, cols]),
        )
        out.start(gf_ref, gf_out)
        attention_back_chain(
            gx_acc[...].astype(BF16).astype(F32), z2_ref, qkv_ref, o_ref, lse_ref, att_ref, norm_att,
            mask_ref, gqkv_ref, ga_ref, go_ref, vec_ref, gx_acc,
        )
        g_ref[...] = gx_acc[...].astype(BF16)
        out.start(ga_ref, ga_out)
        out.start(gqkv_ref, gqkv_out)
        out.start(vec_ref, vec_out)
        for copy in out.started:
            copy.wait()


def second_weights_kernel(at, *refs):
    sources, refs = refs[:20], refs[20:]
    outs, refs = refs[:5], refs[5:]
    held, refs = refs[:20], refs[20:]
    made, (xt_ref, xt2_ref, ot_ref, sem, out_sem) = refs[:5], refs[5:]

    @pl.when(at[1] == 1)
    def _():
        core = at[0]
        loads = Moves(sem)
        for i in range(10):
            for r in range(2):
                loads.start(sources[10 * r + i], held[10 * r + i])
        out = Moves(out_sem)
        rows = held[:10], held[10:]
        for copy in loads.started[:8]:
            copy.wait()
        feed_weight_grads(core, [r[:4] for r in rows], None, made[:2], xt_ref)
        for i in range(2):
            out.start(made[i], outs[i])
        for copy in loads.started[8:]:
            copy.wait()
        attention_weight_grads(core, [r[4:8] for r in rows], None, made[2:4], xt2_ref, ot_ref)
        horizon = rows[0][9].shape[0]
        shared_ref = made[4]
        shared_ref[...] = jnp.zeros(shared_ref.shape, F32)
        shared_ref[:horizon, :] = rows[0][9][...] + rows[1][9][...]
        shared_ref[VECTOR_ROW : VECTOR_ROW + VECTORS, :] = rows[0][8][...] + rows[1][8][...]
        for i in range(2, 5):
            out.start(made[i], outs[i])
        for copy in out.started:
            copy.wait()


def first_feed_back_kernel(second, small, at, entry, other, shrink, shrink_other, *refs):
    z1_in, d_in, x1_in, h_in = refs[:4]
    refs = refs[4:]
    prior, far_in = (refs[:2], refs[2:4]) if second else (None, None)
    refs = refs[4:] if second else refs
    g_ref, norm_ref, norm_other_ref, _, gx_ref, vec_ref = refs[:6]
    outs, refs = refs[6:8], refs[8:]
    if second:
        held, refs = refs[:2], refs[2:]
    else:
        made, refs = refs[:2], refs[2:]
    z1_ref, d_ref, x1_ref, h_ref, up_ref, down_ref, gu_ref, gf_ref, gx_acc, xt_ref, sem, in_sem = refs

    @pl.when(at[1] == 0)
    def _():
        core = at[0]
        loads = Moves(in_sem)
        small.start()
        loads.start(z1_in, z1_ref)
        weights = weight_loads(core, entry, other, shrink, shrink_other, None, up_ref, down_ref, sem)
        loads.start(d_in, d_ref)
        loads.start(x1_in, x1_ref)
        loads.start(h_in, h_ref)
        if second:
            for source, target in zip(prior, held):
                loads.start(source, target)
        small.wait()
        _, norm_feed = chosen_norms(core, norm_ref, norm_other_ref)
        vec_ref[...] = jnp.zeros(vec_ref.shape, F32)
        loads.started[0].wait()

        def ready():
            loads.started[1].wait()
            for one in weights:
                one.wait()

        feed_back_chain(
            g_ref[...].astype(F32), z1_ref, d_ref, up_ref, down_ref, norm_feed,
            gu_ref, gf_ref, vec_ref, gx_acc, ready,
        )
        gx_ref[...] = gx_acc[...].astype(BF16)
        for copy in loads.started[2:]:
            copy.wait()
        feed_weight_grads(
            core, [(x1_ref, h_ref, gu_ref, gf_ref)], held if second else None,
            outs if second else made, xt_ref,
        )
        if not second:
            out = Moves(in_sem)
            for source, target in zip(made, outs):
                out.start(source, target)
            for copy in out.started:
                copy.wait()

    if second:
        @pl.when(at[1] == 1)
        def _():
            loads = Moves(in_sem)
            for source, target in zip(far_in, outs):
                loads.start(source, target)
            for copy in loads.started:
                copy.wait()


def first_attention_back_kernel(second, size, small, at, tallies, classes, entry, other, *refs):
    z0_in, o_in, qkv_in, lse_in, x0_in, tok_in = refs[:6]
    refs = refs[6:]
    prior, far_in = (refs[:3], refs[3:6]) if second else (None, None)
    refs = refs[6:] if second else refs
    g_ref, norm_ref, norm_other_ref, t0_ref, t1_ref, t2_ref, vec_in = refs[:7]
    refs = refs[8:]
    if second:
        (series_ref, keep_ref, send_ref), refs = refs[:3], refs[3:]
        held, refs = refs[:3], refs[3:]
        made = (keep_ref, send_ref)
    else:
        outs, refs = refs[:4], refs[4:]
        (series_ref, *made), refs = refs[:3], refs[3:]
    (z0_ref, o_ref, qkv_ref, lse_ref, x0_ref, tok_ref, mask_ref, att_ref, gqkv_ref, ga_ref, go_ref,
     gx_acc, xt_ref, ot_ref, vec_ref, acc_ref, sem, in_sem) = refs

    if second:
        half = acc_ref.shape[0] // 2
        gap = half // size
        block = keep_ref.shape[0] // size - gap
    else:
        block, gap = None, 0

    def split(total):
        total_ref = held[2]
        total_ref[...] = total
        for index, out in enumerate((keep_ref, send_ref)):
            first = (at[0] if index == 0 else 1 - at[0]) * half
            for p in range(size):
                rows = pl.ds(pl.multiple_of(first + p * gap, 16), gap)
                to = p * (block + gap) + block
                out[to : to + gap, :] = total_ref[rows, :].astype(BF16)

    @pl.when(at[1] == 0)
    def _():
        core = at[0]
        loads = Moves(in_sem)
        small.start()
        loads.start(z0_in, z0_ref)
        weights = weight_loads(core, entry, other, None, None, att_ref, None, None, sem)
        loads.start(o_in, o_ref)
        loads.start(qkv_in, qkv_ref)
        loads.start(lse_in, lse_ref)
        loads.start(x0_in, x0_ref)
        loads.start(tok_in, tok_ref)
        if second:
            for source, target in zip(prior, held):
                loads.start(source, target)
        small.wait()
        norm_att, _ = chosen_norms(core, norm_ref, norm_other_ref)
        (wc, _), (wr, gr) = row_windows(tallies, classes, core + 2 * at[2], x0_ref.shape[0])
        mask_ref[...] = same_window_bias(wc, wr)
        vec_ref[...] = vec_in[...]
        loads.started[0].wait()

        def ready():
            weights[0].wait()
            for copy in loads.started[1:4]:
                copy.wait()

        attention_back_chain(
            g_ref[...].astype(F32), z0_ref, qkv_ref, o_ref, lse_ref, att_ref, norm_att,
            mask_ref, gqkv_ref, ga_ref, go_ref, vec_ref, gx_acc, ready,
        )
        for copy in loads.started[4:]:
            copy.wait()
        attention_weight_grads(
            core, [(x0_ref, gqkv_ref, o_ref, ga_ref)], held[:2] if second else None,
            made, xt_ref, ot_ref, block, gap,
        )
        g = gx_acc[...].astype(BF16)
        look = tok_ref.shape[0]
        at_row = 0
        for i, t_ref in enumerate((t0_ref, t1_ref, t2_ref)):
            skip = look - t_ref.shape[0]
            chosen = gr == i
            part = jnp.where(chosen, nt(t_ref[...], g), 0.0)
            if i == 0:
                gx_s = [part]
            else:
                gx_s.append(part)
            masked = jnp.where(chosen, tok_ref[skip:, :], jnp.zeros((1, 1), BF16))
            acc_ref[at_row : at_row + look - skip, :] = nn(masked, g)
            at_row += look - skip
        short, mid, long = gx_s
        a, b = long.shape[0] - short.shape[0], long.shape[0] - mid.shape[0]
        series_ref[:b, :] = long[:b, :].astype(series_ref.dtype)
        series_ref[b:a, :] = (long[b:a, :] + mid[: a - b, :]).astype(series_ref.dtype)
        series_ref[a:, :] = (long[a:, :] + mid[a - b :, :] + short).astype(series_ref.dtype)
        groups = lax.broadcasted_iota(jnp.int32, (8, gr.shape[1]), 0)
        vec_ref[1:4, :] = nn((groups == gr).astype(BF16), g)[0:3, :]
        acc_ref[VECTOR_ROW : VECTOR_ROW + VECTORS, :] = vec_ref[...]
        rest = VECTOR_ROW + VECTORS
        acc_ref[rest:, :] = jnp.zeros((acc_ref.shape[0] - rest, acc_ref.shape[1]), F32)
        if second:
            split(acc_ref[...] + held[2][...])
        else:
            out = Moves(in_sem)
            for source, target in zip((series_ref, *made, acc_ref), outs):
                out.start(source, target)
            for copy in out.started:
                copy.wait()

    if second:
        @pl.when(at[1] == 1)
        def _():
            loads = Moves(in_sem)
            for source, target in zip(far_in, (held[0], held[1], acc_ref)):
                loads.start(source, target)
            for copy in loads.started:
                copy.wait()
            for source, target in zip(held, (keep_ref, send_ref)):
                store_mixed(target, 0, source[...], block, gap)
            split(acc_ref[...])


def shared_out_kernel(
    at, _, mine_ref, other_ref, mine_away_ref, other_away_ref,
    t0_ref, t1_ref, t2_ref, embb_ref, gain_ref, offset_ref, att_ref, up_ref, down_ref, pw_ref, pb_ref,
    all_ref,
):
    core, far = at[0], at[1]
    half = mine_ref.shape[0]
    for plane, pair in ((far, (mine_ref, other_ref)), (1 - far, (mine_away_ref, other_away_ref))):
        for who, source in ((core, pair[0]), (1 - core, pair[1])):
            all_ref[plane, pl.ds(pl.multiple_of(who * half, 16), half), :] = source[...].astype(F32)
    row = 0
    for out in (t0_ref, t1_ref, t2_ref):
        out[...] = all_ref[0, row : row + out.shape[0], :]
        row += out.shape[0]
    pw_ref[...] = all_ref[1, : pw_ref.shape[0], :]
    v = VECTOR_ROW
    width = all_ref.shape[2]
    pb_ref[...] = all_ref[1, v : v + 1, : pb_ref.shape[1]]
    embb_ref[...] = all_ref[0, v + 1 : v + 4, :]
    for l in range(2):
        for i in range(3):
            att_ref[i, l : l + 1, :] = all_ref[l, v + 4 + i : v + 5 + i, :]
        for b in range(4):
            up_ref[l : l + 1, b * width : (b + 1) * width] = all_ref[l, v + 7 + b : v + 8 + b, :]
        down_ref[l : l + 1, :] = all_ref[l, v + 11 : v + 12, :]
    gain_ref[...] = all_ref[far, pl.ds(v + 12 + 2 * core, 1), :]
    offset_ref[...] = all_ref[far, pl.ds(v + 13 + 2 * core, 1), :]


def entry_out_kernel(at, _, att_ref, att_other_ref, up_ref, up_other_ref, out_ref, mark_ref):
    rows = out_ref.shape[0] // 2
    width = att_ref.shape[1]
    mark_ref[...] = jnp.zeros(mark_ref.shape, F32)

    def write(low, high):
        for b in range(out_ref.shape[1] // width):
            cols = slice(b * width, (b + 1) * width)
            out_ref[:rows, cols] = low[b * rows : (b + 1) * rows, :].astype(F32)
            out_ref[rows:, cols] = high[b * rows : (b + 1) * rows, :].astype(F32)

    pl.when(at[0] == 0)(lambda: write(att_ref, att_other_ref))
    pl.when(at[0] == 1)(lambda: write(up_other_ref, up_ref))


def series_out_kernel(at, _, near_ref, far_ref, down_ref, pred_near_ref, pred_far_ref, out_ref, down_out, pred_out):
    down_out[...] = down_ref[...].astype(F32)

    @pl.when(at[1] == 0)
    def _():
        out_ref[...] = near_ref[...]
        pred_out[...] = pred_near_ref[...]

    @pl.when(at[1] == 1)
    def _():
        out_ref[...] = far_ref[...].astype(F32)
        pred_out[...] = pred_far_ref[...]


def call(kernel, kinds, outs, scratch=(), out_kinds=None, vmem=60 << 20, flops=0, nbytes=0):
    spaces = {
        "s": pl.BlockSpec(memory_space=pltpu.SMEM),
        "a": pl.BlockSpec(memory_space=pltpu.HBM),
        "l": pl.BlockSpec(memory_space=pltpu.HBM),
        "v": pl.BlockSpec(memory_space=pltpu.VMEM),
    }

    def run(*args):
        assert len(args) == len(kinds)
        loaded = [i for i, k in enumerate(kinds) if k == "l"]

        def body(*refs):
            ins = list(refs[: len(kinds)])
            middle, held, sem = refs[len(kinds) : -1 - len(loaded)], refs[-1 - len(loaded) : -1], refs[-1]
            small = Small([(ins[i], place) for i, place in zip(loaded, held)], sem)
            for i, place in zip(loaded, held):
                ins[i] = place
            kernel(small, *ins, *middle)

        own = [pltpu.VMEM(args[i].shape, args[i].dtype) for i in loaded] + [sems(len(loaded))]
        return pl.pallas_call(
            body if loaded else kernel,
            out_shape=[jax.ShapeDtypeStruct(s, d) for s, d in outs],
            in_specs=[spaces[k] for k in kinds],
            out_specs=[spaces[k] for k in out_kinds or "v" * len(outs)],
            scratch_shapes=[s if not isinstance(s, tuple) else pltpu.VMEM(*s) for s in scratch]
            + (own if loaded else []),
            compiler_params=pltpu.CompilerParams(vmem_limit_bytes=vmem),
            cost_estimate=pl.CostEstimate(flops=flops, bytes_accessed=nbytes, transcendentals=0),
        )(*args)

    return run


def scalars(*values):
    return jnp.stack([jnp.asarray(v, jnp.int32) for v in values])


def sems(count):
    return pltpu.SemaphoreType.DMA((count,))


def first_layer(at, tallies, classes, weights, adj, tok, tables, off, bias, upb, downb, norms):
    n, d, ff = tok.shape[1], off.shape[1], upb.shape[1]
    saves = [
        ((n, d), BF16), ((n, d), F32), ((n, 3 * d), BF16), ((n, d), BF16), ((HEADS, n), F32),
        ((n, d), BF16), ((n, d), F32), ((n, ff), BF16), ((n, ff), BF16),
    ]
    return call(
        first_layer_kernel,
        "sssaaaaa" + "l" * 10,
        [((n, d), BF16), (adj.shape, BF16)] + saves,
        saves
        + [((n, n), F32), ((d, ff), BF16), ((d, ff), BF16), ((ff, d), BF16), sems(4), sems(8 + 2 * ff // d)],
        "v" + "a" * 10,
        flops=10_000_000_000,
    )(at, tallies, classes, *weights, adj, tok, *tables, off, bias, upb, downb, *norms)


def second_layer(at, tallies, classes, weights, x2, adj, pm, pb, bias, upb, downb, norms):
    n, d = x2.shape
    ff, out = upb.shape[1], pm.shape[0]
    saves = [
        ((n, 3 * d), BF16), ((n, d), BF16), ((n, d), BF16), ((n, d), BF16), ((n, ff), BF16),
        ((n, ff), BF16), ((n, d), BF16), ((VECTORS, d), F32), ((out, d), F32),
    ]
    g, pred, x2, gqkv, o, ga, x3, gu, h, gf, vec, gpm = call(
        second_layer_kernel,
        "sssaaaav" + "l" * 8,
        [((n, d), BF16), ((out, n), BF16), ((n, d), BF16)] + saves,
        saves
        + [
            ((n, n), F32), ((d, ff), BF16), ((d, ff), BF16), ((ff, d), BF16), ((n, 3 * d), BF16),
            ((HEADS, n), F32), ((n, d), F32), ((n, d), F32), ((n, ff), BF16), ((n, d), F32),
            ((n, d), BF16), sems(4), sems(8 + 2 * ff // d),
        ],
        "vv" + "a" * 10,
        flops=16_000_000_000,
    )(at, tallies, classes, *weights, x2, adj, pm, pb, bias, upb, downb, *norms)
    return g, pred, (x3, h, gu, gf, x2, gqkv, o, ga, vec, gpm)


def share_shapes(d, ff):
    return [((ff // d * (d // 2) + ff // 2, d), BF16)] * 2, [((2 * d, d), BF16)] * 2


def second_weights(at, rows, shared_rows):
    n, d = rows[0][0].shape
    ff = rows[0][1].shape[1]
    feed, att = share_shapes(d, ff)
    outs = feed + att + [((shared_rows, d), F32)]
    return call(
        second_weights_kernel,
        "s" + "a" * 20,
        outs,
        [(a.shape, a.dtype) for a in (*rows[0], *rows[1])]
        + outs
        + [((2, d, n), BF16)] * 3
        + [sems(20), sems(5)],
        "a" * 5,
        flops=6_000_000_000,
    )(at, *rows[0], *rows[1])


def first_feed_back(at, weights, g, x1, z1, h, dd, norms, after, prior=()):
    n, d = x1.shape
    ff = h.shape[1]
    feed, _ = share_shapes(d, ff)
    second = bool(prior)
    return call(
        functools.partial(first_feed_back_kernel, second),
        "saaaa" + "a" * (4 + len(prior)) + "vlla",
        [((n, d), BF16), ((VECTORS, d), F32)] + feed,
        feed
        + [
            ((n, d), F32), ((n, ff), BF16), ((n, d), BF16), ((n, ff), BF16),
            ((d, ff), BF16), ((ff, d), BF16), ((n, ff), BF16), ((n, d), BF16), ((n, d), F32),
            ((1, d, n), BF16), sems(4), sems(8),
        ],
        "vv" + ("v" if second else "a") * 2,
        flops=7_000_000_000,
    )(at, *weights, z1, dd, x1, h, *prior, g, *norms, after)


def first_attention_back(
    at, tallies, classes, weights, g, x0, z0, qkv, o, lse, norms, tok, tables, vec, after, shared_rows, size, prior=()
):
    n, d = x0.shape
    _, att = share_shapes(d, 4 * d)
    second = bool(prior)
    shared = [((shared_rows, d), F32)]
    if second:
        outs = [(tok.shape, BF16)] + [((att[0][0][0] + shared_rows // 2, d), BF16)] * 2
        extra = att + shared
    else:
        outs = [(tok.shape, F32)] + att + shared
        extra = outs[:3]
    return call(
        functools.partial(first_attention_back_kernel, second, size),
        "sssaa" + "a" * (6 + len(prior)) + "vlllllva",
        outs,
        extra
        + [
            ((n, d), F32), ((n, d), BF16), ((n, 3 * d), BF16), ((HEADS, n), F32), ((n, d), BF16),
            (tok.shape, BF16),
            ((n, n), F32), ((d, 4 * d), BF16), ((n, 3 * d), BF16), ((n, d), BF16), ((n, d), BF16),
            ((n, d), F32), ((1, d, n), BF16), ((1, d, n), BF16), ((VECTORS, d), F32),
            ((shared_rows, d), F32), sems(4), sems(9),
        ],
        ("v" if second else "a") * len(outs),
        flops=9_000_000_000,
    )(at, tallies, classes, *weights[:2], z0, o, qkv, lse, x0, tok, *prior, g, *norms, *tables, vec, after)


def shared_out(at, halves, tables, horizon, ff):
    d = halves[0].shape[1]
    outs = [(t.shape, F32) for t in tables]
    outs += [((3, d), F32), ((1, d), F32), ((1, d), F32), ((3, 2, d), F32), ((2, ff), F32), ((2, d), F32)]
    outs += [((horizon, d), F32), ((1, horizon), F32)]
    scratch = [((2, 2 * halves[0].shape[0], d), F32)]
    return call(shared_out_kernel, "savvvv", outs, scratch, vmem=24 << 20)(at, halves[0], *halves)


def entry_out(at, after, att, att_other, up, up_other, shape):
    outs = [(shape, F32), ((8, 128), F32)]
    return call(entry_out_kernel, "savvvv", outs, vmem=24 << 20)(at, after, att, att_other, up, up_other)


def local_out(at, after, near, far, down, pred_near, pred_far):
    outs = [(near.shape, F32), (down.shape, F32), (pred_far.shape, BF16)]
    return call(series_out_kernel, "savvvvv", outs, vmem=24 << 20)(
        at, after, near, far, down, pred_near, pred_far
    )


CORES = [(0, 1), (1, 0), (2, 3), (3, 2)]
TO_NEAR = [(2, 0), (3, 1)]
TO_FAR = [(0, 2), (1, 3)]


def move(array, pairs):
    return lax.ppermute(array, "pipe", pairs)


def bits_of(axis, mask):
    place = lax.axis_index(axis)
    index = 0
    for position, m in enumerate(mask):
        index = index + ((place & m) // m) * (1 << position)
    return index


def xor_swap(array, dim, k):
    axis, mask = dim
    flip = sum(m for position, m in enumerate(mask) if k >> position & 1)
    return lax.ppermute(array, axis, [(i, i ^ flip) for i in range(lax.axis_size(axis))])


class Phase:
    def __init__(self, after=()):
        self.after = list(after)
        self.numbers = []
        self.args = []
        self.outs = []
        self.work = []

    def take(self, arrays):
        at = len(self.args)
        self.args += arrays
        return slice(at, at + len(arrays))

    def make(self, shapes):
        at = len(self.outs)
        self.outs += [(s, BF16) for s in shapes]
        return slice(at, at + len(shapes))

    def sum(self, arrays, group=0, ways=1):
        rows, cols = arrays[0].shape
        ins, outs = self.take(arrays), self.make([(rows // ways, cols)] * ways)
        number = len(self.numbers)
        self.numbers.append(group)

        def work(numbers, args, made):
            for k, out in enumerate(made[outs]):
                base = (numbers[number] ^ k) * out.shape[0]
                step = 128 if out.shape[0] % 128 == 0 else out.shape[0]
                for r in range(0, out.shape[0], step):
                    at = pl.ds(pl.multiple_of(base + r, 16), step)
                    total = sum(one[at, :].astype(F32) for one in args[ins])
                    out[r : r + step, :] = total.astype(BF16)

        self.work.append(work)
        return outs

    def join(self, arrays, group, blocks=None):
        ways = len(arrays)
        rows, cols = arrays[0].shape
        if blocks is None:
            shapes = [(rows * ways, cols)]
        else:
            shapes = [(blocks[0] * blocks[1], cols), (blocks[0] * blocks[2], cols)]
        ins, outs = self.take(arrays), self.make(shapes)
        number = len(self.numbers)
        self.numbers.append(group)

        def work(numbers, args, made):
            for k, one in enumerate(args[ins]):
                which = numbers[number] ^ k
                if blocks is None:
                    made[outs][0][pl.ds(pl.multiple_of(which * rows, 16), rows), :] = one[...]
                    continue
                count, block, gap = blocks
                for p in range(count // ways):
                    at = p * (block + gap)
                    for out, skip, size in zip(made[outs], (0, block), (block, gap)):
                        to = pl.ds(pl.multiple_of((which * (count // ways) + p) * size, 16), size)
                        out[to, :] = one[at + skip : at + skip + size, :]

        self.work.append(work)
        return outs

    def gaps(self, arrays, group, block, gap):
        rows, cols = arrays[0].shape
        parts = rows // (block + gap)
        ins, outs = self.take(arrays), self.make([(len(arrays) * parts * gap, cols)])
        number = len(self.numbers)
        self.numbers.append(group)

        def work(numbers, args, made):
            for k, one in enumerate(args[ins]):
                which = numbers[number] ^ k
                for p in range(parts):
                    at = p * (block + gap) + block
                    to = pl.ds(pl.multiple_of((which * parts + p) * gap, 16), gap)
                    made[outs][0][to, :] = one[at : at + gap, :]

        self.work.append(work)
        return outs

    def run(self):
        count, extra = len(self.args), len(self.after)

        def kernel(numbers, *refs):
            refs = refs[extra:]
            for work in self.work:
                work(numbers, refs[:count], refs[count:])

        made = call(
            kernel, "s" + "a" * extra + "v" * count, self.outs, vmem=24 << 20
        )(scalars(*self.numbers), *self.after, *self.args)
        return made


def plane_dims():
    bits = [1 << i for i in range((lax.axis_size("dp") - 1).bit_length())]
    groups = [tuple(bits[:1])] + [tuple(bits[i : i + 2]) for i in range(1, len(bits), 2)]
    return [("dp", group) for group in groups]


def swaps(pieces, dim):
    return [pieces[0]] + [xor_swap(pieces[k], dim, k) for k in range(1, len(pieces))]


class Track:
    def __init__(self, arrays, dims, start, blocks=None):
        self.arrays, self.dims, self.start = arrays, dims, start
        self.blocks = blocks
        self.places = [bits_of(*dim) for dim in dims]
        self.queued = self.result = self.gaps = self.away = None

    def queue(self, phase, number):
        count = len(self.dims)
        number -= self.start
        self.queued = None
        if number < 0 or number > 2 * count:
            return
        if number < count:
            ways = 1 << len(self.dims[number][1])
            self.queued = phase.sum(self.arrays, self.places[number], ways), self.dims[number], 1
        elif number == count:
            self.queued = phase.sum(self.arrays), self.dims[-1], 1 << len(self.dims[-1][1])
        elif number < 2 * count:
            at = 2 * count - number
            if self.blocks and at == 1:
                self.gaps = phase.gaps(self.arrays, self.places[at], *self.blocks[1:])
            made = phase.join(self.arrays, self.places[at])
            self.queued = made, self.dims[at - 1], 1 << len(self.dims[at - 1][1])
        else:
            self.queued = phase.join(self.arrays, self.places[0], self.blocks), None, 0

    def send(self, made):
        if self.queued is None:
            return
        outs, dim, copies = self.queued
        if self.gaps is not None and self.away is None:
            self.away = move(made[self.gaps][0], TO_FAR + TO_NEAR)
        if dim is None:
            self.result = made[outs]
        else:
            self.arrays = swaps(made[outs] * copies, dim)


def plane_sums(feed, between, blocks, finish_feed):
    dims = plane_dims()
    tracks = [Track([feed[0], move(feed[1], CORES)], dims, 0)]
    rounds = 2 * len(dims)
    att = local = after = None
    for number in range(rounds + 3):
        order = []
        if number == 1:
            order = [after]
        if number == rounds + 2:
            order = [local()]
        phase = Phase(order)
        for track in tracks:
            track.queue(phase, number)
        if number == 1:
            passed = phase.sum([att[1]])
        if number == rounds + 2:
            passed = phase.sum([tracks[-1].away])
        made = phase.run()
        for track in tracks:
            track.send(made)
        if number == 0:
            att = between(made[0])
            after = att[0]
        if number == 1:
            tracks.append(Track([att[0], move(made[passed][0], CORES)], dims, 2, blocks=blocks))
        if number == rounds + 1:
            local = finish_feed(tracks[0].result[0])
    return *tracks[-1].result, made[passed][0]


def per_device(
    lookback_readings,
    prediction_adjoint,
    variate_tallies,
    lookback_classes,
    brief_lift_table,
    moderate_lift_table,
    distant_lift_table,
    lift_offsets,
    part_entry_arrays,
    part_shrink_lines,
    part_layernorm_scale,
    part_layernorm_offset,
    mixing_offsets,
    expand_offsets,
    shrink_offsets,
    prediction_matrix,
    prediction_offset,
):
    place = lax.axis_index("pipe")
    core, far = place & 1, place // 2
    places = [scalars(core, far, r) for r in range(2)]
    at = places[0]
    entry, shrink = part_entry_arrays[0], part_shrink_lines[0]
    entry_other, shrink_other = move(entry, CORES), move(shrink, CORES)
    tok, adjoint = lookback_readings[0].T, prediction_adjoint[0].T
    tables = (brief_lift_table, moderate_lift_table, distant_lift_table)
    norm = jnp.concatenate([part_layernorm_scale, part_layernorm_offset], 0)

    weights = (entry, entry_other, shrink, shrink_other)
    norms = (norm, move(norm, CORES))
    toks = (tok, move(tok, TO_NEAR))
    layout = (variate_tallies, lookback_classes)
    mixing = mixing_offsets.transpose(1, 0, 2)

    first = []
    arrived = []
    for r in range(2):
        out = first_layer(
            places[r], *layout, weights, adjoint, toks[r], tables, lift_offsets, mixing, expand_offsets,
            shrink_offsets, norms,
        )
        first.append(out[2:])
        if r == 0:
            adjoints = (move(out[1], TO_FAR), adjoint)
        arrived.append(move(out[0], TO_FAR))
    second = []
    returned = []
    predictions = []
    for r in range(2):
        g, prediction, saved = second_layer(
            places[r], *layout, weights, arrived[r], adjoints[r], prediction_matrix.T,
            prediction_offset[None], mixing, expand_offsets, shrink_offsets, norms,
        )
        returned.append(move(g, TO_NEAR))
        predictions.append(prediction)
        second.append(saved)
    shared_rows = max(768, 32 * lax.axis_size("dp"))
    away = second_weights(at, second, shared_rows)

    size = lax.axis_size("dp")
    x0, z0, qkv, o, lse, x1, z1, h, d = first[0]
    g, vec, *feed = first_feed_back(at, weights, returned[0], x1, z1, h, d, norms, arrived[1])
    near_series, *att, shared = first_attention_back(
        places[0], *layout, weights, g, x0, z0, qkv, o, lse, norms, toks[0], tables, vec, g,
        shared_rows, size,
    )
    x0, z0, qkv, o, lse, x1, z1, h, d = first[1]
    g, vec, *feed = first_feed_back(
        at, weights, returned[1], x1, z1, h, d, norms, att[0], (*feed, *away[:2])
    )
    far_series = []

    def between(after):
        series, keep, send = first_attention_back(
            places[1], *layout, weights, g, x0, z0, qkv, o, lse, norms, toks[1], tables, vec, after,
            shared_rows, size, (*att, shared, *away[2:]),
        )
        far_series.append(series)
        return keep, send

    held = {}
    rows = entry.shape[0] * entry.shape[1] // shrink.shape[1] // 2

    def finish_feed(feed):
        held["feed"] = feed
        held["up"] = move(feed[:rows], [(0, 1), (2, 3)])
        held["series"] = move(far_series[0], TO_FAR)
        held["prediction"] = move(predictions[0], TO_NEAR)

        def local():
            held["local"] = local_out(
                at, feed, near_series, held["series"], feed[rows:], held["prediction"], predictions[1]
            )
            return held["local"][2]

        return local

    blocks = (size, att[0].shape[0] // size, shared_rows // 2 // size)
    att_sum, shared_sum, away_part = plane_sums(feed, between, blocks, finish_feed)
    dim = plane_dims()[0]
    att_other = move(att_sum, [(1, 0), (3, 2)])
    shared_other = move(shared_sum, CORES)
    away_parts = swaps([away_part] * (1 << len(dim[1])), dim)
    series_grad, down_grad, prediction = held["local"]
    entry_grad, mark = entry_out(
        at, series_grad, att_sum, att_other, held["feed"][:rows], held["up"], entry.shape
    )
    phase = Phase([mark])
    queued = phase.join(away_parts, bits_of(*dim))
    shared_away = phase.run()[queued][0]
    t0, t1, t2, embb, gain, offset, attb, upb, downb, pw, pb = shared_out(
        at, (shared_sum, shared_other, shared_away, move(shared_away, CORES)), tables,
        prediction_matrix.shape[1], entry.shape[1],
    )
    return (
        prediction.T[None],
        series_grad.T[None],
        t0,
        t1,
        t2,
        embb,
        entry_grad[None],
        down_grad[None],
        gain,
        offset,
        attb.transpose(1, 0, 2),
        upb,
        downb,
        pw.T,
        pb[0],
    )


def solution(mesh):
    placed = (
        P("pipe", "dp", None),
        P("pipe", "dp", None),
        P(None, "dp", None),
        P(None, "dp", None),
        P(),
        P(),
        P(),
        P(),
        P("pipe", None, None),
        P("pipe", None, None),
        P("pipe", None),
        P("pipe", None),
        P(),
        P(),
        P(),
        P(),
        P(),
    )
    return jax.shard_map(
        per_device,
        mesh=mesh,
        in_specs=placed,
        out_specs=(
            P("pipe", "dp", None),
            P("pipe", "dp", None),
            P(),
            P(),
            P(),
            P(),
            P("pipe", None, None),
            P("pipe", None, None),
            P("pipe", None),
            P("pipe", None),
            P(),
            P(),
            P(),
            P(),
            P(),
        ),
        check_vma=False,
    )
```

```python
import functools

import jax
import jax.numpy as jnp
from jax import lax
from jax.experimental import pallas as pl
from jax.experimental.pallas import tpu as pltpu
from jax.sharding import PartitionSpec as P

HEADS = 8
HEAD_DIM = 64
F32 = jnp.float32
BF16 = jnp.bfloat16
VECTOR_ROW = 624
VECTORS = 16


def nn(a, b):
    return lax.dot_general(a, b, (((1,), (0,)), ((), ())), preferred_element_type=F32)


def nt(a, b):
    return lax.dot_general(a, b, (((1,), (1,)), ((), ())), preferred_element_type=F32)


def tn(a, b):
    return lax.dot_general(a, b, (((0,), (0,)), ((), ())), preferred_element_type=F32)


def column_sum(a):
    return jnp.sum(a.astype(F32), 0, keepdims=True)


def normalise(z):
    centre = z - jnp.mean(z, -1, keepdims=True)
    inverse = lax.rsqrt(jnp.mean(centre * centre, -1, keepdims=True) + 1e-05)
    return centre * inverse, inverse


def norm_back(upstream, z, gain):
    normed, inverse = normalise(z)
    gain_grad = jnp.sum(upstream * normed, 0, keepdims=True)
    offset_grad = jnp.sum(upstream, 0, keepdims=True)
    scaled = upstream * gain
    back = inverse * (
        scaled
        - jnp.mean(scaled, -1, keepdims=True)
        - normed * jnp.mean(scaled * normed, -1, keepdims=True)
    )
    return back, gain_grad, offset_grad


def gelu_both(u):
    bell = jnp.exp(u * u * -0.5)
    t = 1.0 / (1.0 + (0.3275911 * 0.5**0.5) * jnp.abs(u))
    poly = t * (
        0.127414796
        + t * (-0.142248368 + t * (0.7107068705 + t * (-0.7265760135 + t * 0.5307027145)))
    )
    half = poly * bell
    phi = jnp.where(u >= 0, 1.0 - half, half)
    return u * phi, phi + u * bell * 0.3989422804014327


def same_window_bias(seg_col, seg_row):
    return jnp.where(seg_col == seg_row, 0.0, -1e30).astype(F32)


class Choice:
    def __init__(self, index, sources, place, sem):
        self.index = index
        self.copies = [pltpu.make_async_copy(s, place, sem) for s in sources]

    def start(self):
        for k, copy in enumerate(self.copies):
            pl.when(self.index == k)(copy.start)

    def wait(self):
        for k, copy in enumerate(self.copies):
            pl.when(self.index == k)(copy.wait)


def weight_loads(core, entry, other, shrink, shrink_other, att_ref, up_ref, down_ref, sem):
    loads = []
    if att_ref is not None:
        loads.append(Choice(core, (entry, other), att_ref, sem.at[0]))
    if up_ref is not None:
        loads.append(Choice(1 - core, (entry, other), up_ref, sem.at[1]))
        half = down_ref.shape[0] // 2
        low, high = down_ref.at[pl.ds(0, half)], down_ref.at[pl.ds(half, half)]
        loads.append(Choice(core, (shrink, shrink_other), low, sem.at[2]))
        loads.append(Choice(1 - core, (shrink, shrink_other), high, sem.at[3]))
    for one in loads:
        one.start()
    return loads


def chosen_norms(core, own_ref, other_ref):
    own, other = own_ref[...], other_ref[...]
    first = core == 0
    return jnp.where(first, own, other), jnp.where(first, other, own)


class Moves:
    def __init__(self, sem):
        self.sem = sem
        self.started = []

    def start(self, source, target):
        copy = pltpu.make_async_copy(source, target, self.sem.at[len(self.started)])
        copy.start()
        self.started.append(copy)
        return copy


class Small:
    def __init__(self, pairs, sem):
        self.copies = [pltpu.make_async_copy(s, t, sem.at[i]) for i, (s, t) in enumerate(pairs)]

    def start(self):
        for copy in self.copies:
            copy.start()

    def wait(self):
        for copy in self.copies:
            copy.wait()


def row_windows(tallies, classes, micro, count):
    windows = 4
    ends, total = [], 0
    for w in range(windows - 1):
        total = total + tallies[micro, 0, w]
        ends.append(total)
    out = []
    for shape, axis in (((count, 1), 0), ((1, count), 1)):
        position = lax.broadcasted_iota(jnp.int32, shape, axis)
        window = sum((position >= end).astype(jnp.int32) for end in ends)
        group = jnp.full(shape, classes[micro, 0, 0], jnp.int32)
        for w in range(1, windows):
            group = jnp.where(window == w, classes[micro, 0, w], group)
        out.append((window, group))
    return out


def attention_core(x, w_ref, biases, norm, mask_ref, qkv_ref, o_ref, lse_ref, z_ref):
    width = x.shape[1]
    qkv_ref[:, :width] = ((nn(x, w_ref[:, :width]) + biases[0]) * HEAD_DIM**-0.5).astype(BF16)
    qkv_ref[:, width : 2 * width] = nn(x, w_ref[:, width : 2 * width]).astype(BF16)
    qkv_ref[:, 2 * width : 3 * width] = (
        nn(x, w_ref[:, 2 * width : 3 * width]) + biases[1]
    ).astype(BF16)
    pair = 2 * HEAD_DIM
    low = lax.broadcasted_iota(jnp.int32, (1, pair), 1) < HEAD_DIM
    for p in range(HEADS // 2):
        q2 = qkv_ref[:, p * pair : (p + 1) * pair]
        k2 = qkv_ref[:, width + p * pair : width + (p + 1) * pair]
        v2 = qkv_ref[:, 2 * width + p * pair : 2 * width + (p + 1) * pair]
        v2t = v2.T
        zero = jnp.zeros_like(k2)
        both = nt(jnp.concatenate([jnp.where(low, k2, zero), jnp.where(low, zero, k2)], 0), q2)
        parts = []
        count = k2.shape[0]
        for h in range(2):
            s = both[h * count : (h + 1) * count, :] + mask_ref[...]
            top = jnp.max(s, 0, keepdims=True)
            e = jnp.exp(s - top)
            total = jnp.sum(e, 0, keepdims=True)
            lse_ref[2 * p + h : 2 * p + h + 1, :] = top + jnp.log(total)
            ot = nn(v2t[h * HEAD_DIM : (h + 1) * HEAD_DIM, :], e.astype(BF16))
            parts.append(ot * (1.0 / total))
        o_ref[:, p * pair : (p + 1) * pair] = jnp.concatenate(parts, 0).T.astype(BF16)
    z = x.astype(F32) + (nn(o_ref[...], w_ref[:, 3 * width :]) + biases[2])
    z_ref[...] = z
    return (normalise(z)[0] * norm[0:1, :] + norm[1:2, :]).astype(BF16)


def feed_core(x, up_ref, down_ref, upb, downb, norm, h_ref, d_ref, z_ref, done=None, block=512):
    total = None
    for c in range(0, up_ref.shape[1], block):
        u = nn(x, up_ref[:, c : c + block]) + upb[:, c : c + block]
        h, d = gelu_both(u)
        hb = h.astype(BF16)
        h_ref[:, c : c + block] = hb
        d_ref[:, c : c + block] = d.astype(BF16)
        if done is not None:
            done(slice(c, c + block))
        part = nn(hb, down_ref[c : c + block, :])
        total = part if total is None else total + part
    z = x.astype(F32) + (total + downb)
    z_ref[...] = z
    return (normalise(z)[0] * norm[0:1, :] + norm[1:2, :]).astype(BF16)


def feed_back_chain(upstream, z_ref, d_ref, up_ref, down_ref, norm, gu_ref, gf_ref, vec_ref, gx_acc,
    ready=None, done=None,
):
    back, gain_grad, offset_grad = norm_back(upstream, z_ref[...], norm[0:1, :])
    gf_ref[...] = back.astype(BF16)
    gx_acc[...] = back
    width = back.shape[1]
    if ready is not None:
        ready()
    for b in range(up_ref.shape[1] // width):
        cols = slice(b * width, (b + 1) * width)
        gu = (nt(gf_ref[...], down_ref[cols, :]) * d_ref[:, cols].astype(F32)).astype(BF16)
        gu_ref[:, cols] = gu
        if done is not None:
            done(cols)
        vec_ref[7 + b : 8 + b, :] = column_sum(gu)
        gx_acc[...] += nt(gu, up_ref[:, cols])
    vec_ref[11:12, :] = column_sum(gf_ref[...])
    vec_ref[14:15, :] = gain_grad
    vec_ref[15:16, :] = offset_grad


def attention_back_chain(
    upstream, z_ref, qkv_ref, o_ref, lse_ref, w_ref, norm, mask_ref,
    gqkv_ref, ga_ref, go_ref, vec_ref, gx_acc, ready=None,
):
    back, gain_grad, offset_grad = norm_back(upstream, z_ref[...], norm[0:1, :])
    width = back.shape[1]
    ga_ref[...] = back.astype(BF16)
    gx_acc[...] = back
    vec_ref[6:7, :] = column_sum(ga_ref[...])
    vec_ref[12:13, :] = gain_grad
    vec_ref[13:14, :] = offset_grad
    if ready is not None:
        ready()
    go_ref[...] = nt(ga_ref[...], w_ref[:, 3 * width :]).astype(BF16)
    pair = 2 * HEAD_DIM
    low = lax.broadcasted_iota(jnp.int32, (1, pair), 1) < HEAD_DIM
    for p in range(HEADS // 2):
        q2 = qkv_ref[:, p * pair : (p + 1) * pair]
        k2 = qkv_ref[:, width + p * pair : width + (p + 1) * pair]
        v2 = qkv_ref[:, 2 * width + p * pair : 2 * width + (p + 1) * pair]
        go2 = go_ref[:, p * pair : (p + 1) * pair]
        o2 = o_ref[:, p * pair : (p + 1) * pair]
        k2t = k2.T
        prod = (go2.astype(F32) * o2.astype(F32)).T
        zero = jnp.zeros_like(k2)

        def split(a):
            return jnp.concatenate([jnp.where(low, a, zero), jnp.where(low, zero, a)], 0)

        both = nt(split(k2), q2)
        both_gp = nt(split(v2), go2)
        count = k2.shape[0]
        gq, all_w, all_g = [], [], []
        for h in range(2):
            lanes = slice(h * HEAD_DIM, (h + 1) * HEAD_DIM)
            rows = slice(h * count, (h + 1) * count)
            centred = jnp.sum(prod[lanes, :], 0, keepdims=True)
            weights = jnp.exp(both[rows, :] + mask_ref[...] - lse_ref[2 * p + h : 2 * p + h + 1, :])
            gs = (weights * (both_gp[rows, :] - centred)).astype(BF16)
            all_w.append(weights.astype(BF16))
            all_g.append(gs)
            gq.append(nn(k2t[lanes, :], gs) * HEAD_DIM**-0.5)
        gv = nn(jnp.concatenate(all_w, 1), split(go2))
        gk = nn(jnp.concatenate(all_g, 1), split(q2))
        cols = slice(p * pair, (p + 1) * pair)
        gqkv_ref[:, cols] = jnp.concatenate(gq, 0).T.astype(BF16)
        gqkv_ref[:, width + p * pair : width + (p + 1) * pair] = gk.astype(BF16)
        gqkv_ref[:, 2 * width + p * pair : 2 * width + (p + 1) * pair] = gv.astype(BF16)
    gx_acc[...] += nt(gqkv_ref[...], w_ref[:, : 3 * width])
    vec_ref[4:5, :] = column_sum(gqkv_ref[:, :width])
    vec_ref[5:6, :] = column_sum(gqkv_ref[:, 2 * width :])


def row_halves(core, value):
    half = value.shape[0] // 2
    low, high = value[:half, :], value[half:, :]
    return jnp.where(core == 0, low, high), jnp.where(core == 0, high, low)


def feed_weight_grads(core, rows_of, prior, outs, xt_ref):
    width = rows_of[0][0].shape[1]
    half = width // 2
    blocks = rows_of[0][1].shape[1] // width
    for i, (x, _, _, _) in enumerate(rows_of):
        xt_ref[i] = x[...].T

    def put(index, at, value):
        if prior is not None:
            value = value + prior[index][at, :].astype(F32)
        outs[index][at, :] = value.astype(BF16)

    for j in range(blocks):
        b = lax.rem(j + core * (blocks // 2), blocks)
        cols = pl.ds(pl.multiple_of(b * width, width), width)
        at = blocks * half + (j % (blocks // 2)) * width
        value = sum(tn(h[:, cols], gf[...]) for _, h, _, gf in rows_of)
        put(j // (blocks // 2), slice(at, at + width), value)
        at = pl.ds(pl.multiple_of(b * half, half), half)
        value = sum(nn(xt_ref[i], gu[:, cols]) for i, (_, _, gu, _) in enumerate(rows_of))
        for index, part in enumerate(row_halves(core, value)):
            put(index, at, part)


def store_mixed(out, row, value, block, gap):
    for k in range(0, value.shape[0], block):
        at = (row + k) // block * (block + gap)
        out[at : at + block, :] = value[k : k + block, :]


def attention_weight_grads(core, rows_of, prior, outs, xt_ref, ot_ref, block=None, gap=0):
    width = rows_of[0][0].shape[1]
    half = width // 2

    def put(index, b, value):
        at = slice(b * half, (b + 1) * half)
        if prior is not None:
            value = value + prior[index][at, :].astype(F32)
        store_mixed(outs[index], b * half, value.astype(BF16), block or half, gap)

    for i, (_, _, o, _) in enumerate(rows_of):
        ot_ref[i] = o[...].T
    value = sum(nn(ot_ref[i], ga[...]) for i, (_, _, _, ga) in enumerate(rows_of))
    for index, part in enumerate(row_halves(core, value)):
        put(index, 3, part)
    for i, (x, _, _, _) in enumerate(rows_of):
        xt_ref[i] = x[...].T
    for b in range(3):
        value = sum(
            nn(xt_ref[i], gqkv[:, b * width : (b + 1) * width]) for i, (_, gqkv, _, _) in enumerate(rows_of)
        )
        for index, part in enumerate(row_halves(core, value)):
            put(index, b, part)


def embed(tok, group_col, group_row, tables, off_ref):
    look = tok.shape[0]
    total = None
    for g, t_ref in enumerate(tables):
        skip = look - t_ref.shape[0]
        masked = jnp.where(group_row == g, tok[skip:, :], jnp.zeros((1, 1), BF16))
        part = tn(masked, t_ref[...]) + jnp.where(group_col == g, off_ref[g : g + 1, :], 0.0)
        total = part if total is None else total + part
    return total.astype(BF16)


def first_layer_kernel(
    small, at, tallies, classes, entry, other, shrink, shrink_other,
    adj_in, tok_ref, t0_ref, t1_ref, t2_ref, off_ref, bias_ref, upb_ref, downb_ref, norm_ref, norm_other_ref,
    x2_ref, adj_out, x0_out, z0_out, qkv_out, o_out, lse_out, x1_out, z1_out, h_out, d_out,
    x0_ref, z0_ref, qkv_ref, o_ref, lse_ref, x1_ref, z1_ref, h_ref, d_ref,
    mask_ref, att_ref, up_ref, down_ref, sem, out_sem,
):
    @pl.when(at[1] == 0)
    def _():
        core = at[0]
        small.start()
        loads = weight_loads(
            core, entry, other, shrink, shrink_other, att_ref, up_ref, down_ref, sem
        )
        out = Moves(out_sem)
        (wc, gc), (wr, gr) = row_windows(tallies, classes, core + 2 * at[2], x0_ref.shape[0])
        mask_ref[...] = same_window_bias(wc, wr)
        small.wait()
        x0_ref[...] = embed(tok_ref[...], gc, gr, (t0_ref, t1_ref, t2_ref), off_ref)
        out.start(x0_ref, x0_out)
        out.start(adj_in, adj_out)
        norm_att, norm_feed = chosen_norms(core, norm_ref, norm_other_ref)
        loads[0].wait()
        x1_ref[...] = attention_core(
            x0_ref[...], att_ref, [bias_ref[i, 0:1, :] for i in range(3)], norm_att, mask_ref,
            qkv_ref, o_ref, lse_ref, z0_ref,
        )
        for source, target in (
            (qkv_ref, qkv_out), (o_ref, o_out), (lse_ref, lse_out), (z0_ref, z0_out), (x1_ref, x1_out)
        ):
            out.start(source, target)
        for one in loads[1:]:
            one.wait()

        def done(cols):
            out.start(h_ref.at[:, cols], h_out.at[:, cols])
            out.start(d_ref.at[:, cols], d_out.at[:, cols])

        x2_ref[...] = feed_core(
            x1_ref[...], up_ref, down_ref, upb_ref[0:1, :], downb_ref[0:1, :], norm_feed,
            h_ref, d_ref, z1_ref, done,
        )
        out.start(z1_ref, z1_out)
        for copy in out.started:
            copy.wait()


def second_layer_kernel(
    small, at, tallies, classes, entry, other, shrink, shrink_other,
    x2_ref, adj_ref, pm_ref, pb_ref, bias_ref, upb_ref, downb_ref, norm_ref, norm_other_ref,
    g_ref, pred_ref, x2_out, gqkv_out, o_out, ga_out, x3_out, gu_out, h_out, gf_out, vec_out, gpm_out,
    gqkv_ref, o_ref, ga_ref, x3_ref, gu_ref, h_ref, gf_ref, vec_ref, gpm_ref,
    mask_ref, att_ref, up_ref, down_ref, qkv_ref, lse_ref, z2_ref, z3_ref, d_ref, gx_acc, go_ref,
    sem, out_sem,
):
    @pl.when(at[1] == 1)
    def _():
        core = at[0]
        small.start()
        loads = weight_loads(
            core, entry, other, shrink, shrink_other, att_ref, up_ref, down_ref, sem
        )
        out = Moves(out_sem)
        out.start(x2_ref, x2_out)
        (wc, _), (wr, _) = row_windows(tallies, classes, core + 2 * at[2], x2_ref.shape[0])
        mask_ref[...] = same_window_bias(wc, wr)
        small.wait()
        norm_att, norm_feed = chosen_norms(core, norm_ref, norm_other_ref)
        loads[0].wait()
        x3_ref[...] = attention_core(
            x2_ref[...], att_ref, [bias_ref[i, 1:2, :] for i in range(3)], norm_att, mask_ref,
            qkv_ref, o_ref, lse_ref, z2_ref,
        )
        out.start(o_ref, o_out)
        out.start(x3_ref, x3_out)
        for one in loads[1:]:
            one.wait()
        y = feed_core(
            x3_ref[...], up_ref, down_ref, upb_ref[1:2, :], downb_ref[1:2, :], norm_feed,
            h_ref, d_ref, z3_ref, lambda cols: out.start(h_ref.at[:, cols], h_out.at[:, cols]),
        )
        pm, adj = pm_ref[...], adj_ref[...]
        pred_ref[...] = (nt(pm, y) + pb_ref[...].T).astype(BF16)
        gpm_ref[...] = nn(adj, y)
        out.start(gpm_ref, gpm_out)
        width = y.shape[1]
        horizon = adj.shape[0]
        gpb = jnp.sum(adj.astype(F32), 1, keepdims=True).T
        vec_ref[0:1, :] = jnp.concatenate([gpb, jnp.zeros((1, width - horizon), F32)], 1)
        vec_ref[1:4, :] = jnp.zeros((3, width), F32)
        feed_back_chain(
            tn(adj, pm), z3_ref, d_ref, up_ref, down_ref, norm_feed, gu_ref, gf_ref, vec_ref, gx_acc, None,
            lambda cols: out.start(gu_ref.at[:, cols], gu_out.at[:, cols]),
        )
        out.start(gf_ref, gf_out)
        attention_back_chain(
            gx_acc[...].astype(BF16).astype(F32), z2_ref, qkv_ref, o_ref, lse_ref, att_ref, norm_att,
            mask_ref, gqkv_ref, ga_ref, go_ref, vec_ref, gx_acc,
        )
        g_ref[...] = gx_acc[...].astype(BF16)
        out.start(ga_ref, ga_out)
        out.start(gqkv_ref, gqkv_out)
        out.start(vec_ref, vec_out)
        for copy in out.started:
            copy.wait()


def second_weights_kernel(at, *refs):
    sources, refs = refs[:20], refs[20:]
    outs, refs = refs[:5], refs[5:]
    held, refs = refs[:20], refs[20:]
    made, (xt_ref, xt2_ref, ot_ref, sem, out_sem) = refs[:5], refs[5:]

    @pl.when(at[1] == 1)
    def _():
        core = at[0]
        loads = Moves(sem)
        for i in range(10):
            for r in range(2):
                loads.start(sources[10 * r + i], held[10 * r + i])
        out = Moves(out_sem)
        rows = held[:10], held[10:]
        for copy in loads.started[:8]:
            copy.wait()
        feed_weight_grads(core, [r[:4] for r in rows], None, made[:2], xt_ref)
        for i in range(2):
            out.start(made[i], outs[i])
        for copy in loads.started[8:]:
            copy.wait()
        attention_weight_grads(core, [r[4:8] for r in rows], None, made[2:4], xt2_ref, ot_ref)
        horizon = rows[0][9].shape[0]
        shared_ref = made[4]
        shared_ref[...] = jnp.zeros(shared_ref.shape, F32)
        shared_ref[:horizon, :] = rows[0][9][...] + rows[1][9][...]
        shared_ref[VECTOR_ROW : VECTOR_ROW + VECTORS, :] = rows[0][8][...] + rows[1][8][...]
        for i in range(2, 5):
            out.start(made[i], outs[i])
        for copy in out.started:
            copy.wait()


def first_feed_back_kernel(second, small, at, entry, other, shrink, shrink_other, *refs):
    z1_in, d_in, x1_in, h_in = refs[:4]
    refs = refs[4:]
    prior, far_in = (refs[:2], refs[2:4]) if second else (None, None)
    refs = refs[4:] if second else refs
    g_ref, norm_ref, norm_other_ref, _, gx_ref, vec_ref = refs[:6]
    outs, refs = refs[6:8], refs[8:]
    if second:
        held, refs = refs[:2], refs[2:]
    else:
        made, refs = refs[:2], refs[2:]
    z1_ref, d_ref, x1_ref, h_ref, up_ref, down_ref, gu_ref, gf_ref, gx_acc, xt_ref, sem, in_sem = refs

    @pl.when(at[1] == 0)
    def _():
        core = at[0]
        loads = Moves(in_sem)
        small.start()
        loads.start(z1_in, z1_ref)
        weights = weight_loads(core, entry, other, shrink, shrink_other, None, up_ref, down_ref, sem)
        loads.start(d_in, d_ref)
        loads.start(x1_in, x1_ref)
        loads.start(h_in, h_ref)
        if second:
            for source, target in zip(prior, held):
                loads.start(source, target)
        small.wait()
        _, norm_feed = chosen_norms(core, norm_ref, norm_other_ref)
        vec_ref[...] = jnp.zeros(vec_ref.shape, F32)
        loads.started[0].wait()

        def ready():
            loads.started[1].wait()
            for one in weights:
                one.wait()

        feed_back_chain(
            g_ref[...].astype(F32), z1_ref, d_ref, up_ref, down_ref, norm_feed,
            gu_ref, gf_ref, vec_ref, gx_acc, ready,
        )
        gx_ref[...] = gx_acc[...].astype(BF16)
        for copy in loads.started[2:]:
            copy.wait()
        feed_weight_grads(
            core, [(x1_ref, h_ref, gu_ref, gf_ref)], held if second else None,
            outs if second else made, xt_ref,
        )
        if not second:
            out = Moves(in_sem)
            for source, target in zip(made, outs):
                out.start(source, target)
            for copy in out.started:
                copy.wait()

    if second:
        @pl.when(at[1] == 1)
        def _():
            loads = Moves(in_sem)
            for source, target in zip(far_in, outs):
                loads.start(source, target)
            for copy in loads.started:
                copy.wait()


def first_attention_back_kernel(second, size, small, at, tallies, classes, entry, other, *refs):
    z0_in, o_in, qkv_in, lse_in, x0_in, tok_in = refs[:6]
    refs = refs[6:]
    prior, far_in = (refs[:3], refs[3:6]) if second else (None, None)
    refs = refs[6:] if second else refs
    g_ref, norm_ref, norm_other_ref, t0_ref, t1_ref, t2_ref, vec_in = refs[:7]
    refs = refs[8:]
    if second:
        (series_ref, keep_ref, send_ref), refs = refs[:3], refs[3:]
        held, refs = refs[:3], refs[3:]
        made = (keep_ref, send_ref)
    else:
        outs, refs = refs[:4], refs[4:]
        (series_ref, *made), refs = refs[:3], refs[3:]
    (z0_ref, o_ref, qkv_ref, lse_ref, x0_ref, tok_ref, mask_ref, att_ref, gqkv_ref, ga_ref, go_ref,
     gx_acc, xt_ref, ot_ref, vec_ref, acc_ref, sem, in_sem) = refs

    if second:
        half = acc_ref.shape[0] // 2
        gap = half // size
        block = keep_ref.shape[0] // size - gap
    else:
        block, gap = None, 0

    def split(total):
        total_ref = held[2]
        total_ref[...] = total
        for index, out in enumerate((keep_ref, send_ref)):
            first = (at[0] if index == 0 else 1 - at[0]) * half
            for p in range(size):
                rows = pl.ds(pl.multiple_of(first + p * gap, 16), gap)
                to = p * (block + gap) + block
                out[to : to + gap, :] = total_ref[rows, :].astype(BF16)

    @pl.when(at[1] == 0)
    def _():
        core = at[0]
        loads = Moves(in_sem)
        small.start()
        loads.start(z0_in, z0_ref)
        weights = weight_loads(core, entry, other, None, None, att_ref, None, None, sem)
        loads.start(o_in, o_ref)
        loads.start(qkv_in, qkv_ref)
        loads.start(lse_in, lse_ref)
        loads.start(x0_in, x0_ref)
        loads.start(tok_in, tok_ref)
        if second:
            for source, target in zip(prior, held):
                loads.start(source, target)
        small.wait()
        norm_att, _ = chosen_norms(core, norm_ref, norm_other_ref)
        (wc, _), (wr, gr) = row_windows(tallies, classes, core + 2 * at[2], x0_ref.shape[0])
        mask_ref[...] = same_window_bias(wc, wr)
        vec_ref[...] = vec_in[...]
        loads.started[0].wait()

        def ready():
            weights[0].wait()
            for copy in loads.started[1:4]:
                copy.wait()

        attention_back_chain(
            g_ref[...].astype(F32), z0_ref, qkv_ref, o_ref, lse_ref, att_ref, norm_att,
            mask_ref, gqkv_ref, ga_ref, go_ref, vec_ref, gx_acc, ready,
        )
        for copy in loads.started[4:]:
            copy.wait()
        attention_weight_grads(
            core, [(x0_ref, gqkv_ref, o_ref, ga_ref)], held[:2] if second else None,
            made, xt_ref, ot_ref, block, gap,
        )
        g = gx_acc[...].astype(BF16)
        look = tok_ref.shape[0]
        at_row = 0
        for i, t_ref in enumerate((t0_ref, t1_ref, t2_ref)):
            skip = look - t_ref.shape[0]
            chosen = gr == i
            part = jnp.where(chosen, nt(t_ref[...], g), 0.0)
            if i == 0:
                gx_s = [part]
            else:
                gx_s.append(part)
            masked = jnp.where(chosen, tok_ref[skip:, :], jnp.zeros((1, 1), BF16))
            acc_ref[at_row : at_row + look - skip, :] = nn(masked, g)
            at_row += look - skip
        short, mid, long = gx_s
        a, b = long.shape[0] - short.shape[0], long.shape[0] - mid.shape[0]
        series_ref[:b, :] = long[:b, :].astype(series_ref.dtype)
        series_ref[b:a, :] = (long[b:a, :] + mid[: a - b, :]).astype(series_ref.dtype)
        series_ref[a:, :] = (long[a:, :] + mid[a - b :, :] + short).astype(series_ref.dtype)
        groups = lax.broadcasted_iota(jnp.int32, (8, gr.shape[1]), 0)
        vec_ref[1:4, :] = nn((groups == gr).astype(BF16), g)[0:3, :]
        acc_ref[VECTOR_ROW : VECTOR_ROW + VECTORS, :] = vec_ref[...]
        rest = VECTOR_ROW + VECTORS
        acc_ref[rest:, :] = jnp.zeros((acc_ref.shape[0] - rest, acc_ref.shape[1]), F32)
        if second:
            split(acc_ref[...] + held[2][...])
        else:
            out = Moves(in_sem)
            for source, target in zip((series_ref, *made, acc_ref), outs):
                out.start(source, target)
            for copy in out.started:
                copy.wait()

    if second:
        @pl.when(at[1] == 1)
        def _():
            loads = Moves(in_sem)
            for source, target in zip(far_in, (held[0], held[1], acc_ref)):
                loads.start(source, target)
            for copy in loads.started:
                copy.wait()
            for source, target in zip(held, (keep_ref, send_ref)):
                store_mixed(target, 0, source[...], block, gap)
            split(acc_ref[...])


def shared_out_kernel(
    at, _, mine_ref, other_ref, mine_away_ref, other_away_ref,
    t0_ref, t1_ref, t2_ref, embb_ref, gain_ref, offset_ref, att_ref, up_ref, down_ref, pw_ref, pb_ref,
    all_ref,
):
    core, far = at[0], at[1]
    half = mine_ref.shape[0]
    for plane, pair in ((far, (mine_ref, other_ref)), (1 - far, (mine_away_ref, other_away_ref))):
        for who, source in ((core, pair[0]), (1 - core, pair[1])):
            all_ref[plane, pl.ds(pl.multiple_of(who * half, 16), half), :] = source[...].astype(F32)
    row = 0
    for out in (t0_ref, t1_ref, t2_ref):
        out[...] = all_ref[0, row : row + out.shape[0], :]
        row += out.shape[0]
    pw_ref[...] = all_ref[1, : pw_ref.shape[0], :]
    v = VECTOR_ROW
    width = all_ref.shape[2]
    pb_ref[...] = all_ref[1, v : v + 1, : pb_ref.shape[1]]
    embb_ref[...] = all_ref[0, v + 1 : v + 4, :]
    for l in range(2):
        for i in range(3):
            att_ref[i, l : l + 1, :] = all_ref[l, v + 4 + i : v + 5 + i, :]
        for b in range(4):
            up_ref[l : l + 1, b * width : (b + 1) * width] = all_ref[l, v + 7 + b : v + 8 + b, :]
        down_ref[l : l + 1, :] = all_ref[l, v + 11 : v + 12, :]
    gain_ref[...] = all_ref[far, pl.ds(v + 12 + 2 * core, 1), :]
    offset_ref[...] = all_ref[far, pl.ds(v + 13 + 2 * core, 1), :]


def entry_out_kernel(at, _, att_ref, att_other_ref, up_ref, up_other_ref, out_ref, mark_ref):
    rows = out_ref.shape[0] // 2
    width = att_ref.shape[1]
    mark_ref[...] = jnp.zeros(mark_ref.shape, F32)

    def write(low, high):
        for b in range(out_ref.shape[1] // width):
            cols = slice(b * width, (b + 1) * width)
            out_ref[:rows, cols] = low[b * rows : (b + 1) * rows, :].astype(F32)
            out_ref[rows:, cols] = high[b * rows : (b + 1) * rows, :].astype(F32)

    pl.when(at[0] == 0)(lambda: write(att_ref, att_other_ref))
    pl.when(at[0] == 1)(lambda: write(up_other_ref, up_ref))


def series_out_kernel(at, _, near_ref, far_ref, down_ref, pred_near_ref, pred_far_ref, out_ref, down_out, pred_out):
    down_out[...] = down_ref[...].astype(F32)

    @pl.when(at[1] == 0)
    def _():
        out_ref[...] = near_ref[...]
        pred_out[...] = pred_near_ref[...]

    @pl.when(at[1] == 1)
    def _():
        out_ref[...] = far_ref[...].astype(F32)
        pred_out[...] = pred_far_ref[...]


def call(kernel, kinds, outs, scratch=(), out_kinds=None, vmem=60 << 20, flops=0, nbytes=0):
    spaces = {
        "s": pl.BlockSpec(memory_space=pltpu.SMEM),
        "a": pl.BlockSpec(memory_space=pltpu.HBM),
        "l": pl.BlockSpec(memory_space=pltpu.HBM),
        "v": pl.BlockSpec(memory_space=pltpu.VMEM),
    }

    def run(*args):
        assert len(args) == len(kinds)
        loaded = [i for i, k in enumerate(kinds) if k == "l"]

        def body(*refs):
            ins = list(refs[: len(kinds)])
            middle, held, sem = refs[len(kinds) : -1 - len(loaded)], refs[-1 - len(loaded) : -1], refs[-1]
            small = Small([(ins[i], place) for i, place in zip(loaded, held)], sem)
            for i, place in zip(loaded, held):
                ins[i] = place
            kernel(small, *ins, *middle)

        own = [pltpu.VMEM(args[i].shape, args[i].dtype) for i in loaded] + [sems(len(loaded))]
        return pl.pallas_call(
            body if loaded else kernel,
            out_shape=[jax.ShapeDtypeStruct(s, d) for s, d in outs],
            in_specs=[spaces[k] for k in kinds],
            out_specs=[spaces[k] for k in out_kinds or "v" * len(outs)],
            scratch_shapes=[s if not isinstance(s, tuple) else pltpu.VMEM(*s) for s in scratch]
            + (own if loaded else []),
            compiler_params=pltpu.CompilerParams(vmem_limit_bytes=vmem),
            cost_estimate=pl.CostEstimate(flops=flops, bytes_accessed=nbytes, transcendentals=0),
        )(*args)

    return run


def scalars(*values):
    return jnp.stack([jnp.asarray(v, jnp.int32) for v in values])


def sems(count):
    return pltpu.SemaphoreType.DMA((count,))


def first_layer(at, tallies, classes, weights, adj, tok, tables, off, bias, upb, downb, norms):
    n, d, ff = tok.shape[1], off.shape[1], upb.shape[1]
    saves = [
        ((n, d), BF16), ((n, d), F32), ((n, 3 * d), BF16), ((n, d), BF16), ((HEADS, n), F32),
        ((n, d), BF16), ((n, d), F32), ((n, ff), BF16), ((n, ff), BF16),
    ]
    return call(
        first_layer_kernel,
        "sssaaaaa" + "l" * 10,
        [((n, d), BF16), (adj.shape, BF16)] + saves,
        saves
        + [((n, n), F32), ((d, ff), BF16), ((d, ff), BF16), ((ff, d), BF16), sems(4), sems(8 + 2 * ff // d)],
        "v" + "a" * 10,
        flops=10_000_000_000,
    )(at, tallies, classes, *weights, adj, tok, *tables, off, bias, upb, downb, *norms)


def second_layer(at, tallies, classes, weights, x2, adj, pm, pb, bias, upb, downb, norms):
    n, d = x2.shape
    ff, out = upb.shape[1], pm.shape[0]
    saves = [
        ((n, 3 * d), BF16), ((n, d), BF16), ((n, d), BF16), ((n, d), BF16), ((n, ff), BF16),
        ((n, ff), BF16), ((n, d), BF16), ((VECTORS, d), F32), ((out, d), F32),
    ]
    g, pred, x2, gqkv, o, ga, x3, gu, h, gf, vec, gpm = call(
        second_layer_kernel,
        "sssaaaav" + "l" * 8,
        [((n, d), BF16), ((out, n), BF16), ((n, d), BF16)] + saves,
        saves
        + [
            ((n, n), F32), ((d, ff), BF16), ((d, ff), BF16), ((ff, d), BF16), ((n, 3 * d), BF16),
            ((HEADS, n), F32), ((n, d), F32), ((n, d), F32), ((n, ff), BF16), ((n, d), F32),
            ((n, d), BF16), sems(4), sems(8 + 2 * ff // d),
        ],
        "vv" + "a" * 10,
        flops=16_000_000_000,
    )(at, tallies, classes, *weights, x2, adj, pm, pb, bias, upb, downb, *norms)
    return g, pred, (x3, h, gu, gf, x2, gqkv, o, ga, vec, gpm)


def share_shapes(d, ff):
    return [((ff // d * (d // 2) + ff // 2, d), BF16)] * 2, [((2 * d, d), BF16)] * 2


def second_weights(at, rows, shared_rows):
    n, d = rows[0][0].shape
    ff = rows[0][1].shape[1]
    feed, att = share_shapes(d, ff)
    outs = feed + att + [((shared_rows, d), F32)]
    return call(
        second_weights_kernel,
        "s" + "a" * 20,
        outs,
        [(a.shape, a.dtype) for a in (*rows[0], *rows[1])]
        + outs
        + [((2, d, n), BF16)] * 3
        + [sems(20), sems(5)],
        "a" * 5,
        flops=6_000_000_000,
    )(at, *rows[0], *rows[1])


def first_feed_back(at, weights, g, x1, z1, h, dd, norms, after, prior=()):
    n, d = x1.shape
    ff = h.shape[1]
    feed, _ = share_shapes(d, ff)
    second = bool(prior)
    return call(
        functools.partial(first_feed_back_kernel, second),
        "saaaa" + "a" * (4 + len(prior)) + "vlla",
        [((n, d), BF16), ((VECTORS, d), F32)] + feed,
        feed
        + [
            ((n, d), F32), ((n, ff), BF16), ((n, d), BF16), ((n, ff), BF16),
            ((d, ff), BF16), ((ff, d), BF16), ((n, ff), BF16), ((n, d), BF16), ((n, d), F32),
            ((1, d, n), BF16), sems(4), sems(8),
        ],
        "vv" + ("v" if second else "a") * 2,
        flops=7_000_000_000,
    )(at, *weights, z1, dd, x1, h, *prior, g, *norms, after)


def first_attention_back(
    at, tallies, classes, weights, g, x0, z0, qkv, o, lse, norms, tok, tables, vec, after, shared_rows, size, prior=()
):
    n, d = x0.shape
    _, att = share_shapes(d, 4 * d)
    second = bool(prior)
    shared = [((shared_rows, d), F32)]
    if second:
        outs = [(tok.shape, BF16)] + [((att[0][0][0] + shared_rows // 2, d), BF16)] * 2
        extra = att + shared
    else:
        outs = [(tok.shape, F32)] + att + shared
        extra = outs[:3]
    return call(
        functools.partial(first_attention_back_kernel, second, size),
        "sssaa" + "a" * (6 + len(prior)) + "vlllllva",
        outs,
        extra
        + [
            ((n, d), F32), ((n, d), BF16), ((n, 3 * d), BF16), ((HEADS, n), F32), ((n, d), BF16),
            (tok.shape, BF16),
            ((n, n), F32), ((d, 4 * d), BF16), ((n, 3 * d), BF16), ((n, d), BF16), ((n, d), BF16),
            ((n, d), F32), ((1, d, n), BF16), ((1, d, n), BF16), ((VECTORS, d), F32),
            ((shared_rows, d), F32), sems(4), sems(9),
        ],
        ("v" if second else "a") * len(outs),
        flops=9_000_000_000,
    )(at, tallies, classes, *weights[:2], z0, o, qkv, lse, x0, tok, *prior, g, *norms, *tables, vec, after)


def shared_out(at, halves, tables, horizon, ff):
    d = halves[0].shape[1]
    outs = [(t.shape, F32) for t in tables]
    outs += [((3, d), F32), ((1, d), F32), ((1, d), F32), ((3, 2, d), F32), ((2, ff), F32), ((2, d), F32)]
    outs += [((horizon, d), F32), ((1, horizon), F32)]
    scratch = [((2, 2 * halves[0].shape[0], d), F32)]
    return call(shared_out_kernel, "savvvv", outs, scratch, vmem=24 << 20)(at, halves[0], *halves)


def entry_out(at, after, att, att_other, up, up_other, shape):
    outs = [(shape, F32), ((8, 128), F32)]
    return call(entry_out_kernel, "savvvv", outs, vmem=24 << 20)(at, after, att, att_other, up, up_other)


def local_out(at, after, near, far, down, pred_near, pred_far):
    outs = [(near.shape, F32), (down.shape, F32), (pred_far.shape, BF16)]
    return call(series_out_kernel, "savvvvv", outs, vmem=24 << 20)(
        at, after, near, far, down, pred_near, pred_far
    )


CORES = [(0, 1), (1, 0), (2, 3), (3, 2)]
TO_NEAR = [(2, 0), (3, 1)]
TO_FAR = [(0, 2), (1, 3)]


def move(array, pairs):
    return lax.ppermute(array, "pipe", pairs)


def bits_of(axis, mask):
    place = lax.axis_index(axis)
    index = 0
    for position, m in enumerate(mask):
        index = index + ((place & m) // m) * (1 << position)
    return index


def xor_swap(array, dim, k):
    axis, mask = dim
    flip = sum(m for position, m in enumerate(mask) if k >> position & 1)
    return lax.ppermute(array, axis, [(i, i ^ flip) for i in range(lax.axis_size(axis))])


class Phase:
    def __init__(self, after=()):
        self.after = list(after)
        self.numbers = []
        self.args = []
        self.outs = []
        self.work = []

    def take(self, arrays):
        at = len(self.args)
        self.args += arrays
        return slice(at, at + len(arrays))

    def make(self, shapes):
        at = len(self.outs)
        self.outs += [(s, BF16) for s in shapes]
        return slice(at, at + len(shapes))

    def sum(self, arrays, group=0, ways=1):
        rows, cols = arrays[0].shape
        ins, outs = self.take(arrays), self.make([(rows // ways, cols)] * ways)
        number = len(self.numbers)
        self.numbers.append(group)

        def work(numbers, args, made):
            for k, out in enumerate(made[outs]):
                base = (numbers[number] ^ k) * out.shape[0]
                step = 128 if out.shape[0] % 128 == 0 else out.shape[0]
                for r in range(0, out.shape[0], step):
                    at = pl.ds(pl.multiple_of(base + r, 16), step)
                    total = sum(one[at, :].astype(F32) for one in args[ins])
                    out[r : r + step, :] = total.astype(BF16)

        self.work.append(work)
        return outs

    def join(self, arrays, group, blocks=None):
        ways = len(arrays)
        rows, cols = arrays[0].shape
        if blocks is None:
            shapes = [(rows * ways, cols)]
        else:
            shapes = [(blocks[0] * blocks[1], cols), (blocks[0] * blocks[2], cols)]
        ins, outs = self.take(arrays), self.make(shapes)
        number = len(self.numbers)
        self.numbers.append(group)

        def work(numbers, args, made):
            for k, one in enumerate(args[ins]):
                which = numbers[number] ^ k
                if blocks is None:
                    made[outs][0][pl.ds(pl.multiple_of(which * rows, 16), rows), :] = one[...]
                    continue
                count, block, gap = blocks
                for p in range(count // ways):
                    at = p * (block + gap)
                    for out, skip, size in zip(made[outs], (0, block), (block, gap)):
                        to = pl.ds(pl.multiple_of((which * (count // ways) + p) * size, 16), size)
                        out[to, :] = one[at + skip : at + skip + size, :]

        self.work.append(work)
        return outs

    def gaps(self, arrays, group, block, gap):
        rows, cols = arrays[0].shape
        parts = rows // (block + gap)
        ins, outs = self.take(arrays), self.make([(len(arrays) * parts * gap, cols)])
        number = len(self.numbers)
        self.numbers.append(group)

        def work(numbers, args, made):
            for k, one in enumerate(args[ins]):
                which = numbers[number] ^ k
                for p in range(parts):
                    at = p * (block + gap) + block
                    to = pl.ds(pl.multiple_of((which * parts + p) * gap, 16), gap)
                    made[outs][0][to, :] = one[at : at + gap, :]

        self.work.append(work)
        return outs

    def run(self):
        count, extra = len(self.args), len(self.after)

        def kernel(numbers, *refs):
            refs = refs[extra:]
            for work in self.work:
                work(numbers, refs[:count], refs[count:])

        made = call(
            kernel, "s" + "a" * extra + "v" * count, self.outs, vmem=24 << 20
        )(scalars(*self.numbers), *self.after, *self.args)
        return made


def plane_dims():
    bits = [1 << i for i in range((lax.axis_size("dp") - 1).bit_length())]
    groups = [tuple(bits[:1])] + [tuple(bits[i : i + 2]) for i in range(1, len(bits), 2)]
    return [("dp", group) for group in groups]


def swaps(pieces, dim):
    return [pieces[0]] + [xor_swap(pieces[k], dim, k) for k in range(1, len(pieces))]


class Track:
    def __init__(self, arrays, dims, start, blocks=None):
        self.arrays, self.dims, self.start = arrays, dims, start
        self.blocks = blocks
        self.places = [bits_of(*dim) for dim in dims]
        self.queued = self.result = self.gaps = self.away = None

    def queue(self, phase, number):
        count = len(self.dims)
        number -= self.start
        self.queued = None
        if number < 0 or number > 2 * count:
            return
        if number < count:
            ways = 1 << len(self.dims[number][1])
            self.queued = phase.sum(self.arrays, self.places[number], ways), self.dims[number], 1
        elif number == count:
            self.queued = phase.sum(self.arrays), self.dims[-1], 1 << len(self.dims[-1][1])
        elif number < 2 * count:
            at = 2 * count - number
            if self.blocks and at == 1:
                self.gaps = phase.gaps(self.arrays, self.places[at], *self.blocks[1:])
            made = phase.join(self.arrays, self.places[at])
            self.queued = made, self.dims[at - 1], 1 << len(self.dims[at - 1][1])
        else:
            self.queued = phase.join(self.arrays, self.places[0], self.blocks), None, 0

    def send(self, made):
        if self.queued is None:
            return
        outs, dim, copies = self.queued
        if self.gaps is not None and self.away is None:
            self.away = move(made[self.gaps][0], TO_FAR + TO_NEAR)
        if dim is None:
            self.result = made[outs]
        else:
            self.arrays = swaps(made[outs] * copies, dim)


def plane_sums(feed, between, blocks, finish_feed):
    dims = plane_dims()
    tracks = [Track([feed[0], move(feed[1], CORES)], dims, 0)]
    rounds = 2 * len(dims)
    att = local = after = None
    for number in range(rounds + 3):
        order = []
        if number == 1:
            order = [after]
        if number == rounds + 2:
            order = [local()]
        phase = Phase(order)
        for track in tracks:
            track.queue(phase, number)
        if number == 1:
            passed = phase.sum([att[1]])
        if number == rounds + 2:
            passed = phase.sum([tracks[-1].away])
        made = phase.run()
        for track in tracks:
            track.send(made)
        if number == 0:
            att = between(made[0])
            after = att[0]
        if number == 1:
            tracks.append(Track([att[0], move(made[passed][0], CORES)], dims, 2, blocks=blocks))
        if number == rounds + 1:
            local = finish_feed(tracks[0].result[0])
    return *tracks[-1].result, made[passed][0]


def per_device(
    lookback_readings,
    prediction_adjoint,
    variate_tallies,
    lookback_classes,
    brief_lift_table,
    moderate_lift_table,
    distant_lift_table,
    lift_offsets,
    part_entry_arrays,
    part_shrink_lines,
    part_layernorm_scale,
    part_layernorm_offset,
    mixing_offsets,
    expand_offsets,
    shrink_offsets,
    prediction_matrix,
    prediction_offset,
):
    place = lax.axis_index("pipe")
    core, far = place & 1, place // 2
    places = [scalars(core, far, r) for r in range(2)]
    at = places[0]
    entry, shrink = part_entry_arrays[0], part_shrink_lines[0]
    entry_other, shrink_other = move(entry, CORES), move(shrink, CORES)
    tok, adjoint = lookback_readings[0].T, prediction_adjoint[0].T
    tables = (brief_lift_table, moderate_lift_table, distant_lift_table)
    norm = jnp.concatenate([part_layernorm_scale, part_layernorm_offset], 0)

    weights = (entry, entry_other, shrink, shrink_other)
    norms = (norm, move(norm, CORES))
    toks = (tok, move(tok, TO_NEAR))
    layout = (variate_tallies, lookback_classes)
    mixing = mixing_offsets.transpose(1, 0, 2)

    first = []
    arrived = []
    for r in range(2):
        out = first_layer(
            places[r], *layout, weights, adjoint, toks[r], tables, lift_offsets, mixing, expand_offsets,
            shrink_offsets, norms,
        )
        first.append(out[2:])
        if r == 0:
            adjoints = (move(out[1], TO_FAR), adjoint)
        arrived.append(move(out[0], TO_FAR))
    second = []
    returned = []
    predictions = []
    for r in range(2):
        g, prediction, saved = second_layer(
            places[r], *layout, weights, arrived[r], adjoints[r], prediction_matrix.T,
            prediction_offset[None], mixing, expand_offsets, shrink_offsets, norms,
        )
        returned.append(move(g, TO_NEAR))
        predictions.append(prediction)
        second.append(saved)
    shared_rows = max(768, 32 * lax.axis_size("dp"))
    away = second_weights(at, second, shared_rows)

    size = lax.axis_size("dp")
    x0, z0, qkv, o, lse, x1, z1, h, d = first[0]
    g, vec, *feed = first_feed_back(at, weights, returned[0], x1, z1, h, d, norms, arrived[1])
    near_series, *att, shared = first_attention_back(
        places[0], *layout, weights, g, x0, z0, qkv, o, lse, norms, toks[0], tables, vec, g,
        shared_rows, size,
    )
    x0, z0, qkv, o, lse, x1, z1, h, d = first[1]
    g, vec, *feed = first_feed_back(
        at, weights, returned[1], x1, z1, h, d, norms, att[0], (*feed, *away[:2])
    )
    far_series = []

    def between(after):
        series, keep, send = first_attention_back(
            places[1], *layout, weights, g, x0, z0, qkv, o, lse, norms, toks[1], tables, vec, after,
            shared_rows, size, (*att, shared, *away[2:]),
        )
        far_series.append(series)
        return keep, send

    held = {}
    rows = entry.shape[0] * entry.shape[1] // shrink.shape[1] // 2

    def finish_feed(feed):
        held["feed"] = feed
        held["up"] = move(feed[:rows], [(0, 1), (2, 3)])
        held["series"] = move(far_series[0], TO_FAR)
        held["prediction"] = move(predictions[0], TO_NEAR)

        def local():
            held["local"] = local_out(
                at, feed, near_series, held["series"], feed[rows:], held["prediction"], predictions[1]
            )
            return held["local"][2]

        return local

    blocks = (size, att[0].shape[0] // size, shared_rows // 2 // size)
    att_sum, shared_sum, away_part = plane_sums(feed, between, blocks, finish_feed)
    dim = plane_dims()[0]
    att_other = move(att_sum, [(1, 0), (3, 2)])
    shared_other = move(shared_sum, CORES)
    away_parts = swaps([away_part] * (1 << len(dim[1])), dim)
    series_grad, down_grad, prediction = held["local"]
    entry_grad, mark = entry_out(
        at, series_grad, att_sum, att_other, held["feed"][:rows], held["up"], entry.shape
    )
    phase = Phase([mark])
    queued = phase.join(away_parts, bits_of(*dim))
    shared_away = phase.run()[queued][0]
    t0, t1, t2, embb, gain, offset, attb, upb, downb, pw, pb = shared_out(
        at, (shared_sum, shared_other, shared_away, move(shared_away, CORES)), tables,
        prediction_matrix.shape[1], entry.shape[1],
    )
    return (
        prediction.T[None],
        series_grad.T[None],
        t0,
        t1,
        t2,
        embb,
        entry_grad[None],
        down_grad[None],
        gain,
        offset,
        attb.transpose(1, 0, 2),
        upb,
        downb,
        pw.T,
        pb[0],
    )


def solution(mesh):
    placed = (
        P("pipe", "dp", None),
        P("pipe", "dp", None),
        P(None, "dp", None),
        P(None, "dp", None),
        P(),
        P(),
        P(),
        P(),
        P("pipe", None, None),
        P("pipe", None, None),
        P("pipe", None),
        P("pipe", None),
        P(),
        P(),
        P(),
        P(),
        P(),
    )
    return jax.shard_map(
        per_device,
        mesh=mesh,
        in_specs=placed,
        out_specs=(
            P("pipe", "dp", None),
            P("pipe", "dp", None),
            P(),
            P(),
            P(),
            P(),
            P("pipe", None, None),
            P("pipe", None, None),
            P("pipe", None),
            P("pipe", None),
            P(),
            P(),
            P(),
            P(),
            P(),
        ),
        check_vma=False,
    )
```
